512 devices in a mesh: ctx: 64 (over z, y_lo, x), tp: 8 (over y_hi, core).
Axes of the slice: x: 4, y: 8 (y_hi: 4, y_lo: 2; y = y_hi * 2 + y_lo), z: 8, core: 2. Of those that a mesh axis runs over, the one named last changes fastest.
Arguments:
- byte_states: bfloat16 [16384, 1024], P('ctx'), may hold values from -12 to 12, as said below
- patch_of_byte: int32 [16384], P('ctx'), may hold values from 0 to 125, as said below
- patch_first: int32 [64], replicated, may hold values from 0 to 4063, as said below
- moved: int32 [2, 64], replicated, may hold values from 0 to 32, as said below
- w_qkv: bfloat16 [3, 1024, 2048], P(None, None, 'tp'), may hold values from -0.25 to 0.25, as said below
- d_attn: bfloat16 [4096, 2048], P('ctx', 'tp'), may hold values from -6 to 6
Outputs:
- attn_out: bfloat16 [4096, 2048], P('ctx', 'tp')
- byte_grad: bfloat16 [16384, 1024], P('ctx', 'tp')
The draws below stay inside these ranges and needn't reach their ends.
Inputs may be any that keep to these rules, and one draw needn't show every extreme that they name: `patch_of_byte`: within each byte shard the numbers start at 0 and rise by 0 or 1 from byte to byte; a shard holds at most 126 patches, reached on some shard. `patch_first`: the sum of the patch counts of all earlier byte shards; shard 0 starts at 0. moved[0, 0] = 0 and moved[1, 63] = 0; every other entry is 1 to 32; every patch shard thereby receives exactly 64 patches, and the patch counts agree with patch_first and patch_of_byte. `w_qkv`: independent entries of order 1024 ** -0.5. `byte_states`: entries of order one.
All inputs are finite; a program needn't handle non-finite values.
Results may differ from the reference program's by a relative error of at most 0.011.
Values may be sent and summed in bfloat16 or wider, within the bound.
No kernel may reach another device: no remote copies, remote signals or barrier semaphores. Data moves between devices by JAX's collectives and lax.ppermute only.
A program may use at most 64 MiB of HBM per device.

```python
import jax
import jax.numpy as jnp
from jax import lax

DL = 1024
HEADS = 16
HD = 128
P_DEV = 64
BYTE_DEV = 256
KEYS = 4096
BYTES = 16384
N_CTX = 64


def shard_plan(key):
    reach = P_DEV // 2
    lower_moves = jax.random.randint(jax.random.fold_in(key, 11), (N_CTX,), 1, reach + 1)
    upper_moves = jax.random.randint(jax.random.fold_in(key, 13), (N_CTX,), 1, reach + 1)
    chosen = jax.random.randint(jax.random.fold_in(key, 17), (), 1, N_CTX - 1)
    place = jnp.arange(N_CTX)
    lower_moves = jnp.where(place == chosen, reach, lower_moves)
    upper_moves = jnp.where(place == chosen, reach, upper_moves)
    upper_moves = jnp.where(place == chosen - 1, 1, upper_moves)
    lower_moves = jnp.where(place == chosen + 1, 1, lower_moves)
    lower_moves = jnp.where(place == 0, 0, lower_moves)
    upper_moves = jnp.where(place == N_CTX - 1, 0, upper_moves)
    below_high = jnp.concatenate([jnp.zeros((1,), jnp.int32), upper_moves[:-1]])
    above_low = jnp.concatenate([lower_moves[1:], jnp.zeros((1,), jnp.int32)])
    counts = P_DEV - below_high - above_low + lower_moves + upper_moves
    return (counts.astype(jnp.int32), lower_moves.astype(jnp.int32), upper_moves.astype(jnp.int32))


def draw_patch_first(key, part):
    counts, lower_moves, upper_moves = shard_plan(key)
    return (jnp.cumsum(counts) - counts).astype(jnp.int32)


def draw_moved(key, part):
    counts, lower_moves, upper_moves = shard_plan(key)
    return jnp.stack([lower_moves, upper_moves], axis=0).astype(jnp.int32)


def draw_patch_of_byte(key, part):
    counts, lower_moves, upper_moves = shard_plan(key)
    shard_keys = jax.random.split(jax.random.fold_in(key, 23), N_CTX)

    def one_shard(shard_key, count):
        order = jax.random.permutation(shard_key, BYTE_DEV - 1)
        cut = (order < count - 1).astype(jnp.int32)
        return jnp.concatenate([jnp.zeros((1,), jnp.int32), jnp.cumsum(cut).astype(jnp.int32)])
    return jax.vmap(one_shard)(shard_keys, counts).reshape(-1).astype(jnp.int32)


def draw_byte_states(key, part):
    values = jax.random.normal(key, (BYTES, DL), jnp.float32)
    return jnp.clip(values, -12.0, 12.0).astype(jnp.bfloat16)


def draw_w_qkv(key, part):
    values = jax.random.normal(key, (3, DL, HEADS * HD), jnp.float32) * DL ** (-0.5)
    return jnp.clip(values, -0.25, 0.25).astype(jnp.bfloat16)


def shard_levels(own_key, extent, cuts, least, top_value):
    level, own = 1.0, jax.random.fold_in(own_key, 6)
    for dim, parts in cuts:
        steps = jnp.exp(jax.random.uniform(jax.random.fold_in(own, dim), (parts,), jnp.float32, least / len(cuts), top_value / len(cuts)))
        level = level * jnp.repeat(steps, extent[dim] // parts).reshape([-1 if axis == dim else 1 for axis in range(len(extent))])
    return level


def scatter_about(own_key, extent, deviation, most, cuts=(), held_as=jnp.bfloat16):
    loudness = shard_levels(own_key, extent, cuts, -0.22, 0.18) if cuts else 1.0
    entries = jax.random.normal(own_key, extent, jnp.float32) * deviation * loudness
    return jnp.minimum(jnp.maximum(entries, -most), most).astype(held_as)


def setup_inputs(seed: int = 0) -> dict:
    key_list = jax.random.split(jax.random.key(seed), 7)
    return {
        "byte_states": draw_byte_states(jax.random.fold_in(key_list[6], 71), 0),
        "patch_of_byte": draw_patch_of_byte(jax.random.fold_in(key_list[6], 71), 0),
        "patch_first": draw_patch_first(jax.random.fold_in(key_list[6], 71), 0),
        "moved": draw_moved(jax.random.fold_in(key_list[6], 71), 0),
        "w_qkv": draw_w_qkv(jax.random.fold_in(key_list[6], 71), 0),
        "d_attn": scatter_about(key_list[5], (KEYS, HEADS * HD), 1.0, 6.0, ((0, 64), (1, 8))),
    }


def reference(byte_states, patch_of_byte, patch_first, moved, w_qkv, d_attn):
    shard = jnp.arange(BYTES, dtype=jnp.int32) // BYTE_DEV
    gid = (patch_first[shard] + patch_of_byte).astype(jnp.int32)
    sums = jax.ops.segment_sum(byte_states.astype(jnp.float32), gid, num_segments=KEYS)
    lengths = jax.ops.segment_sum(jnp.ones((BYTES,), jnp.float32), gid, num_segments=KEYS)
    pooled_global = (sums / lengths[:, None]).astype(jnp.bfloat16)

    place = jnp.arange(KEYS, dtype=jnp.int32)
    ends = jnp.concatenate([patch_first[1:], jnp.full((1,), KEYS, jnp.int32)]).astype(jnp.int32)
    counts = (ends - patch_first).astype(jnp.int32)
    lower_moves = moved[0]
    upper_moves = moved[1]
    below_high = jnp.concatenate([jnp.zeros((1,), jnp.int32), upper_moves[:-1]]).astype(jnp.int32)
    home = (jnp.sum((place[:, None] >= patch_first[None, :]).astype(jnp.int32), axis=1) - 1).astype(jnp.int32)
    local = (place - patch_first[home]).astype(jnp.int32)
    low_here = lower_moves[home]
    high_here = upper_moves[home]
    count_here = counts[home]
    goes_low = local < low_here
    goes_high = local >= count_here - high_here
    owner = jnp.where(goes_low, home - 1, jnp.where(goes_high, home + 1, home))
    rank = jnp.where(goes_low, P_DEV - low_here + local,
                     jnp.where(goes_high, local - (count_here - high_here), below_high[home] + local - low_here))
    slot = (owner * P_DEV + rank).astype(jnp.int32)
    order = jnp.zeros((KEYS,), jnp.int32).at[slot].set(place)

    pooled = pooled_global[order]
    query = jnp.dot(pooled, w_qkv[0], preferred_element_type=jnp.float32).astype(jnp.bfloat16)
    keyed = jnp.dot(pooled, w_qkv[1], preferred_element_type=jnp.float32).astype(jnp.bfloat16)
    valued = jnp.dot(pooled, w_qkv[2], preferred_element_type=jnp.float32).astype(jnp.bfloat16)
    scale = HD ** -0.5
    causal = order[:, None] >= order[None, :]

    def heads_first(x):
        return jnp.transpose(x.reshape(KEYS, HEADS, HD), (1, 0, 2))

    def per_head(items):
        q_head, k_head, v_head, g_head = items
        score = jnp.dot(q_head, k_head.T, preferred_element_type=jnp.float32) * scale
        masked = jnp.where(causal, score, -jnp.inf)
        top = jnp.max(masked, axis=1, keepdims=True)
        lse = top + jnp.log(jnp.sum(jnp.exp(masked - top), axis=1, keepdims=True))
        prob = jnp.exp(jnp.where(causal, score - lse, -jnp.inf))
        probs = prob.astype(jnp.bfloat16)
        output = jnp.dot(probs, v_head, preferred_element_type=jnp.float32).astype(jnp.bfloat16)
        delta = jnp.sum(g_head.astype(jnp.float32) * output.astype(jnp.float32), axis=1, keepdims=True)
        dprob = jnp.dot(g_head, v_head.T, preferred_element_type=jnp.float32)
        dscore = (prob * (dprob - delta)).astype(jnp.bfloat16)
        d_query = (jnp.dot(dscore, k_head, preferred_element_type=jnp.float32) * scale).astype(jnp.bfloat16)
        d_key = (jnp.dot(dscore.T, q_head, preferred_element_type=jnp.float32) * scale).astype(jnp.bfloat16)
        d_value = jnp.dot(probs.T, g_head, preferred_element_type=jnp.float32).astype(jnp.bfloat16)
        return output, d_query, d_key, d_value

    results = lax.map(per_head, (heads_first(query), heads_first(keyed), heads_first(valued), heads_first(d_attn)))

    def rows_first(x):
        return jnp.transpose(x, (1, 0, 2)).reshape(KEYS, HEADS * HD)

    attn_out = rows_first(results[0])
    d_query, d_key, d_value = rows_first(results[1]), rows_first(results[2]), rows_first(results[3])
    d_pooled = jnp.dot(d_query, w_qkv[0].T, preferred_element_type=jnp.float32)
    d_pooled = d_pooled + jnp.dot(d_key, w_qkv[1].T, preferred_element_type=jnp.float32)
    d_pooled = d_pooled + jnp.dot(d_value, w_qkv[2].T, preferred_element_type=jnp.float32)
    d_pooled = d_pooled.astype(jnp.bfloat16)
    byte_slot = slot[gid]
    byte_grad = (d_pooled[byte_slot].astype(jnp.float32) / lengths[gid][:, None]).astype(jnp.bfloat16)
    return attn_out, byte_grad
```

```python
import jax
import jax.numpy as jnp
from jax import lax
from jax.sharding import Mesh, PartitionSpec as P

HD = 128
SIZES = (4, 2, 2, 4, 4, 2)
NAMES = ("zh", "zl", "yl", "x", "yh", "core")
CTX = ("zh", "zl", "yl", "x")
KEYED = ("zl", "yl", "x")
TP = ("yh", "core")
N_CTX = 64
N_QUERY = 4
N_KEY = 16
BF = jnp.bfloat16
F32 = jnp.float32


def dot(a, b, dims):
    return lax.dot_general(a, b, (dims, ((), ())), preferred_element_type=F32)


def shift(x, axis, n, by):
    return lax.ppermute(x, axis, [(i, (i + by) % n) for i in range(n)])


def swap(x, axis):
    return lax.all_to_all(x, axis, split_axis=0, concat_axis=0, tiled=True)


def shards(byte_states, patch_of_byte, patch_first, moved, w_qkv, d_attn):
    rows, feats = d_attn.shape
    heads = feats // HD
    total = rows * N_CTX
    window = 2 * rows
    half = rows // 2
    scale = HD ** (-0.5)
    c = lax.axis_index(CTX)
    zh = lax.axis_index("zh")

    def entry(values, at):
        return jnp.where((at >= 0) & (at < N_CTX), values[jnp.clip(at, 0, N_CTX - 1)], 0)

    first = patch_first[c]
    low = moved[0, c]
    next_first = jnp.where(c + 1 < N_CTX, entry(patch_first, c + 1), total)
    next_low = entry(moved[0], c + 1)
    prev_high = entry(moved[1], c - 1)
    base = rows * c - half

    places = lax.broadcasted_iota(jnp.int32, (window, 1), 0)
    member = places == (first - base + patch_of_byte)[None, :]
    lengths = jnp.sum(member.astype(F32), axis=1)
    pooled = (
        dot(member.astype(BF), byte_states, ((1,), (0,))) / jnp.maximum(lengths, 1.0)[:, None]
    ).astype(BF)
    rank = jnp.arange(rows, dtype=jnp.int32)
    order = jnp.where(
        rank < prev_high,
        first - prev_high + rank,
        jnp.where(
            rank >= rows - next_low,
            next_first + rank - (rows - next_low),
            first + low + rank - prev_high,
        ),
    )
    slotted = (places == (order - base)[None, :]).astype(BF)
    grads = dot(slotted, d_attn, ((1,), (0,))).astype(BF)
    parts = [dot(pooled, w_qkv[i], ((1,), (0,))).astype(BF) for i in range(3)]
    both = jnp.concatenate([parts[0], grads, parts[1], parts[2]], axis=1)
    mine = both[rows:] + shift(both[:rows], CTX, N_CTX, -1)

    asked = mine[:, : 2 * feats]
    asked = jnp.concatenate(
        [asked] + [shift(asked, "zh", N_QUERY, k) for k in range(1, N_QUERY)], axis=0
    )
    held = swap(jnp.broadcast_to(mine[None, :, 2 * feats :], (N_KEY, rows, 2 * feats)), KEYED)
    held = held.reshape(N_KEY * rows, 2 * feats)
    n_q, n_k = N_QUERY * rows, N_KEY * rows
    row = jnp.arange(n_q, dtype=jnp.int32)
    block = (zh - row // rows) % N_QUERY
    group = c % N_KEY
    query_id = (rows * (block * N_KEY + group) + half + row % rows) % total
    key_id = (n_k * zh + half + jnp.arange(n_k, dtype=jnp.int32)) % total
    causal = query_id[:, None] >= key_id[None, :]

    stats, saved = [], []
    for h in range(heads):
        q = asked[:, h * HD : (h + 1) * HD]
        g = asked[:, feats + h * HD : feats + (h + 1) * HD]
        k = held[:, h * HD : (h + 1) * HD]
        v = held[:, feats + h * HD : feats + (h + 1) * HD]
        score = jnp.where(causal, dot(q, k, ((1,), (1,))) * scale, -1e30)
        top = jnp.max(score, axis=1)
        weight = jnp.where(causal, jnp.exp(score - top[:, None]), 0.0)
        out = dot(weight.astype(BF), v, ((1,), (0,)))
        dprob = dot(g, v, ((1,), (1,)))
        stats += [top, jnp.sum(weight, axis=1), jnp.sum(out * g.astype(F32), axis=1)]
        saved.append((q, g, k, weight, out, dprob))
    stats = jnp.stack(stats + [stats[0]] * (8 - len(stats)), axis=0)
    shared = [stats]
    for k in range(1, N_QUERY):
        shared.append(jnp.roll(shift(stats, "zh", N_QUERY, k), k * rows, axis=1))
    shared = jnp.stack(shared, axis=0)

    query_terms, out_terms, key_terms, value_terms = [], [], [], []
    for h in range(heads):
        q, g, k, weight, out, dprob = saved[h]
        tops, sums, dots = (shared[:, 3 * h + i] for i in range(3))
        peak = jnp.max(tops, axis=0)
        each = jnp.exp(tops - peak[None])
        norm = jnp.sum(each * sums, axis=0)
        delta = jnp.sum(each * dots, axis=0) / norm
        factor = jnp.exp(tops[0] - peak) / norm
        prob = weight * factor[:, None]
        dscore = (prob * (dprob - delta[:, None])).astype(BF)
        query_terms.append(dot(dscore, k, ((1,), (0,))) * scale)
        out_terms.append(out * factor[:, None])
        key_terms.append(dot(dscore, q, ((0,), (0,))) * scale)
        value_terms.append(dot(prob.astype(BF), g, ((0,), (0,))))
    held_terms = jnp.concatenate(key_terms + value_terms, axis=1).astype(BF)
    held_terms = swap(held_terms.reshape(N_KEY, rows, 2 * feats), KEYED)
    held_grads = jnp.sum(held_terms.astype(F32), axis=0).astype(BF)
    asked_terms = jnp.concatenate(query_terms + out_terms, axis=1)
    asked_sum = asked_terms[:rows]
    asked_terms = asked_terms.astype(BF)
    for k in range(1, N_QUERY):
        arrived = shift(asked_terms[k * rows : (k + 1) * rows], "zh", N_QUERY, -k)
        asked_sum = asked_sum + arrived.astype(F32)
    asked_sum = asked_sum.astype(BF)
    d_query, out = asked_sum[:, :feats], asked_sum[:, feats:]

    partial = dot(d_query, w_qkv[0], ((1,), (1,)))
    partial = partial + dot(held_grads[:, :feats], w_qkv[1], ((1,), (1,)))
    partial = partial + dot(held_grads[:, feats:], w_qkv[2], ((1,), (1,)))
    n_tp = 8
    pieces = partial.astype(BF).reshape(rows, n_tp, -1).transpose(1, 0, 2)
    d_pooled = jnp.sum(swap(pieces, TP).astype(F32), axis=0).astype(BF)

    out_window = jnp.concatenate([shift(out, CTX, N_CTX, 1), out], axis=0)
    attn_out = dot(slotted, out_window, ((0,), (0,))).astype(BF)
    grad_window = jnp.concatenate([shift(d_pooled, CTX, N_CTX, 1), d_pooled], axis=0)
    spread = dot(member.astype(BF), grad_window, ((0,), (0,)))
    byte_lengths = jnp.sum(jnp.where(member, lengths[:, None], 0.0), axis=0)
    byte_grad = (spread / byte_lengths[:, None]).astype(BF)
    return attn_out, byte_grad


def solution(mesh):
    fine = Mesh(mesh.devices.reshape(SIZES), NAMES)
    placed = (P(CTX, None), P(CTX), P(), P(), P(None, None, TP), P(CTX, TP))
    return jax.shard_map(
        shards,
        mesh=fine,
        in_specs=placed,
        out_specs=(P(CTX, TP), P(CTX, TP)),
        check_vma=False,
    )
```

```python
import jax
import jax.numpy as jnp
from jax import lax
from jax.experimental import pallas as pl
from jax.experimental.pallas import tpu as pltpu
from jax.sharding import Mesh, PartitionSpec as P

HD = 128
SIZES = (4, 2, 2, 4, 4, 2)
NAMES = ("zh", "zl", "yl", "x", "yh", "core")
CTX = ("zh", "zl", "yl", "x")
ASK = ("zl", "x")
KEYED = ("zh", "yl")
TP = ("yh", "core")
N_CTX = 64
GROUP = 8
ROWS = 64
HEADS = 2
FEATS = HEADS * HD
TOTAL = N_CTX * ROWS
WINDOW = 2 * ROWS
HALF = ROWS // 2
TILE = GROUP * ROWS
SCALE = HD ** (-0.5)
LOG2E = 1.4426950408889634
NEG = -1e30
FLOOR = -1e29
BF = jnp.bfloat16
F32 = jnp.float32
I32 = jnp.int32


def dot(a, b, dims):
    return lax.dot_general(a, b, (dims, ((), ())), preferred_element_type=F32)


def shift(x, axis, n, by):
    return lax.ppermute(x, axis, [(i, (i + by) % n) for i in range(n)])


def swap(x, axis):
    return lax.all_to_all(x, axis, split_axis=0, concat_axis=0, tiled=True)


def iota(shape, dim):
    return lax.broadcasted_iota(I32, shape, dim)


def call(kernel, ins, outs, flops, scalars=0):
    smem = pl.BlockSpec(memory_space=pltpu.SMEM)
    vmem = pl.BlockSpec(memory_space=pltpu.VMEM)
    size = sum(x.size * x.dtype.itemsize for x in list(ins) + list(outs))
    return pl.pallas_call(
        kernel,
        out_shape=tuple(outs),
        in_specs=[smem] * scalars + [vmem] * (len(ins) - scalars),
        out_specs=tuple([vmem] * len(outs)),
        cost_estimate=pl.CostEstimate(flops=flops, bytes_accessed=size, transcendentals=0),
        compiler_params=pltpu.CompilerParams(vmem_limit_bytes=40 * 1024 * 1024),
    )(*ins)


def shaped(shape, dtype):
    return jax.ShapeDtypeStruct(shape, dtype)


def slot_order(c, first_ref, moved_ref, shape, dim):
    before, after = jnp.maximum(c - 1, 0), jnp.minimum(c + 1, N_CTX - 1)
    first = first_ref[c]
    low = moved_ref[0, c]
    prev_high = jnp.where(c > 0, moved_ref[1, before], 0)
    next_low = jnp.where(c < N_CTX - 1, moved_ref[0, after], 0)
    next_first = jnp.where(c < N_CTX - 1, first_ref[after], TOTAL)
    rank = iota(shape, dim)
    order = jnp.where(
        rank < prev_high,
        first - prev_high + rank,
        jnp.where(
            rank >= ROWS - next_low,
            next_first + rank - (ROWS - next_low),
            first + low + rank - prev_high,
        ),
    )
    return order - (ROWS * c - HALF)


def pool_kernel(c_ref, first_ref, moved_ref, bytes_ref, place_ref, grad_ref, w_ref, sent_ref, own_ref):
    c = c_ref[0]
    offset = first_ref[c] - (ROWS * c - HALF)
    member = iota((WINDOW, bytes_ref.shape[0]), 0) == place_ref[...] + offset
    lengths = jnp.sum(member.astype(F32), axis=1, keepdims=True)
    pooled = dot(member.astype(F32).astype(BF), bytes_ref[...], ((1,), (0,)))
    pooled = (pooled / jnp.maximum(lengths, 1.0)).astype(BF)
    order = slot_order(c, first_ref, moved_ref, (WINDOW, ROWS), 1)
    slotted = (iota((WINDOW, ROWS), 0) == order).astype(F32).astype(BF)
    grads = dot(slotted, grad_ref[...], ((1,), (0,))).astype(BF)
    for at, value in (
        (0, dot(pooled, w_ref[0], ((1,), (0,))).astype(BF)),
        (1, grads),
        (2, dot(pooled, w_ref[1], ((1,), (0,))).astype(BF)),
        (3, dot(pooled, w_ref[2], ((1,), (0,))).astype(BF)),
    ):
        sent_ref[:, at * FEATS : (at + 1) * FEATS] = value[:ROWS]
        own_ref[:, at * FEATS : (at + 1) * FEATS] = value[ROWS:]


def spread_kernel(own_ref, got_ref, ask_ref, held_ref):
    both = own_ref[...] + got_ref[...]
    for i in range(GROUP):
        ask_ref[i] = both[:, : 2 * FEATS]
        held_ref[i] = both[:, 2 * FEATS :]


def tile_ids(at_ref):
    row = iota((1, TILE), 1)
    block, inner = row >> 6, row & 63
    query = at_ref[0] + ROWS * (8 * (block >> 2) + (block & 3)) + inner
    col = iota((TILE, 1), 0)
    block, inner = col >> 6, col & 63
    key = at_ref[1] + ROWS * (16 * (block >> 1) + 4 * (block & 1)) + inner
    return query & (TOTAL - 1), key & (TOTAL - 1)


def columns(ref, at):
    return ref[:, :, at * HD : (at + 1) * HD].reshape(TILE, HD)


def forward_kernel(at_ref, ask_ref, held_ref, stats_ref):
    query_id, key_id = tile_ids(at_ref)
    allowed = query_id >= key_id
    rows = []
    for h in range(HEADS):
        q, g = columns(ask_ref, h), columns(ask_ref, HEADS + h)
        k, v = columns(held_ref, h), columns(held_ref, HEADS + h)
        score = jnp.where(allowed, dot(k, q, ((1,), (1,))) * (SCALE * LOG2E), NEG)
        top = jnp.maximum(jnp.max(score, axis=0, keepdims=True), FLOOR)
        weight = jnp.exp2(score - top)
        dprob = dot(v, g, ((1,), (1,)))
        rows += [
            top,
            jnp.sum(weight, axis=0, keepdims=True),
            jnp.sum(weight * dprob, axis=0, keepdims=True),
        ]
    rows = jnp.concatenate(rows + [rows[0], rows[0]], axis=0)
    for i in range(GROUP):
        stats_ref[i] = rows


def backward_kernel(at_ref, ask_ref, held_ref, stats_ref, key_ref, query_ref):
    query_id, key_id = tile_ids(at_ref)
    allowed = query_id >= key_id
    stats = stats_ref[...]
    for h in range(HEADS):
        tops, sums, dots = (stats[:, 3 * h + i, :] for i in range(3))
        peak = jnp.max(tops, axis=0, keepdims=True)
        each = jnp.exp2(tops - peak)
        norm = jnp.sum(each * sums, axis=0, keepdims=True)
        delta = jnp.sum(each * dots, axis=0, keepdims=True) / norm
        lse = peak + jnp.log(norm) * LOG2E
        q, g = columns(ask_ref, h), columns(ask_ref, HEADS + h)
        k, v = columns(held_ref, h), columns(held_ref, HEADS + h)
        score = jnp.where(allowed, dot(k, q, ((1,), (1,))) * (SCALE * LOG2E), NEG)
        prob = jnp.exp2(score - lse)
        dprob = dot(v, g, ((1,), (1,)))
        dscore = (prob * (dprob - delta)).astype(BF)
        prob = prob.astype(BF)
        d_key = (dot(dscore, q, ((1,), (0,))) * SCALE).astype(BF)
        d_value = dot(prob, g, ((1,), (0,))).astype(BF)
        d_query = (dot(dscore, k, ((0,), (0,))) * SCALE).astype(BF)
        out = dot(prob, v, ((0,), (0,))).astype(BF)
        for ref, at, value in (
            (key_ref, h, d_key),
            (key_ref, HEADS + h, d_value),
            (query_ref, h, d_query),
            (query_ref, HEADS + h, out),
        ):
            ref[:, :, at * HD : (at + 1) * HD] = value.reshape(GROUP, ROWS, HD)


def key_sum_kernel(terms_ref, w_ref, part_ref):
    total = jnp.sum(terms_ref[...].astype(F32), axis=0).astype(BF)
    part_ref[...] = dot(total[:, :FEATS], w_ref[1], ((1,), (1,))) + dot(
        total[:, FEATS:], w_ref[2], ((1,), (1,))
    )


def query_sum_kernel(terms_ref, part_ref, w_ref, piece_ref, out_ref):
    total = jnp.sum(terms_ref[...].astype(F32), axis=0).astype(BF)
    out_ref[...] = total[:, FEATS:]
    part = (part_ref[...] + dot(total[:, :FEATS], w_ref[0], ((1,), (1,)))).astype(BF)
    for i in range(GROUP):
        piece_ref[i] = part[:, i * HD : (i + 1) * HD]


def head_sum_kernel(pieces_ref, sum_ref):
    sum_ref[...] = jnp.sum(pieces_ref[...].astype(F32), axis=0).astype(BF)


def slot_kernel(c_ref, first_ref, moved_ref, before_ref, own_ref, out_ref):
    order = slot_order(c_ref[0], first_ref, moved_ref, (ROWS, WINDOW), 0)
    picker = (iota((ROWS, WINDOW), 1) == order).astype(F32).astype(BF)
    window = jnp.concatenate([before_ref[...], own_ref[...]], axis=0)
    out_ref[...] = dot(picker, window, ((1,), (0,))).astype(BF)


def byte_kernel(c_ref, first_ref, place_ref, before_ref, own_ref, out_ref):
    c = c_ref[0]
    offset = first_ref[c] - (ROWS * c - HALF)
    member = (iota((place_ref.shape[0], WINDOW), 1) == place_ref[...] + offset).astype(F32)
    lengths = jnp.sum(member, axis=0, keepdims=True)
    own_length = jnp.sum(member * lengths, axis=1, keepdims=True)
    window = jnp.concatenate([before_ref[...], own_ref[...]], axis=0)
    out_ref[...] = (dot(member.astype(BF), window, ((1,), (0,))) / own_length).astype(BF)


def shards(byte_states, patch_of_byte, patch_first, moved, w_qkv, d_attn):
    zh, zl, yl, x = (lax.axis_index(name) for name in CTX)
    c = lax.axis_index(CTX).astype(I32)
    c_ref = c.reshape(1)
    at = jnp.stack([ROWS * (16 * zh + 4 * yl) + HALF, ROWS * (8 * zl + x) + HALF]).astype(I32)
    n_bytes = patch_of_byte.shape[0]
    block = shaped((ROWS, 4 * FEATS), BF)
    stack = shaped((GROUP, ROWS, 2 * FEATS), BF)

    sent, own = call(
        pool_kernel,
        (c_ref, patch_first, moved, byte_states, patch_of_byte.reshape(1, n_bytes), d_attn, w_qkv),
        (block, block),
        300_000_000,
        3,
    )
    ask, held = call(spread_kernel, (own, shift(sent, CTX, N_CTX, -1)), (stack, stack), 1_000_000)
    ask = swap(ask, ASK)
    held = swap(held, KEYED)
    (stats,) = call(
        forward_kernel,
        (at, ask, held),
        (shaped((GROUP, 8, TILE), F32),),
        300_000_000,
        1,
    )
    stats = swap(stats, ASK)
    key_terms, query_terms = call(
        backward_kernel, (at, ask, held, stats), (stack, stack), 900_000_000, 1
    )
    key_terms = swap(key_terms, KEYED)
    query_terms = swap(query_terms, ASK)
    (part,) = call(
        key_sum_kernel, (key_terms, w_qkv), (shaped((ROWS, 4 * FEATS), F32),), 70_000_000
    )
    pieces, out = call(
        query_sum_kernel,
        (query_terms, part, w_qkv),
        (shaped((GROUP, ROWS, HD), BF), shaped((ROWS, FEATS), BF)),
        35_000_000,
    )
    (d_pooled,) = call(head_sum_kernel, (swap(pieces, TP),), (shaped((ROWS, HD), BF),), 100_000)
    (attn_out,) = call(
        slot_kernel,
        (c_ref, patch_first, moved, shift(out, CTX, N_CTX, 1), out),
        (shaped((ROWS, FEATS), BF),),
        5_000_000,
        3,
    )
    (byte_grad,) = call(
        byte_kernel,
        (c_ref, patch_first, patch_of_byte.reshape(n_bytes, 1), shift(d_pooled, CTX, N_CTX, 1), d_pooled),
        (shaped((n_bytes, HD), BF),),
        10_000_000,
        2,
    )
    return attn_out, byte_grad


def solution(mesh):
    fine = Mesh(mesh.devices.reshape(SIZES), NAMES)
    placed = (P(CTX, None), P(CTX), P(), P(), P(None, None, TP), P(CTX, TP))
    return jax.shard_map(
        shards,
        mesh=fine,
        in_specs=placed,
        out_specs=(P(CTX, TP), P(CTX, TP)),
        check_vma=False,
    )
```

```python
import jax
import jax.numpy as jnp
from jax import lax
from jax.experimental import pallas as pl
from jax.experimental.pallas import tpu as pltpu
from jax.sharding import Mesh, PartitionSpec as P

HD = 128
SIZES = (8, 2, 4, 8)
NAMES = ("z", "yl", "x", "tp")
CTX = ("z", "yl", "x")
N_CTX = 64
N_TP = 8
ROWS = 64
HEADS = 2
FEATS = HEADS * HD
TOTAL = N_CTX * ROWS
WINDOW = 2 * ROWS
HALF = ROWS // 2
PARTS_Q = 8
PARTS_K = 4
ROWS_Q = ROWS // PARTS_Q
ROWS_K = ROWS // PARTS_K
TILE_Q = N_CTX * ROWS_Q
TILE_K = N_CTX * ROWS_K
PIECE = 2 * ROWS_Q + 2 * ROWS_K
SCALE = HD ** (-0.5)
LOG2E = 1.4426950408889634
NEG = -1e30
FLOOR = -1e29
BF = jnp.bfloat16
F32 = jnp.float32
I32 = jnp.int32


def dot(a, b, dims):
    return lax.dot_general(a, b, (dims, ((), ())), preferred_element_type=F32)


def shift(x, axis, n, by):
    return lax.ppermute(x, axis, [(i, (i + by) % n) for i in range(n)])


def swap(x, axis):
    return lax.all_to_all(x, axis, split_axis=0, concat_axis=0, tiled=True)


def iota(shape, dim):
    return lax.broadcasted_iota(I32, shape, dim)


def call(kernel, ins, outs, flops, scalars=0):
    smem = pl.BlockSpec(memory_space=pltpu.SMEM)
    vmem = pl.BlockSpec(memory_space=pltpu.VMEM)
    size = sum(x.size * x.dtype.itemsize for x in list(ins) + list(outs))
    return pl.pallas_call(
        kernel,
        out_shape=tuple(outs),
        in_specs=[smem] * scalars + [vmem] * (len(ins) - scalars),
        out_specs=tuple([vmem] * len(outs)),
        cost_estimate=pl.CostEstimate(flops=flops, bytes_accessed=size, transcendentals=0),
        compiler_params=pltpu.CompilerParams(vmem_limit_bytes=40 * 1024 * 1024),
    )(*ins)


def shaped(shape, dtype):
    return jax.ShapeDtypeStruct(shape, dtype)


def slot_order(c, first_ref, moved_ref, shape, dim):
    before, after = jnp.maximum(c - 1, 0), jnp.minimum(c + 1, N_CTX - 1)
    first = first_ref[c]
    low = moved_ref[0, c]
    prev_high = jnp.where(c > 0, moved_ref[1, before], 0)
    next_low = jnp.where(c < N_CTX - 1, moved_ref[0, after], 0)
    next_first = jnp.where(c < N_CTX - 1, first_ref[after], TOTAL)
    rank = iota(shape, dim)
    order = jnp.where(
        rank < prev_high,
        first - prev_high + rank,
        jnp.where(
            rank >= ROWS - next_low,
            next_first + rank - (ROWS - next_low),
            first + low + rank - prev_high,
        ),
    )
    return order - (ROWS * c - HALF)


def pool_kernel(
    c_ref, first_hbm, moved_hbm, place_hbm, bytes_hbm, grad_hbm, w_hbm, sent_ref, own_ref,
    first_ref, moved_ref, place_ref, bytes_ref, grad_ref, w_ref, sems,
):
    pairs = (
        (first_hbm, first_ref),
        (moved_hbm, moved_ref),
        (place_hbm, place_ref),
        (bytes_hbm, bytes_ref),
        (grad_hbm, grad_ref),
        (w_hbm, w_ref),
    )
    copies = [pltpu.make_async_copy(a, b, sems.at[i]) for i, (a, b) in enumerate(pairs)]
    for copy in copies:
        copy.start()
    for copy in copies[:5]:
        copy.wait()
    c = c_ref[0]
    offset = first_ref[c] - (ROWS * c - HALF)
    member = iota((WINDOW, bytes_ref.shape[0]), 0) == place_ref[...] + offset
    lengths = jnp.sum(member.astype(F32), axis=1, keepdims=True)
    pooled = dot(member.astype(F32).astype(BF), bytes_ref[...], ((1,), (0,)))
    pooled = (pooled / jnp.maximum(lengths, 1.0)).astype(BF)
    order = slot_order(c, first_ref, moved_ref, (WINDOW, ROWS), 1)
    slotted = (iota((WINDOW, ROWS), 0) == order).astype(F32).astype(BF)
    grads = dot(slotted, grad_ref[...], ((1,), (0,))).astype(BF)
    copies[5].wait()
    for at, value in (
        (0, dot(pooled, w_ref[0], ((1,), (0,))).astype(BF)),
        (1, grads),
        (2, dot(pooled, w_ref[1], ((1,), (0,))).astype(BF)),
        (3, dot(pooled, w_ref[2], ((1,), (0,))).astype(BF)),
    ):
        sent_ref[:, at * FEATS : (at + 1) * FEATS] = value[:ROWS]
        own_ref[:, at * FEATS : (at + 1) * FEATS] = value[ROWS:]


def columns(value, kind, head):
    at = kind * FEATS + head * HD
    return value[:, at : at + HD]


def spread_kernel(own_ref, got_ref, piece_ref):
    both = own_ref[...] + got_ref[...]
    for e in range(HEADS):
        q, g, k, v = (columns(both, kind, e) for kind in range(4))
        for a in range(PARTS_Q):
            asked = slice(a * ROWS_Q, (a + 1) * ROWS_Q)
            for b in range(PARTS_K):
                held = slice(b * ROWS_K, (b + 1) * ROWS_K)
                piece_ref[(a * HEADS + e) * PARTS_K + b] = jnp.concatenate(
                    [q[asked], g[asked], k[held], v[held]], axis=0
                )


def unpack(piece_ref):
    q = piece_ref[:, :ROWS_Q, :].reshape(TILE_Q, HD)
    g = piece_ref[:, ROWS_Q : 2 * ROWS_Q, :].reshape(TILE_Q, HD)
    k = piece_ref[:, 2 * ROWS_Q : 2 * ROWS_Q + ROWS_K, :].reshape(TILE_K, HD)
    v = piece_ref[:, 2 * ROWS_Q + ROWS_K :, :].reshape(TILE_K, HD)
    return q, g, k, v


def scores(c, q, k):
    row = iota((1, TILE_Q), 1)
    query = ROWS * (row // ROWS_Q) + ROWS_Q * (c // (HEADS * PARTS_K)) + row % ROWS_Q + HALF
    col = iota((TILE_K, 1), 0)
    key = ROWS * (col // ROWS_K) + ROWS_K * (c % PARTS_K) + col % ROWS_K + HALF
    allowed = (query & (TOTAL - 1)) >= (key & (TOTAL - 1))
    return jnp.where(allowed, dot(k, q, ((1,), (1,))) * (SCALE * LOG2E), NEG)


def forward_kernel(c_ref, piece_ref, stats_ref):
    q, g, k, v = unpack(piece_ref)
    score = scores(c_ref[0], q, k)
    top = jnp.maximum(jnp.max(score, axis=0, keepdims=True), FLOOR)
    weight = jnp.exp2(score - top)
    dprob = dot(v, g, ((1,), (1,)))
    rows = [
        top,
        jnp.sum(weight, axis=0, keepdims=True),
        jnp.sum(weight * dprob, axis=0, keepdims=True),
    ]
    rows = jnp.concatenate(rows + [top] * 5, axis=0)
    for i in range(PARTS_K):
        stats_ref[i] = rows


def backward_kernel(c_ref, piece_ref, stats_ref, term_ref):
    tops, sums, dots = (stats_ref[:, i, :] for i in range(3))
    peak = jnp.max(tops, axis=0, keepdims=True)
    each = jnp.exp2(tops - peak)
    norm = jnp.sum(each * sums, axis=0, keepdims=True)
    delta = jnp.sum(each * dots, axis=0, keepdims=True) / norm
    lse = peak + jnp.log(norm) * LOG2E
    q, g, k, v = unpack(piece_ref)
    prob = jnp.exp2(scores(c_ref[0], q, k) - lse)
    dprob = dot(v, g, ((1,), (1,)))
    dscore = (prob * (dprob - delta)).astype(BF)
    prob = prob.astype(BF)
    d_query = dot(dscore, k, ((0,), (0,))) * SCALE
    out = dot(prob, v, ((0,), (0,)))
    d_key = dot(dscore, q, ((1,), (0,))) * SCALE
    d_value = dot(prob, g, ((1,), (0,)))
    term_ref[:, :ROWS_Q, :] = d_query.reshape(N_CTX, ROWS_Q, HD).astype(BF)
    term_ref[:, ROWS_Q : 2 * ROWS_Q, :] = out.reshape(N_CTX, ROWS_Q, HD).astype(BF)
    term_ref[:, 2 * ROWS_Q : 2 * ROWS_Q + ROWS_K, :] = d_key.reshape(N_CTX, ROWS_K, HD).astype(BF)
    term_ref[:, 2 * ROWS_Q + ROWS_K :, :] = d_value.reshape(N_CTX, ROWS_K, HD).astype(BF)


def sum_kernel(term_ref, w_ref, piece_ref, out_ref):
    terms = term_ref[...].astype(F32).reshape(PARTS_Q, HEADS, PARTS_K, PIECE, HD)
    asked = jnp.sum(terms[:, :, :, : 2 * ROWS_Q], axis=2)
    held = jnp.sum(terms[:, :, :, 2 * ROWS_Q :], axis=0)

    def joined(values):
        return jnp.concatenate([v.reshape(ROWS, HD) for v in values], axis=1).astype(BF)

    d_query = joined([asked[:, e, :ROWS_Q] for e in range(HEADS)])
    out_ref[...] = joined([asked[:, e, ROWS_Q:] for e in range(HEADS)])
    d_key = joined([held[e, :, :ROWS_K] for e in range(HEADS)])
    d_value = joined([held[e, :, ROWS_K:] for e in range(HEADS)])
    part = dot(d_query, w_ref[0], ((1,), (1,)))
    part = part + dot(d_key, w_ref[1], ((1,), (1,)))
    part = (part + dot(d_value, w_ref[2], ((1,), (1,)))).astype(BF)
    for i in range(N_TP):
        piece_ref[i] = part[:, i * HD : (i + 1) * HD]


def head_sum_kernel(pieces_ref, sum_ref):
    sum_ref[...] = jnp.sum(pieces_ref[...].astype(F32), axis=0).astype(BF)


def slot_kernel(c_ref, first_ref, moved_ref, before_ref, own_ref, out_ref):
    order = slot_order(c_ref[0], first_ref, moved_ref, (ROWS, WINDOW), 0)
    picker = (iota((ROWS, WINDOW), 1) == order).astype(F32).astype(BF)
    window = jnp.concatenate([before_ref[...], own_ref[...]], axis=0)
    out_ref[...] = dot(picker, window, ((1,), (0,))).astype(BF)


def byte_kernel(c_ref, first_ref, place_ref, before_ref, own_ref, out_ref):
    c = c_ref[0]
    offset = first_ref[c] - (ROWS * c - HALF)
    member = (iota((place_ref.shape[0], WINDOW), 1) == place_ref[...] + offset).astype(F32)
    lengths = jnp.sum(member, axis=0, keepdims=True)
    own_length = jnp.sum(member * lengths, axis=1, keepdims=True)
    window = jnp.concatenate([before_ref[...], own_ref[...]], axis=0)
    out_ref[...] = (dot(member.astype(BF), window, ((1,), (0,))) / own_length).astype(BF)


def pool(c_ref, first, moved, place, byte_states, d_attn, w_qkv):
    hbm = pl.BlockSpec(memory_space=pltpu.HBM)
    vmem = pl.BlockSpec(memory_space=pltpu.VMEM)
    ins = (first, moved, place, byte_states, d_attn, w_qkv)
    spaces = (pltpu.SMEM, pltpu.SMEM) + (pltpu.VMEM,) * 4
    block = shaped((ROWS, 4 * FEATS), BF)
    return pl.pallas_call(
        pool_kernel,
        out_shape=(block, block),
        in_specs=[pl.BlockSpec(memory_space=pltpu.SMEM)] + [hbm] * len(ins),
        out_specs=(vmem, vmem),
        scratch_shapes=[space(x.shape, x.dtype) for space, x in zip(spaces, ins)]
        + [pltpu.SemaphoreType.DMA((len(ins),))],
        cost_estimate=pl.CostEstimate(flops=300_000_000, bytes_accessed=2_500_000, transcendentals=0),
        compiler_params=pltpu.CompilerParams(vmem_limit_bytes=60 * 1024 * 1024),
    )(c_ref, *ins)


def shards(byte_states, patch_of_byte, patch_first, moved, w_qkv, d_attn):
    c_ref = lax.axis_index(CTX).astype(I32).reshape(1)
    n_bytes = patch_of_byte.shape[0]
    stack = shaped((N_CTX, PIECE, HD), BF)

    sent, own = pool(
        c_ref, patch_first, moved, patch_of_byte.reshape(1, n_bytes), byte_states, d_attn, w_qkv
    )
    (pieces,) = call(spread_kernel, (own, shift(sent, CTX, N_CTX, -1)), (stack,), 1_000_000)
    pieces = swap(pieces, CTX)
    (stats,) = call(
        forward_kernel,
        (c_ref, pieces),
        (shaped((PARTS_K, 8, TILE_Q), F32),),
        300_000_000,
        1,
    )
    (terms,) = call(
        backward_kernel, (c_ref, pieces, swap(stats, "x")), (stack,), 900_000_000, 1
    )
    pieces, out = call(
        sum_kernel,
        (swap(terms, CTX), w_qkv),
        (shaped((N_TP, ROWS, HD), BF), shaped((ROWS, FEATS), BF)),
        100_000_000,
    )
    (d_pooled,) = call(head_sum_kernel, (swap(pieces, "tp"),), (shaped((ROWS, HD), BF),), 100_000)
    (attn_out,) = call(
        slot_kernel,
        (c_ref, patch_first, moved, shift(out, CTX, N_CTX, 1), out),
        (shaped((ROWS, FEATS), BF),),
        5_000_000,
        3,
    )
    (byte_grad,) = call(
        byte_kernel,
        (c_ref, patch_first, patch_of_byte.reshape(n_bytes, 1), shift(d_pooled, CTX, N_CTX, 1), d_pooled),
        (shaped((n_bytes, HD), BF),),
        10_000_000,
        2,
    )
    return attn_out, byte_grad


def solution(mesh):
    fine = Mesh(mesh.devices.reshape(SIZES), NAMES)
    placed = (P(CTX, None), P(CTX), P(), P(), P(None, None, "tp"), P(CTX, "tp"))
    return jax.shard_map(
        shards,
        mesh=fine,
        in_specs=placed,
        out_specs=(P(CTX, "tp"), P(CTX, "tp")),
        check_vma=False,
    )
```

```python
import jax
import jax.numpy as jnp
from jax import lax
from jax.experimental import pallas as pl
from jax.experimental.pallas import tpu as pltpu
from jax.sharding import Mesh, PartitionSpec as P

HD = 128
SIZES = (8, 2, 4, 8)
NAMES = ("z", "yl", "x", "tp")
CTX = ("z", "yl", "x")
N_CTX = 64
N_TP = 8
ROWS = 64
HEADS = 2
FEATS = HEADS * HD
TOTAL = N_CTX * ROWS
WINDOW = 2 * ROWS
HALF = ROWS // 2
PARTS_Q = 8
PARTS_K = 4
ROWS_Q = ROWS // PARTS_Q
ROWS_K = ROWS // PARTS_K
TILE_Q = N_CTX * ROWS_Q
TILE_K = N_CTX * ROWS_K
PIECE = 2 * ROWS_Q + 2 * ROWS_K
SCALE = HD ** (-0.5)
LOG2E = 1.4426950408889634
NEG = -1e30
FLOOR = -1e29
BF = jnp.bfloat16
F32 = jnp.float32
I32 = jnp.int32


def dot(a, b, dims):
    return lax.dot_general(a, b, (dims, ((), ())), preferred_element_type=F32)


def shift(x, axis, n, by):
    return lax.ppermute(x, axis, [(i, (i + by) % n) for i in range(n)])


def swap(x, axis):
    return lax.all_to_all(x, axis, split_axis=0, concat_axis=0, tiled=True)


def iota(shape, dim):
    return lax.broadcasted_iota(I32, shape, dim)


def call(kernel, ins, outs, flops, scalars=0):
    smem = pl.BlockSpec(memory_space=pltpu.SMEM)
    vmem = pl.BlockSpec(memory_space=pltpu.VMEM)
    size = sum(x.size * x.dtype.itemsize for x in list(ins) + list(outs))
    return pl.pallas_call(
        kernel,
        out_shape=tuple(outs),
        in_specs=[smem] * scalars + [vmem] * (len(ins) - scalars),
        out_specs=tuple([vmem] * len(outs)),
        cost_estimate=pl.CostEstimate(flops=flops, bytes_accessed=size, transcendentals=0),
        compiler_params=pltpu.CompilerParams(vmem_limit_bytes=40 * 1024 * 1024),
    )(*ins)


def shaped(shape, dtype):
    return jax.ShapeDtypeStruct(shape, dtype)


def slot_order(c, first_ref, moved_ref, shape, dim):
    before, after = jnp.maximum(c - 1, 0), jnp.minimum(c + 1, N_CTX - 1)
    first = first_ref[c]
    low = moved_ref[0, c]
    prev_high = jnp.where(c > 0, moved_ref[1, before], 0)
    next_low = jnp.where(c < N_CTX - 1, moved_ref[0, after], 0)
    next_first = jnp.where(c < N_CTX - 1, first_ref[after], TOTAL)
    rank = iota(shape, dim)
    order = jnp.where(
        rank < prev_high,
        first - prev_high + rank,
        jnp.where(
            rank >= ROWS - next_low,
            next_first + rank - (ROWS - next_low),
            first + low + rank - prev_high,
        ),
    )
    return order - (ROWS * c - HALF)


def pool_kernel(
    c_ref, first_hbm, moved_hbm, place_hbm, bytes_hbm, grad_hbm, w_hbm, sent_ref, own_ref,
    first_ref, moved_ref, place_ref, bytes_ref, grad_ref, w_ref, sems,
):
    pairs = [
        (first_hbm, first_ref),
        (moved_hbm, moved_ref),
        (place_hbm, place_ref),
        (bytes_hbm, bytes_ref),
        (grad_hbm, grad_ref),
    ] + [(w_hbm.at[i], w_ref.at[i]) for i in range(3)]
    copies = [pltpu.make_async_copy(a, b, sems.at[i]) for i, (a, b) in enumerate(pairs)]
    for copy in copies:
        copy.start()
    for copy in copies[:5]:
        copy.wait()
    c = c_ref[0]
    offset = first_ref[c] - (ROWS * c - HALF)
    member = iota((WINDOW, bytes_ref.shape[0]), 0) == place_ref[...] + offset
    lengths = jnp.sum(member.astype(F32), axis=1, keepdims=True)
    pooled = dot(member.astype(F32).astype(BF), bytes_ref[...], ((1,), (0,)))
    pooled = (pooled / jnp.maximum(lengths, 1.0)).astype(BF)
    order = slot_order(c, first_ref, moved_ref, (WINDOW, ROWS), 1)
    slotted = (iota((WINDOW, ROWS), 0) == order).astype(F32).astype(BF)
    grads = dot(slotted, grad_ref[...], ((1,), (0,))).astype(BF)
    for at, value in ((0, None), (1, grads), (2, None), (3, None)):
        if value is None:
            part = max(at - 1, 0)
            copies[5 + part].wait()
            value = dot(pooled, w_ref[part], ((1,), (0,))).astype(BF)
        sent_ref[:, at * FEATS : (at + 1) * FEATS] = value[:ROWS]
        own_ref[:, at * FEATS : (at + 1) * FEATS] = value[ROWS:]


def columns(value, kind, head):
    at = kind * FEATS + head * HD
    return value[:, at : at + HD]


def hold_kernel(own_ref, held_ref):
    held_ref[...] = own_ref[...]


def spread_kernel(own_ref, got_ref, piece_ref):
    both = own_ref[...] + got_ref[...]
    for e in range(HEADS):
        q, g, k, v = (columns(both, kind, e) for kind in range(4))
        for a in range(PARTS_Q):
            asked = slice(a * ROWS_Q, (a + 1) * ROWS_Q)
            for b in range(PARTS_K):
                held = slice(b * ROWS_K, (b + 1) * ROWS_K)
                piece_ref[(a * HEADS + e) * PARTS_K + b] = jnp.concatenate(
                    [q[asked], g[asked], k[held], v[held]], axis=0
                )


def unpack(piece_ref):
    q = piece_ref[:, :ROWS_Q, :].reshape(TILE_Q, HD)
    g = piece_ref[:, ROWS_Q : 2 * ROWS_Q, :].reshape(TILE_Q, HD)
    k = piece_ref[:, 2 * ROWS_Q : 2 * ROWS_Q + ROWS_K, :].reshape(TILE_K, HD)
    v = piece_ref[:, 2 * ROWS_Q + ROWS_K :, :].reshape(TILE_K, HD)
    return q, g, k, v


def scores(c, q, k):
    row = iota((1, TILE_Q), 1)
    query = ROWS * (row // ROWS_Q) + ROWS_Q * (c // (HEADS * PARTS_K)) + row % ROWS_Q + HALF
    col = iota((TILE_K, 1), 0)
    key = ROWS * (col // ROWS_K) + ROWS_K * (c % PARTS_K) + col % ROWS_K + HALF
    allowed = (query & (TOTAL - 1)) >= (key & (TOTAL - 1))
    return jnp.where(allowed, dot(k, q, ((1,), (1,))) * (SCALE * LOG2E), NEG)


def forward_kernel(c_ref, piece_ref, stats_ref):
    q, g, k, v = unpack(piece_ref)
    score = scores(c_ref[0], q, k)
    top = jnp.maximum(jnp.max(score, axis=0, keepdims=True), FLOOR)
    weight = jnp.exp2(score - top)
    dprob = dot(v, g, ((1,), (1,)))
    rows = [
        top,
        jnp.sum(weight, axis=0, keepdims=True),
        jnp.sum(weight * dprob, axis=0, keepdims=True),
    ]
    rows = jnp.concatenate(rows + [top] * 5, axis=0)
    for i in range(PARTS_K):
        stats_ref[i] = rows


def backward_kernel(c_ref, piece_ref, stats_ref, term_ref):
    tops, sums, dots = (stats_ref[:, i, :] for i in range(3))
    peak = jnp.max(tops, axis=0, keepdims=True)
    each = jnp.exp2(tops - peak)
    norm = jnp.sum(each * sums, axis=0, keepdims=True)
    delta = jnp.sum(each * dots, axis=0, keepdims=True) / norm
    lse = peak + jnp.log(norm) * LOG2E
    q, g, k, v = unpack(piece_ref)
    prob = jnp.exp2(scores(c_ref[0], q, k) - lse)
    dprob = dot(v, g, ((1,), (1,)))
    dscore = (prob * (dprob - delta)).astype(BF)
    prob = prob.astype(BF)
    d_query = dot(dscore, k, ((0,), (0,))) * SCALE
    out = dot(prob, v, ((0,), (0,)))
    d_key = dot(dscore, q, ((1,), (0,))) * SCALE
    d_value = dot(prob, g, ((1,), (0,)))
    term_ref[:, :ROWS_Q, :] = d_query.reshape(N_CTX, ROWS_Q, HD).astype(BF)
    term_ref[:, ROWS_Q : 2 * ROWS_Q, :] = out.reshape(N_CTX, ROWS_Q, HD).astype(BF)
    term_ref[:, 2 * ROWS_Q : 2 * ROWS_Q + ROWS_K, :] = d_key.reshape(N_CTX, ROWS_K, HD).astype(BF)
    term_ref[:, 2 * ROWS_Q + ROWS_K :, :] = d_value.reshape(N_CTX, ROWS_K, HD).astype(BF)


def sum_kernel(term_ref, w_ref, piece_ref, out_ref):
    terms = term_ref[...].astype(F32).reshape(PARTS_Q, HEADS, PARTS_K, PIECE, HD)
    asked = jnp.sum(terms[:, :, :, : 2 * ROWS_Q], axis=2)
    held = jnp.sum(terms[:, :, :, 2 * ROWS_Q :], axis=0)

    def joined(values):
        return jnp.concatenate([v.reshape(ROWS, HD) for v in values], axis=1).astype(BF)

    d_query = joined([asked[:, e, :ROWS_Q] for e in range(HEADS)])
    out_ref[...] = joined([asked[:, e, ROWS_Q:] for e in range(HEADS)])
    d_key = joined([held[e, :, :ROWS_K] for e in range(HEADS)])
    d_value = joined([held[e, :, ROWS_K:] for e in range(HEADS)])
    part = dot(d_query, w_ref[0], ((1,), (1,)))
    part = part + dot(d_key, w_ref[1], ((1,), (1,)))
    part = (part + dot(d_value, w_ref[2], ((1,), (1,)))).astype(BF)
    for i in range(N_TP):
        piece_ref[i] = part[:, i * HD : (i + 1) * HD]


def place_kernel(c_ref, first_ref, moved_ref, place_ref, picker_ref, member_ref, length_ref):
    c = c_ref[0]
    order = slot_order(c, first_ref, moved_ref, (ROWS, WINDOW), 0)
    picker_ref[...] = (iota((ROWS, WINDOW), 1) == order).astype(F32).astype(BF)
    offset = first_ref[c] - (ROWS * c - HALF)
    member = (iota((WINDOW, place_ref.shape[1]), 0) == place_ref[...] + offset).astype(F32)
    lengths = jnp.sum(member, axis=1, keepdims=True)
    member = member.T
    member_ref[...] = member.astype(BF)
    spread = jnp.broadcast_to(lengths, (WINDOW, HD)).astype(BF)
    length_ref[...] = dot(member.astype(BF), spread, ((1,), (0,)))


def head_sum_kernel(pieces_ref, out_ref, both_ref):
    both_ref[:, :HD] = jnp.sum(pieces_ref[...].astype(F32), axis=0).astype(BF)
    both_ref[:, HD:] = out_ref[...]


def last_kernel(before_ref, own_ref, picker_ref, member_ref, length_ref, out_ref, grad_ref):
    window = jnp.concatenate([before_ref[...], own_ref[...]], axis=0)
    out_ref[...] = dot(picker_ref[...], window[:, HD:], ((1,), (0,))).astype(BF)
    spread = dot(member_ref[...], window[:, :HD], ((1,), (0,)))
    grad_ref[...] = (spread / length_ref[...]).astype(BF)


def pool(c_ref, first, moved, place, byte_states, d_attn, w_qkv):
    hbm = pl.BlockSpec(memory_space=pltpu.HBM)
    vmem = pl.BlockSpec(memory_space=pltpu.VMEM)
    ins = (first, moved, place, byte_states, d_attn, w_qkv)
    spaces = (pltpu.SMEM, pltpu.SMEM) + (pltpu.VMEM,) * 4
    block = shaped((ROWS, 4 * FEATS), BF)
    return pl.pallas_call(
        pool_kernel,
        out_shape=(block, block),
        in_specs=[pl.BlockSpec(memory_space=pltpu.SMEM)] + [hbm] * len(ins),
        out_specs=(vmem, vmem),
        scratch_shapes=[space(x.shape, x.dtype) for space, x in zip(spaces, ins)]
        + [pltpu.SemaphoreType.DMA((len(ins) + 2,))],
        cost_estimate=pl.CostEstimate(flops=300_000_000, bytes_accessed=2_500_000, transcendentals=0),
        compiler_params=pltpu.CompilerParams(vmem_limit_bytes=60 * 1024 * 1024),
    )(c_ref, *ins)


def shards(byte_states, patch_of_byte, patch_first, moved, w_qkv, d_attn):
    c_ref = lax.axis_index(CTX).astype(I32).reshape(1)
    n_bytes = patch_of_byte.shape[0]
    stack = shaped((N_CTX, PIECE, HD), BF)
    place = patch_of_byte.reshape(1, n_bytes)

    sent, own = pool(
        c_ref, patch_first, moved, place, byte_states, d_attn, w_qkv
    )
    (own,) = call(hold_kernel, (own,), (shaped(own.shape, BF),), 100_000)
    (pieces,) = call(spread_kernel, (own, shift(sent, CTX, N_CTX, -1)), (stack,), 1_000_000)
    pieces = swap(pieces, CTX)
    (stats,) = call(
        forward_kernel,
        (c_ref, pieces),
        (shaped((PARTS_K, 8, TILE_Q), F32),),
        300_000_000,
        1,
    )
    (terms,) = call(
        backward_kernel, (c_ref, pieces, swap(stats, "x")), (stack,), 900_000_000, 1
    )
    pieces, out = call(
        sum_kernel,
        (swap(terms, CTX), w_qkv),
        (shaped((N_TP, ROWS, HD), BF), shaped((ROWS, FEATS), BF)),
        100_000_000,
    )
    (both,) = call(
        head_sum_kernel, (swap(pieces, "tp"), out), (shaped((ROWS, HD + FEATS), BF),), 100_000
    )
    picker, member, length = call(
        place_kernel,
        (c_ref, patch_first, moved, place),
        (
            shaped((ROWS, WINDOW), BF),
            shaped((n_bytes, WINDOW), BF),
            shaped((n_bytes, HD), F32),
        ),
        10_000_000,
        3,
    )
    attn_out, byte_grad = call(
        last_kernel,
        (shift(both, CTX, N_CTX, 1), both, picker, member, length),
        (shaped((ROWS, FEATS), BF), shaped((n_bytes, HD), BF)),
        10_000_000,
    )
    return attn_out, byte_grad


def solution(mesh):
    fine = Mesh(mesh.devices.reshape(SIZES), NAMES)
    placed = (P(CTX, None), P(CTX), P(), P(), P(None, None, "tp"), P(CTX, "tp"))
    return jax.shard_map(
        shards,
        mesh=fine,
        in_specs=placed,
        out_specs=(P(CTX, "tp"), P(CTX, "tp")),
        check_vma=False,
    )
```

```python
import jax
import jax.numpy as jnp
from jax import lax
from jax.experimental import pallas as pl
from jax.experimental.pallas import tpu as pltpu
from jax.sharding import Mesh, PartitionSpec as P

HD = 128
SIZES = (4, 2, 2, 2, 2, 8)
NAMES = ("zh", "zl", "yl", "xh", "xl", "tp")
CTX = ("zh", "zl", "yl", "xh", "xl")
FAR = ("zh", "zl", "xh")
NEAR = ("yl", "xl")
N_CTX = 64
N_TP = 8
N_FAR = 16
N_NEAR = 4
N_ASK = 8
ROWS = 64
HEADS = 2
FEATS = HEADS * HD
TOTAL = N_CTX * ROWS
WINDOW = 2 * ROWS
HALF = ROWS // 2
TILE_Q = N_ASK * ROWS
TILE_K = N_FAR * ROWS
SCALE = HD ** (-0.5)
LOG2E = 1.4426950408889634
NEG = -1e30
FLOOR = -1e29
BF = jnp.bfloat16
F32 = jnp.float32
I32 = jnp.int32


def dot(a, b, dims):
    return lax.dot_general(a, b, (dims, ((), ())), preferred_element_type=F32)


def shift(x, axis, n, by):
    return lax.ppermute(x, axis, [(i, (i + by) % n) for i in range(n)])


def swap(x, axis):
    return lax.all_to_all(x, axis, split_axis=0, concat_axis=0, tiled=True)


def iota(shape, dim):
    return lax.broadcasted_iota(I32, shape, dim)


def call(kernel, ins, outs, flops, scalars=0):
    smem = pl.BlockSpec(memory_space=pltpu.SMEM)
    vmem = pl.BlockSpec(memory_space=pltpu.VMEM)
    size = sum(x.size * x.dtype.itemsize for x in list(ins) + list(outs))
    return pl.pallas_call(
        kernel,
        out_shape=tuple(outs),
        in_specs=[smem] * scalars + [vmem] * (len(ins) - scalars),
        out_specs=tuple([vmem] * len(outs)),
        cost_estimate=pl.CostEstimate(flops=flops, bytes_accessed=size, transcendentals=0),
        compiler_params=pltpu.CompilerParams(vmem_limit_bytes=40 * 1024 * 1024),
    )(*ins)


def shaped(shape, dtype):
    return jax.ShapeDtypeStruct(shape, dtype)


def slot_order(c, first_ref, moved_ref, shape, dim):
    before, after = jnp.maximum(c - 1, 0), jnp.minimum(c + 1, N_CTX - 1)
    first = first_ref[c]
    low = moved_ref[0, c]
    prev_high = jnp.where(c > 0, moved_ref[1, before], 0)
    next_low = jnp.where(c < N_CTX - 1, moved_ref[0, after], 0)
    next_first = jnp.where(c < N_CTX - 1, first_ref[after], TOTAL)
    rank = iota(shape, dim)
    order = jnp.where(
        rank < prev_high,
        first - prev_high + rank,
        jnp.where(
            rank >= ROWS - next_low,
            next_first + rank - (ROWS - next_low),
            first + low + rank - prev_high,
        ),
    )
    return order - (ROWS * c - HALF)


def pool_kernel(
    c_ref, first_hbm, moved_hbm, place_hbm, bytes_hbm, grad_hbm, w_hbm, sent_ref, own_ref,
    first_ref, moved_ref, place_ref, bytes_ref, grad_ref, w_ref, sems,
):
    pairs = [
        (first_hbm, first_ref),
        (moved_hbm, moved_ref),
        (place_hbm, place_ref),
        (bytes_hbm, bytes_ref),
        (grad_hbm, grad_ref),
    ] + [(w_hbm.at[i], w_ref.at[i]) for i in range(3)]
    copies = [pltpu.make_async_copy(a, b, sems.at[i]) for i, (a, b) in enumerate(pairs)]
    for copy in copies:
        copy.start()
    for copy in copies[:5]:
        copy.wait()
    c = c_ref[0]
    offset = first_ref[c] - (ROWS * c - HALF)
    member = iota((WINDOW, bytes_ref.shape[0]), 0) == place_ref[...] + offset
    lengths = jnp.sum(member.astype(F32), axis=1, keepdims=True)
    pooled = dot(member.astype(F32).astype(BF), bytes_ref[...], ((1,), (0,)))
    pooled = (pooled / jnp.maximum(lengths, 1.0)).astype(BF)
    order = slot_order(c, first_ref, moved_ref, (WINDOW, ROWS), 1)
    slotted = (iota((WINDOW, ROWS), 0) == order).astype(F32).astype(BF)
    grads = dot(slotted, grad_ref[...], ((1,), (0,))).astype(BF)
    for at, value in ((0, None), (1, grads), (2, None), (3, None)):
        if value is None:
            part = max(at - 1, 0)
            copies[5 + part].wait()
            value = dot(pooled, w_ref[part], ((1,), (0,))).astype(BF)
        sent_ref[:, at * FEATS : (at + 1) * FEATS] = value[:ROWS]
        own_ref[:, at * FEATS : (at + 1) * FEATS] = value[ROWS:]


def columns(value, kind, head):
    at = kind * FEATS + head * HD
    return value[:, at : at + HD]


def hold_kernel(own_ref, held_ref):
    held_ref[...] = own_ref[...]


def spread_kernel(c_ref, own_ref, got_ref, keep_ref, give_ref, held_ref):
    both = own_ref[...] + got_ref[...]
    asked, held = [], []
    for e in range(HEADS):
        q, g, k, v = (columns(both, kind, e) for kind in range(4))
        asked.append(jnp.concatenate([q, g], axis=1))
        held.append(jnp.concatenate([k, v], axis=1))
    second = ((c_ref[0] >> 3) & 1) == 1
    keep_ref[...] = jnp.where(second, asked[1], asked[0])
    give_ref[...] = jnp.where(second, asked[0], asked[1])
    for i in range(N_FAR):
        held_ref[i] = held[(i >> 1) & 1]


def unpack(asked_ref, held_ref):
    k = held_ref[:, :, :HD].reshape(TILE_K, HD)
    v = held_ref[:, :, HD:].reshape(TILE_K, HD)
    return asked_ref[:, :HD], asked_ref[:, HD:], k, v


def scores(c, q, k):
    row = iota((1, TILE_Q), 1)
    block = ((row >> 6) & 1) * 8 + ((row >> 7) & 1) + ((row >> 8) & 1) * 4 + (c & 50)
    query = ROWS * block + (row & 63) + HALF
    col = iota((TILE_K, 1), 0)
    block = (col >> 8) * 16 + ((col >> 7) & 1) * 8 + ((col >> 6) & 1) * 2 + (c & 5)
    key = ROWS * block + (col & 63) + HALF
    allowed = (query & (TOTAL - 1)) >= (key & (TOTAL - 1))
    return jnp.where(allowed, dot(k, q, ((1,), (1,))) * (SCALE * LOG2E), NEG)


def forward_kernel(c_ref, asked_ref, held_ref, stats_ref):
    q, g, k, v = unpack(asked_ref, held_ref)
    score = scores(c_ref[0], q, k)
    top = jnp.maximum(jnp.max(score, axis=0, keepdims=True), FLOOR)
    weight = jnp.exp2(score - top)
    dprob = dot(v, g, ((1,), (1,)))
    rows = [
        top,
        jnp.sum(weight, axis=0, keepdims=True),
        jnp.sum(weight * dprob, axis=0, keepdims=True),
    ]
    rows = jnp.concatenate(rows + [top] * 5, axis=0)
    for i in range(N_NEAR):
        stats_ref[i] = rows


def backward_kernel(c_ref, asked_ref, held_ref, stats_ref, term_ref, keep_ref, give_ref):
    tops, sums, dots = (stats_ref[:, i, :] for i in range(3))
    peak = jnp.max(tops, axis=0, keepdims=True)
    each = jnp.exp2(tops - peak)
    norm = jnp.sum(each * sums, axis=0, keepdims=True)
    delta = jnp.sum(each * dots, axis=0, keepdims=True) / norm
    lse = peak + jnp.log(norm) * LOG2E
    q, g, k, v = unpack(asked_ref, held_ref)
    prob = jnp.exp2(scores(c_ref[0], q, k) - lse)
    dprob = dot(v, g, ((1,), (1,)))
    dscore = (prob * (dprob - delta)).astype(BF)
    prob = prob.astype(BF)
    d_key = (dot(dscore, q, ((1,), (0,))) * SCALE).astype(BF)
    d_value = dot(prob, g, ((1,), (0,))).astype(BF)
    term_ref[:, :, :HD] = d_key.reshape(N_FAR, ROWS, HD)
    term_ref[:, :, HD:] = d_value.reshape(N_FAR, ROWS, HD)
    d_query = dot(dscore, k, ((0,), (0,))) * SCALE
    out = dot(prob, v, ((0,), (0,)))
    second = ((c_ref[0] >> 2) & 1) == 1
    half = TILE_Q // 2
    for value, at in ((d_query, 0), (out, HD)):
        keep_ref[:, at : at + HD] = jnp.where(second, value[half:], value[:half])
        give_ref[:, at : at + HD] = jnp.where(second, value[:half], value[half:]).astype(BF)


def sum_kernel(c_ref, term_ref, keep_ref, got_ref, w_ref, piece_ref, out_ref):
    second = ((c_ref[0] >> 3) & 1) == 1
    keep, got = keep_ref[...].astype(BF), got_ref[...]
    asked = [jnp.where(second, got, keep), jnp.where(second, keep, got)]
    d_query = jnp.concatenate([x[:, :HD] for x in asked], axis=1)
    out_ref[...] = jnp.concatenate([x[:, HD:] for x in asked], axis=1)
    held = []
    for e in range(HEADS):
        total = jnp.zeros((ROWS, 2 * HD), F32)
        for i in range(N_FAR):
            if (i >> 1) & 1 == e:
                total = total + term_ref[i].astype(F32)
        held.append(total.astype(BF))
    d_key = jnp.concatenate([x[:, :HD] for x in held], axis=1)
    d_value = jnp.concatenate([x[:, HD:] for x in held], axis=1)
    part = dot(d_query, w_ref[0], ((1,), (1,)))
    part = part + dot(d_key, w_ref[1], ((1,), (1,)))
    part = (part + dot(d_value, w_ref[2], ((1,), (1,)))).astype(BF)
    for i in range(N_TP):
        piece_ref[i] = part[:, i * HD : (i + 1) * HD]


def place_kernel(c_ref, first_ref, moved_ref, place_ref, picker_ref, member_ref, length_ref):
    c = c_ref[0]
    order = slot_order(c, first_ref, moved_ref, (ROWS, WINDOW), 0)
    picker_ref[...] = (iota((ROWS, WINDOW), 1) == order).astype(F32).astype(BF)
    offset = first_ref[c] - (ROWS * c - HALF)
    member = (iota((WINDOW, place_ref.shape[1]), 0) == place_ref[...] + offset).astype(F32)
    lengths = jnp.sum(member, axis=1, keepdims=True)
    member = member.T
    member_ref[...] = member.astype(BF)
    spread = jnp.broadcast_to(lengths, (WINDOW, HD)).astype(BF)
    length_ref[...] = dot(member.astype(BF), spread, ((1,), (0,)))


def head_sum_kernel(pieces_ref, out_ref, both_ref):
    both_ref[:, :HD] = jnp.sum(pieces_ref[...].astype(F32), axis=0).astype(BF)
    both_ref[:, HD:] = out_ref[...]


def last_kernel(before_ref, own_ref, picker_ref, member_ref, length_ref, out_ref, grad_ref):
    window = jnp.concatenate([before_ref[...], own_ref[...]], axis=0)
    out_ref[...] = dot(picker_ref[...], window[:, HD:], ((1,), (0,))).astype(BF)
    spread = dot(member_ref[...], window[:, :HD], ((1,), (0,)))
    grad_ref[...] = (spread / length_ref[...]).astype(BF)


def pool(c_ref, first, moved, place, byte_states, d_attn, w_qkv):
    hbm = pl.BlockSpec(memory_space=pltpu.HBM)
    vmem = pl.BlockSpec(memory_space=pltpu.VMEM)
    ins = (first, moved, place, byte_states, d_attn, w_qkv)
    spaces = (pltpu.SMEM, pltpu.SMEM) + (pltpu.VMEM,) * 4
    block = shaped((ROWS, 4 * FEATS), BF)
    return pl.pallas_call(
        pool_kernel,
        out_shape=(block, block),
        in_specs=[pl.BlockSpec(memory_space=pltpu.SMEM)] + [hbm] * len(ins),
        out_specs=(vmem, vmem),
        scratch_shapes=[space(x.shape, x.dtype) for space, x in zip(spaces, ins)]
        + [pltpu.SemaphoreType.DMA((len(ins) + 2,))],
        cost_estimate=pl.CostEstimate(flops=300_000_000, bytes_accessed=2_500_000, transcendentals=0),
        compiler_params=pltpu.CompilerParams(vmem_limit_bytes=60 * 1024 * 1024),
    )(c_ref, *ins)


def doubled(mine, axis):
    got = shift(mine, axis, 2, 1)
    second = lax.axis_index(axis) == 1
    return jnp.concatenate([jnp.where(second, got, mine), jnp.where(second, mine, got)], axis=0)


def halved(keep, got, axis):
    total = keep + got.astype(F32)
    half = total.shape[0] // 2
    second = lax.axis_index(axis) == 1
    keep = jnp.where(second, total[half:], total[:half])
    return keep, jnp.where(second, total[:half], total[half:]).astype(BF)


def shards(byte_states, patch_of_byte, patch_first, moved, w_qkv, d_attn):
    c_ref = lax.axis_index(CTX).astype(I32).reshape(1)
    n_bytes = patch_of_byte.shape[0]
    place = patch_of_byte.reshape(1, n_bytes)
    pair = shaped((ROWS, 2 * HD), BF)
    stack = shaped((N_FAR, ROWS, 2 * HD), BF)

    sent, own = pool(c_ref, patch_first, moved, place, byte_states, d_attn, w_qkv)
    (own,) = call(hold_kernel, (own,), (shaped(own.shape, BF),), 100_000)
    keep, give, held = call(
        spread_kernel, (c_ref, own, shift(sent, CTX, N_CTX, -1)), (pair, pair, stack), 1_000_000, 1
    )
    held = swap(held, FAR)
    got = shift(give, "zl", 2, 1)
    second = lax.axis_index("zl") == 1
    asked = jnp.concatenate([jnp.where(second, got, keep), jnp.where(second, keep, got)], axis=0)
    asked = doubled(doubled(asked, "xl"), "yl")
    (stats,) = call(
        forward_kernel,
        (c_ref, asked, held),
        (shaped((N_NEAR, 8, TILE_Q), F32),),
        300_000_000,
        1,
    )
    half = (TILE_Q // 2, 2 * HD)
    terms, keep, give = call(
        backward_kernel,
        (c_ref, asked, held, swap(stats, NEAR)),
        (stack, shaped(half, F32), shaped(half, BF)),
        900_000_000,
        1,
    )
    terms = swap(terms, FAR)
    keep, give = halved(keep, shift(give, "yl", 2, 1), "xl")
    keep, give = halved(keep, shift(give, "xl", 2, 1), "zl")
    pieces, out = call(
        sum_kernel,
        (c_ref, terms, keep, shift(give, "zl", 2, 1), w_qkv),
        (shaped((N_TP, ROWS, HD), BF), shaped((ROWS, FEATS), BF)),
        100_000_000,
        1,
    )
    (both,) = call(
        head_sum_kernel, (swap(pieces, "tp"), out), (shaped((ROWS, HD + FEATS), BF),), 100_000
    )
    picker, member, length = call(
        place_kernel,
        (c_ref, patch_first, moved, place),
        (
            shaped((ROWS, WINDOW), BF),
            shaped((n_bytes, WINDOW), BF),
            shaped((n_bytes, HD), F32),
        ),
        10_000_000,
        3,
    )
    attn_out, byte_grad = call(
        last_kernel,
        (shift(both, CTX, N_CTX, 1), both, picker, member, length),
        (shaped((ROWS, FEATS), BF), shaped((n_bytes, HD), BF)),
        10_000_000,
    )
    return attn_out, byte_grad


def solution(mesh):
    fine = Mesh(mesh.devices.reshape(SIZES), NAMES)
    placed = (P(CTX, None), P(CTX), P(), P(), P(None, None, "tp"), P(CTX, "tp"))
    return jax.shard_map(
        shards,
        mesh=fine,
        in_specs=placed,
        out_specs=(P(CTX, "tp"), P(CTX, "tp")),
        check_vma=False,
    )
```

```python
import jax
import jax.numpy as jnp
from jax import lax
from jax.experimental import pallas as pl
from jax.experimental.pallas import tpu as pltpu
from jax.sharding import Mesh, PartitionSpec as P

HD = 128
SIZES = (4, 2, 2, 2, 2, 8)
NAMES = ("zh", "zl", "yl", "xh", "xl", "tp")
CTX = ("zh", "zl", "yl", "xh", "xl")
FAR = ("zh", "zl", "xh")
NEAR = ("yl", "xl")
N_CTX = 64
N_TP = 8
N_FAR = 16
N_NEAR = 4
N_ASK = 8
ROWS = 64
HEADS = 2
FEATS = HEADS * HD
TOTAL = N_CTX * ROWS
WINDOW = 2 * ROWS
HALF = ROWS // 2
TILE_Q = N_ASK * ROWS
TILE_K = N_FAR * ROWS
SCALE = HD ** (-0.5)
LOG2E = 1.4426950408889634
NEG = -1e30
FLOOR = -1e29
BF = jnp.bfloat16
F32 = jnp.float32
I32 = jnp.int32


def dot(a, b, dims):
    return lax.dot_general(a, b, (dims, ((), ())), preferred_element_type=F32)


def shift(x, axis, n, by):
    return lax.ppermute(x, axis, [(i, (i + by) % n) for i in range(n)])


def swap(x, axis):
    return lax.all_to_all(x, axis, split_axis=0, concat_axis=0, tiled=True)


def iota(shape, dim):
    return lax.broadcasted_iota(I32, shape, dim)


def call(kernel, ins, outs, flops, scalars=0):
    smem = pl.BlockSpec(memory_space=pltpu.SMEM)
    vmem = pl.BlockSpec(memory_space=pltpu.VMEM)
    size = sum(x.size * x.dtype.itemsize for x in list(ins) + list(outs))
    return pl.pallas_call(
        kernel,
        out_shape=tuple(outs),
        in_specs=[smem] * scalars + [vmem] * (len(ins) - scalars),
        out_specs=tuple([vmem] * len(outs)),
        cost_estimate=pl.CostEstimate(flops=flops, bytes_accessed=size, transcendentals=0),
        compiler_params=pltpu.CompilerParams(vmem_limit_bytes=40 * 1024 * 1024),
    )(*ins)


def shaped(shape, dtype):
    return jax.ShapeDtypeStruct(shape, dtype)


def slot_order(c, first_ref, moved_ref, shape, dim):
    before, after = jnp.maximum(c - 1, 0), jnp.minimum(c + 1, N_CTX - 1)
    first = first_ref[c]
    low = moved_ref[0, c]
    prev_high = jnp.where(c > 0, moved_ref[1, before], 0)
    next_low = jnp.where(c < N_CTX - 1, moved_ref[0, after], 0)
    next_first = jnp.where(c < N_CTX - 1, first_ref[after], TOTAL)
    rank = iota(shape, dim)
    order = jnp.where(
        rank < prev_high,
        first - prev_high + rank,
        jnp.where(
            rank >= ROWS - next_low,
            next_first + rank - (ROWS - next_low),
            first + low + rank - prev_high,
        ),
    )
    return order - (ROWS * c - HALF)


def pool_kernel(
    c_ref, first_hbm, moved_hbm, place_hbm, bytes_hbm, grad_hbm, w_hbm, sent_ref, own_ref,
    first_ref, moved_ref, place_ref, bytes_ref, grad_ref, w_ref, sems,
):
    pairs = [
        (first_hbm, first_ref),
        (moved_hbm, moved_ref),
        (place_hbm, place_ref),
        (bytes_hbm, bytes_ref),
        (grad_hbm, grad_ref),
    ] + [(w_hbm.at[i], w_ref.at[i]) for i in range(3)]
    copies = [pltpu.make_async_copy(a, b, sems.at[i]) for i, (a, b) in enumerate(pairs)]
    for copy in copies:
        copy.start()
    for copy in copies[:5]:
        copy.wait()
    c = c_ref[0]
    offset = first_ref[c] - (ROWS * c - HALF)
    member = iota((WINDOW, bytes_ref.shape[0]), 0) == place_ref[...] + offset
    lengths = jnp.sum(member.astype(F32), axis=1, keepdims=True)
    pooled = dot(member.astype(F32).astype(BF), bytes_ref[...], ((1,), (0,)))
    pooled = (pooled / jnp.maximum(lengths, 1.0)).astype(BF)
    order = slot_order(c, first_ref, moved_ref, (WINDOW, ROWS), 1)
    slotted = (iota((WINDOW, ROWS), 0) == order).astype(F32).astype(BF)
    grads = dot(slotted, grad_ref[...], ((1,), (0,))).astype(BF)
    for at, value in ((0, None), (1, grads), (2, None), (3, None)):
        if value is None:
            part = max(at - 1, 0)
            copies[5 + part].wait()
            value = dot(pooled, w_ref[part], ((1,), (0,))).astype(BF)
        sent_ref[:, at * FEATS : (at + 1) * FEATS] = value[:ROWS]
        own_ref[:, at * FEATS : (at + 1) * FEATS] = value[ROWS:]


def columns(value, kind, head):
    at = kind * FEATS + head * HD
    return value[:, at : at + HD]


def hold_kernel(own_ref, held_ref):
    held_ref[...] = own_ref[...]


def spread_kernel(own_ref, got_ref, asked_ref, held_ref):
    both = own_ref[...] + got_ref[...]
    held = []
    for e in range(HEADS):
        q, g, k, v = (columns(both, kind, e) for kind in range(4))
        asked_ref[e] = jnp.concatenate([q, g], axis=1)
        held.append(jnp.concatenate([k, v], axis=1))
    for i in range(N_FAR):
        held_ref[i] = held[(i >> 1) & 1]


def near_index(c):
    return ((c >> 2) & 1) * 2 + (c & 1)


def quarter(at):
    return pl.ds(pl.multiple_of(at * (TILE_Q // N_NEAR), TILE_Q // N_NEAR), TILE_Q // N_NEAR)


def unpack(asked_ref, held_ref):
    k = held_ref[:, :, :HD].reshape(TILE_K, HD)
    v = held_ref[:, :, HD:].reshape(TILE_K, HD)
    return asked_ref[:, :HD], asked_ref[:, HD:], k, v


def scores(c, q, k):
    row = iota((1, TILE_Q), 1)
    block = ((row >> 6) & 1) * 8 + ((row >> 7) & 1) + (row >> 8) * 4 + (c & 50)
    query = ROWS * block + (row & 63) + HALF
    col = iota((TILE_K, 1), 0)
    block = (col >> 8) * 16 + ((col >> 7) & 1) * 8 + ((col >> 6) & 1) * 2 + (c & 5)
    key = ROWS * block + (col & 63) + HALF
    allowed = (query & (TOTAL - 1)) >= (key & (TOTAL - 1))
    return jnp.where(allowed, dot(k, q, ((1,), (1,))) * (SCALE * LOG2E), NEG)


def forward_kernel(c_ref, mine_ref, one_ref, two_ref, three_ref, held_ref, stats_ref, asked_ref):
    me = near_index(c_ref[0])
    for k, ref in enumerate((mine_ref, one_ref, two_ref, three_ref)):
        asked_ref[quarter(me ^ k), :] = ref[...]
    q, g, k, v = unpack(asked_ref, held_ref)
    score = scores(c_ref[0], q, k)
    top = jnp.maximum(jnp.max(score, axis=0, keepdims=True), FLOOR)
    weight = jnp.exp2(score - top)
    dprob = dot(v, g, ((1,), (1,)))
    rows = [
        top,
        jnp.sum(weight, axis=0, keepdims=True),
        jnp.sum(weight * dprob, axis=0, keepdims=True),
    ]
    rows = jnp.concatenate(rows + [top] * 5, axis=0)
    for i in range(N_NEAR):
        stats_ref[i] = rows


def backward_kernel(c_ref, asked_ref, held_ref, stats_ref, term_ref, grad_ref):
    tops, sums, dots = (stats_ref[:, i, :] for i in range(3))
    peak = jnp.max(tops, axis=0, keepdims=True)
    each = jnp.exp2(tops - peak)
    norm = jnp.sum(each * sums, axis=0, keepdims=True)
    delta = jnp.sum(each * dots, axis=0, keepdims=True) / norm
    lse = peak + jnp.log(norm) * LOG2E
    q, g, k, v = unpack(asked_ref, held_ref)
    prob = jnp.exp2(scores(c_ref[0], q, k) - lse)
    dprob = dot(v, g, ((1,), (1,)))
    dscore = (prob * (dprob - delta)).astype(BF)
    prob = prob.astype(BF)
    d_key = (dot(dscore, q, ((1,), (0,))) * SCALE).astype(BF)
    d_value = dot(prob, g, ((1,), (0,))).astype(BF)
    term_ref[:, :, :HD] = d_key.reshape(N_FAR, ROWS, HD)
    term_ref[:, :, HD:] = d_value.reshape(N_FAR, ROWS, HD)
    grad_ref[:, :HD] = dot(dscore, k, ((0,), (0,))) * SCALE
    grad_ref[:, HD:] = dot(prob, v, ((0,), (0,)))


def part_kernel(c_ref, grad_ref, keep_ref, one_ref, two_ref, three_ref):
    me = near_index(c_ref[0])
    keep_ref[...] = grad_ref[quarter(me), :]
    for k, ref in ((1, one_ref), (2, two_ref), (3, three_ref)):
        ref[...] = grad_ref[quarter(me ^ k), :].astype(BF)


def join_kernel(c_ref, keep_ref, one_ref, two_ref, three_ref, rest_ref, give_ref):
    total = keep_ref[...]
    for ref in (one_ref, two_ref, three_ref):
        total = total + ref[...].astype(F32)
    second = ((c_ref[0] >> 3) & 1) == 1
    rest_ref[...] = jnp.where(second, total[ROWS:], total[:ROWS]).astype(BF)
    give_ref[...] = jnp.where(second, total[:ROWS], total[ROWS:]).astype(BF)


def sum_kernel(c_ref, term_ref, keep_ref, got_ref, w_ref, piece_ref, out_ref):
    second = ((c_ref[0] >> 3) & 1) == 1
    keep, got = keep_ref[...], got_ref[...]
    asked = [jnp.where(second, got, keep), jnp.where(second, keep, got)]
    d_query = jnp.concatenate([x[:, :HD] for x in asked], axis=1)
    out_ref[...] = jnp.concatenate([x[:, HD:] for x in asked], axis=1)
    held = []
    for e in range(HEADS):
        total = jnp.zeros((ROWS, 2 * HD), F32)
        for i in range(N_FAR):
            if (i >> 1) & 1 == e:
                total = total + term_ref[i].astype(F32)
        held.append(total.astype(BF))
    d_key = jnp.concatenate([x[:, :HD] for x in held], axis=1)
    d_value = jnp.concatenate([x[:, HD:] for x in held], axis=1)
    part = dot(d_query, w_ref[0], ((1,), (1,)))
    part = part + dot(d_key, w_ref[1], ((1,), (1,)))
    part = (part + dot(d_value, w_ref[2], ((1,), (1,)))).astype(BF)
    for i in range(N_TP):
        piece_ref[i] = part[:, i * HD : (i + 1) * HD]


def place_kernel(c_ref, first_ref, moved_ref, place_ref, picker_ref, member_ref, length_ref):
    c = c_ref[0]
    order = slot_order(c, first_ref, moved_ref, (ROWS, WINDOW), 0)
    picker_ref[...] = (iota((ROWS, WINDOW), 1) == order).astype(F32).astype(BF)
    offset = first_ref[c] - (ROWS * c - HALF)
    member = (iota((WINDOW, place_ref.shape[1]), 0) == place_ref[...] + offset).astype(F32)
    lengths = jnp.sum(member, axis=1, keepdims=True)
    member = member.T
    member_ref[...] = member.astype(BF)
    spread = jnp.broadcast_to(lengths, (WINDOW, HD)).astype(BF)
    length_ref[...] = dot(member.astype(BF), spread, ((1,), (0,)))


def head_sum_kernel(pieces_ref, out_ref, both_ref):
    both_ref[:, :HD] = jnp.sum(pieces_ref[...].astype(F32), axis=0).astype(BF)
    both_ref[:, HD:] = out_ref[...]


def last_kernel(before_ref, own_ref, picker_ref, member_ref, length_ref, out_ref, grad_ref):
    window = jnp.concatenate([before_ref[...], own_ref[...]], axis=0)
    out_ref[...] = dot(picker_ref[...], window[:, HD:], ((1,), (0,))).astype(BF)
    spread = dot(member_ref[...], window[:, :HD], ((1,), (0,)))
    grad_ref[...] = (spread / length_ref[...]).astype(BF)


def pool(c_ref, first, moved, place, byte_states, d_attn, w_qkv):
    hbm = pl.BlockSpec(memory_space=pltpu.HBM)
    vmem = pl.BlockSpec(memory_space=pltpu.VMEM)
    ins = (first, moved, place, byte_states, d_attn, w_qkv)
    spaces = (pltpu.SMEM, pltpu.SMEM) + (pltpu.VMEM,) * 4
    block = shaped((ROWS, 4 * FEATS), BF)
    return pl.pallas_call(
        pool_kernel,
        out_shape=(block, block),
        in_specs=[pl.BlockSpec(memory_space=pltpu.SMEM)] + [hbm] * len(ins),
        out_specs=(vmem, vmem),
        scratch_shapes=[space(x.shape, x.dtype) for space, x in zip(spaces, ins)]
        + [pltpu.SemaphoreType.DMA((len(ins) + 2,))],
        cost_estimate=pl.CostEstimate(flops=300_000_000, bytes_accessed=2_500_000, transcendentals=0),
        compiler_params=pltpu.CompilerParams(vmem_limit_bytes=60 * 1024 * 1024),
    )(c_ref, *ins)


def across(x, k):
    return lax.ppermute(x, NEAR, [(i, i ^ k) for i in range(N_NEAR)])


def shards(byte_states, patch_of_byte, patch_first, moved, w_qkv, d_attn):
    c_ref = lax.axis_index(CTX).astype(I32).reshape(1)
    n_bytes = patch_of_byte.shape[0]
    place = patch_of_byte.reshape(1, n_bytes)
    pair = shaped((ROWS, 2 * HD), BF)
    stack = shaped((N_FAR, ROWS, 2 * HD), BF)

    sent, own = pool(c_ref, patch_first, moved, place, byte_states, d_attn, w_qkv)
    (own,) = call(hold_kernel, (own,), (shaped(own.shape, BF),), 100_000)
    asked, held = call(
        spread_kernel,
        (own, shift(sent, CTX, N_CTX, -1)),
        (shaped((HEADS, ROWS, 2 * HD), BF), stack),
        1_000_000,
    )
    held = swap(held, FAR)
    second = lax.axis_index("zl") == 1
    keep = jnp.where(second, asked[1], asked[0])
    got = shift(jnp.where(second, asked[0], asked[1]), "zl", 2, 1)
    mine = jnp.concatenate([jnp.where(second, got, keep), jnp.where(second, keep, got)], axis=0)
    stats, asked = call(
        forward_kernel,
        (c_ref, mine, across(mine, 1), across(mine, 2), across(mine, 3), held),
        (shaped((N_NEAR, 8, TILE_Q), F32), shaped((TILE_Q, 2 * HD), BF)),
        300_000_000,
        1,
    )
    terms, grads = call(
        backward_kernel,
        (c_ref, asked, held, swap(stats, NEAR)),
        (stack, shaped((TILE_Q, 2 * HD), F32)),
        900_000_000,
        1,
    )
    terms = swap(terms, FAR)
    part = shaped((TILE_Q // N_NEAR, 2 * HD), BF)
    keep, one, two, three = call(
        part_kernel, (c_ref, grads), (shaped(part.shape, F32), part, part, part), 1_000_000, 1
    )
    keep, give = call(
        join_kernel,
        (c_ref, keep, across(one, 1), across(two, 2), across(three, 3)),
        (pair, pair),
        1_000_000,
        1,
    )
    pieces, out = call(
        sum_kernel,
        (c_ref, terms, keep, shift(give, "zl", 2, 1), w_qkv),
        (shaped((N_TP, ROWS, HD), BF), shaped((ROWS, FEATS), BF)),
        100_000_000,
        1,
    )
    (both,) = call(
        head_sum_kernel, (swap(pieces, "tp"), out), (shaped((ROWS, HD + FEATS), BF),), 100_000
    )
    picker, member, length = call(
        place_kernel,
        (c_ref, patch_first, moved, place),
        (
            shaped((ROWS, WINDOW), BF),
            shaped((n_bytes, WINDOW), BF),
            shaped((n_bytes, HD), F32),
        ),
        10_000_000,
        3,
    )
    attn_out, byte_grad = call(
        last_kernel,
        (shift(both, CTX, N_CTX, 1), both, picker, member, length),
        (shaped((ROWS, FEATS), BF), shaped((n_bytes, HD), BF)),
        10_000_000,
    )
    return attn_out, byte_grad


def solution(mesh):
    fine = Mesh(mesh.devices.reshape(SIZES), NAMES)
    placed = (P(CTX, None), P(CTX), P(), P(), P(None, None, "tp"), P(CTX, "tp"))
    return jax.shard_map(
        shards,
        mesh=fine,
        in_specs=placed,
        out_specs=(P(CTX, "tp"), P(CTX, "tp")),
        check_vma=False,
    )
```

```python
import functools

import jax
import jax.numpy as jnp
from jax import lax
from jax.experimental import pallas as pl
from jax.experimental.pallas import tpu as pltpu
from jax.sharding import Mesh, PartitionSpec as P

HD = 128
SIZES = (4, 2, 2, 2, 2, 8)
NAMES = ("zh", "zl", "yl", "xh", "xl", "tp")
CTX = ("zh", "zl", "yl", "xh", "xl")
FAR = ("zh", "zl", "xh")
NEAR = ("yl", "xl")
N_CTX = 64
N_TP = 8
N_FAR = 16
N_NEAR = 4
N_ASK = 8
ROWS = 64
HEADS = 2
FEATS = HEADS * HD
TOTAL = N_CTX * ROWS
WINDOW = 2 * ROWS
HALF = ROWS // 2
TILE_Q = N_ASK * ROWS
TILE_K = N_FAR * ROWS
SCALE = HD ** (-0.5)
LOG2E = 1.4426950408889634
NEG = -1e30
FLOOR = -1e29
HEAVY = 10_000_000_000
BF = jnp.bfloat16
F32 = jnp.float32
I32 = jnp.int32


def dot(a, b, dims):
    return lax.dot_general(a, b, (dims, ((), ())), preferred_element_type=F32)


def shift(x, axis, n, by):
    return lax.ppermute(x, axis, [(i, (i + by) % n) for i in range(n)])


def swap(x, axis):
    return lax.all_to_all(x, axis, split_axis=0, concat_axis=0, tiled=True)


def iota(shape, dim):
    return lax.broadcasted_iota(I32, shape, dim)


def call(kernel, ins, outs, flops, scalars=0, passed=False):
    smem = pl.BlockSpec(memory_space=pltpu.SMEM)
    vmem = pl.BlockSpec(memory_space=pltpu.VMEM)
    hbm = pl.BlockSpec(memory_space=pl.ANY)
    size = sum(x.size * x.dtype.itemsize for x in list(ins) + list(outs))
    return pl.pallas_call(
        kernel,
        out_shape=tuple(outs),
        in_specs=[smem] * scalars + [vmem] * (len(ins) - scalars - passed) + [hbm] * passed,
        out_specs=tuple([vmem] * (len(outs) - passed) + [hbm] * passed),
        input_output_aliases={len(ins) - 1: len(outs) - 1} if passed else {},
        cost_estimate=pl.CostEstimate(flops=flops, bytes_accessed=size, transcendentals=0),
        compiler_params=pltpu.CompilerParams(vmem_limit_bytes=40 * 1024 * 1024),
    )(*ins)


def shaped(shape, dtype):
    return jax.ShapeDtypeStruct(shape, dtype)


def slot_order(c, first_ref, moved_ref, shape, dim):
    before, after = jnp.maximum(c - 1, 0), jnp.minimum(c + 1, N_CTX - 1)
    first = first_ref[c]
    low = moved_ref[0, c]
    prev_high = jnp.where(c > 0, moved_ref[1, before], 0)
    next_low = jnp.where(c < N_CTX - 1, moved_ref[0, after], 0)
    next_first = jnp.where(c < N_CTX - 1, first_ref[after], TOTAL)
    rank = iota(shape, dim)
    order = jnp.where(
        rank < prev_high,
        first - prev_high + rank,
        jnp.where(
            rank >= ROWS - next_low,
            next_first + rank - (ROWS - next_low),
            first + low + rank - prev_high,
        ),
    )
    return order - (ROWS * c - HALF)


def pool_kernel(
    c_ref, first_hbm, moved_hbm, place_hbm, bytes_hbm, grad_hbm, w_hbm, sent_ref, own_ref, swap_ref, both_ref,
    first_ref, moved_ref, place_ref, bytes_ref, grad_ref, w_ref, sems,
):
    pairs = [
        (first_hbm, first_ref),
        (moved_hbm, moved_ref),
        (place_hbm, place_ref),
        (bytes_hbm, bytes_ref),
        (grad_hbm, grad_ref),
    ] + [(w_hbm.at[i], w_ref.at[i]) for i in range(3)]
    copies = [pltpu.make_async_copy(a, b, sems.at[i]) for i, (a, b) in enumerate(pairs)]
    for copy in copies:
        copy.start()
    for copy in copies[:5]:
        copy.wait()
    c = c_ref[0]
    offset = first_ref[c] - (ROWS * c - HALF)
    member = iota((WINDOW, bytes_ref.shape[0]), 0) == place_ref[...] + offset
    lengths = jnp.sum(member.astype(F32), axis=1, keepdims=True)
    pooled = dot(member.astype(F32).astype(BF), bytes_ref[...], ((1,), (0,)))
    pooled = (pooled / jnp.maximum(lengths, 1.0)).astype(BF)
    order = slot_order(c, first_ref, moved_ref, (WINDOW, ROWS), 1)
    slotted = (iota((WINDOW, ROWS), 0) == order).astype(F32).astype(BF)
    grads = dot(slotted, grad_ref[...], ((1,), (0,))).astype(BF)
    parts = []
    for i in range(3):
        copies[5 + i].wait()
        parts.append(dot(pooled, w_ref[i], ((1,), (0,))).astype(BF))
    query, key, value = parts

    def asked(rows, second):
        for ref, at in ((query, 0), (grads, HD)):
            one, two = ref[rows, :HD], ref[rows, HD:]
            yield slice(at, at + HD), jnp.where(second, two, one)

    before, after = slice(0, ROWS), slice(ROWS, WINDOW)
    mine = ((c >> 3) & 1) == 1
    left = (((c + N_CTX - 1) >> 3) & 1) == 1
    for ref, rows, second in (
        (sent_ref, before, left),
        (own_ref, after, mine),
        (swap_ref, after, jnp.logical_not(mine)),
        (both_ref, before, jnp.logical_not(left)),
    ):
        for at, part in asked(rows, second):
            ref[:, at] = part
    for ref, rows in ((sent_ref, before), (own_ref, after)):
        for e in range(HEADS):
            at = 2 * HD * (1 + e)
            ref[:, at : at + HD] = key[rows, e * HD : (e + 1) * HD]
            ref[:, at + HD : at + 2 * HD] = value[rows, e * HD : (e + 1) * HD]


def hold_kernel(own_ref, held_ref):
    held_ref[...] = own_ref[...]


def spread_kernel(c_ref, own_ref, got_ref, swap_ref, both_ref, asked_ref, held_ref):
    mine = own_ref[...] + got_ref[...]
    other = swap_ref[...] + both_ref[...]
    second = ((c_ref[0] >> 3) & 1) == 1
    here = mine[:, : 2 * HD]
    asked_ref[:ROWS] = jnp.where(second, other, here)
    asked_ref[ROWS:] = jnp.where(second, here, other)
    for i in range(N_FAR):
        at = 2 * HD * (1 + ((i >> 1) & 1))
        held_ref[i] = mine[:, at : at + 2 * HD]


def join_kernel(bit, c_ref, mine_ref, got_ref, out_ref):
    second = ((c_ref[0] >> bit) & 1) == 1
    n = mine_ref.shape[0]
    mine, got = mine_ref[...], got_ref[...]
    out_ref[:n] = jnp.where(second, got, mine)
    out_ref[n:] = jnp.where(second, mine, got)


def halve_kernel(bit, c_ref, keep_ref, got_ref, *refs):
    rest_ref, give_ref = refs[-3:-1] if len(refs) > 2 else refs
    second = ((c_ref[0] >> bit) & 1) == 1
    total = keep_ref[...] + got_ref[...].astype(F32)
    half = total.shape[0] // 2
    rest_ref[...] = jnp.where(second, total[half:], total[:half]).astype(rest_ref.dtype)
    give_ref[...] = jnp.where(second, total[:half], total[half:]).astype(BF)


def unpack(asked_ref, held_ref):
    k = held_ref[:, :, :HD].reshape(TILE_K, HD)
    v = held_ref[:, :, HD:].reshape(TILE_K, HD)
    return asked_ref[:, :HD], asked_ref[:, HD:], k, v


def scores(c, q, k):
    row = iota((1, TILE_Q), 1)
    block = ((row >> 6) & 1) * 8 + ((row >> 7) & 1) + ((row >> 8) & 1) * 4 + (c & 50)
    query = ROWS * block + (row & 63) + HALF
    col = iota((TILE_K, 1), 0)
    block = (col >> 8) * 16 + ((col >> 7) & 1) * 8 + ((col >> 6) & 1) * 2 + (c & 5)
    key = ROWS * block + (col & 63) + HALF
    allowed = (query & (TOTAL - 1)) >= (key & (TOTAL - 1))
    return jnp.where(allowed, dot(k, q, ((1,), (1,))) * (SCALE * LOG2E), NEG)


def forward_kernel(c_ref, asked_ref, held_ref, stats_ref):
    q, g, k, v = unpack(asked_ref, held_ref)
    score = scores(c_ref[0], q, k)
    top = jnp.maximum(jnp.max(score, axis=0, keepdims=True), FLOOR)
    weight = jnp.exp2(score - top)
    dprob = dot(v, g, ((1,), (1,)))
    rows = [
        top,
        jnp.sum(weight, axis=0, keepdims=True),
        jnp.sum(weight * dprob, axis=0, keepdims=True),
    ]
    rows = jnp.concatenate(rows + [top] * 5, axis=0)
    for i in range(N_NEAR):
        stats_ref[i] = rows


def backward_kernel(c_ref, asked_ref, held_ref, stats_ref, term_ref, keep_ref, give_ref):
    tops, sums, dots = (stats_ref[:, i, :] for i in range(3))
    peak = jnp.max(tops, axis=0, keepdims=True)
    each = jnp.exp2(tops - peak)
    norm = jnp.sum(each * sums, axis=0, keepdims=True)
    delta = jnp.sum(each * dots, axis=0, keepdims=True) / norm
    lse = peak + jnp.log(norm) * LOG2E
    q, g, k, v = unpack(asked_ref, held_ref)
    prob = jnp.exp2(scores(c_ref[0], q, k) - lse)
    dprob = dot(v, g, ((1,), (1,)))
    dscore = (prob * (dprob - delta)).astype(BF)
    prob = prob.astype(BF)
    d_key = (dot(dscore, q, ((1,), (0,))) * SCALE).astype(BF)
    d_value = dot(prob, g, ((1,), (0,))).astype(BF)
    term_ref[:, :, :HD] = d_key.reshape(N_FAR, ROWS, HD)
    term_ref[:, :, HD:] = d_value.reshape(N_FAR, ROWS, HD)
    d_query = dot(dscore, k, ((0,), (0,))) * SCALE
    out = dot(prob, v, ((0,), (0,)))
    second = ((c_ref[0] >> 2) & 1) == 1
    half = TILE_Q // 2
    for value, at in ((d_query, 0), (out, HD)):
        keep_ref[:, at : at + HD] = jnp.where(second, value[half:], value[:half])
        give_ref[:, at : at + HD] = jnp.where(second, value[:half], value[half:]).astype(BF)


def sum_kernel(c_ref, term_ref, keep_ref, got_ref, w_ref, piece_ref, out_ref):
    second = ((c_ref[0] >> 3) & 1) == 1
    keep, got = keep_ref[...], got_ref[...]
    asked = [jnp.where(second, got, keep), jnp.where(second, keep, got)]
    d_query = jnp.concatenate([x[:, :HD] for x in asked], axis=1)
    out_ref[...] = jnp.concatenate([x[:, HD:] for x in asked], axis=1)
    held = []
    for e in range(HEADS):
        total = jnp.zeros((ROWS, 2 * HD), F32)
        for i in range(N_FAR):
            if (i >> 1) & 1 == e:
                total = total + term_ref[i].astype(F32)
        held.append(total.astype(BF))
    d_key = jnp.concatenate([x[:, :HD] for x in held], axis=1)
    d_value = jnp.concatenate([x[:, HD:] for x in held], axis=1)
    part = dot(d_query, w_ref[0], ((1,), (1,)))
    part = part + dot(d_key, w_ref[1], ((1,), (1,)))
    part = (part + dot(d_value, w_ref[2], ((1,), (1,)))).astype(BF)
    for i in range(N_TP):
        piece_ref[i] = part[:, i * HD : (i + 1) * HD]


def place_kernel(c_ref, first_ref, moved_ref, place_ref, picker_ref, member_ref, length_ref):
    c = c_ref[0]
    order = slot_order(c, first_ref, moved_ref, (ROWS, WINDOW), 0)
    picker_ref[...] = (iota((ROWS, WINDOW), 1) == order).astype(F32).astype(BF)
    offset = first_ref[c] - (ROWS * c - HALF)
    member = (iota((WINDOW, place_ref.shape[1]), 0) == place_ref[...] + offset).astype(F32)
    lengths = jnp.sum(member, axis=1, keepdims=True)
    member = member.T
    member_ref[...] = member.astype(BF)
    spread = jnp.broadcast_to(lengths, (WINDOW, HD)).astype(BF)
    length_ref[...] = dot(member.astype(BF), spread, ((1,), (0,)))


def head_sum_kernel(pieces_ref, out_ref, both_ref):
    both_ref[:, :HD] = jnp.sum(pieces_ref[...].astype(F32), axis=0).astype(BF)
    both_ref[:, HD:] = out_ref[...]


def last_kernel(before_ref, own_ref, picker_ref, member_ref, length_ref, out_ref, grad_ref):
    window = jnp.concatenate([before_ref[...], own_ref[...]], axis=0)
    out_ref[...] = dot(picker_ref[...], window[:, HD:], ((1,), (0,))).astype(BF)
    spread = dot(member_ref[...], window[:, :HD], ((1,), (0,)))
    grad_ref[...] = (spread / length_ref[...]).astype(BF)


def pool(c_ref, first, moved, place, byte_states, d_attn, w_qkv):
    hbm = pl.BlockSpec(memory_space=pltpu.HBM)
    vmem = pl.BlockSpec(memory_space=pltpu.VMEM)
    ins = (first, moved, place, byte_states, d_attn, w_qkv)
    spaces = (pltpu.SMEM, pltpu.SMEM) + (pltpu.VMEM,) * 4
    block, pair = shaped((ROWS, 3 * FEATS), BF), shaped((ROWS, FEATS), BF)
    return pl.pallas_call(
        pool_kernel,
        out_shape=(block, block, pair, pair),
        in_specs=[pl.BlockSpec(memory_space=pltpu.SMEM)] + [hbm] * len(ins),
        out_specs=(vmem,) * 4,
        scratch_shapes=[space(x.shape, x.dtype) for space, x in zip(spaces, ins)]
        + [pltpu.SemaphoreType.DMA((len(ins) + 2,))],
        cost_estimate=pl.CostEstimate(flops=300_000_000, bytes_accessed=2_500_000, transcendentals=0),
        compiler_params=pltpu.CompilerParams(vmem_limit_bytes=60 * 1024 * 1024),
    )(c_ref, *ins)


def doubled(c_ref, mine, axis, bit, cost):
    out = shaped((2 * mine.shape[0], mine.shape[1]), BF)
    kernel = functools.partial(join_kernel, bit)
    return call(kernel, (c_ref, mine, shift(mine, axis, 2, 1)), (out,), cost, 1)[0]


def shards(byte_states, patch_of_byte, patch_first, moved, w_qkv, d_attn):
    c_ref = lax.axis_index(CTX).astype(I32).reshape(1)
    n_bytes = patch_of_byte.shape[0]
    place = patch_of_byte.reshape(1, n_bytes)
    pair = shaped((ROWS, 2 * HD), BF)
    stack = shaped((N_FAR, ROWS, 2 * HD), BF)

    sent, own, swapped, crossed = pool(
        c_ref, patch_first, moved, place, byte_states, d_attn, w_qkv
    )
    ring = [(i, (i - 1) % N_CTX) for i in range(N_CTX)]
    sent = lax.ppermute(sent, CTX, ring)
    swapped = lax.ppermute(swapped, CTX, [(i, i ^ 8) for i in range(N_CTX)])
    crossed = lax.ppermute(crossed, CTX, [(i, j ^ 8) for i, j in ring])
    (own,) = call(hold_kernel, (own,), (shaped(own.shape, BF),), 100_000)
    asked, held = call(
        spread_kernel,
        (c_ref, own, sent, swapped, crossed),
        (shaped((2 * ROWS, 2 * HD), BF), stack),
        1_000_000,
        1,
    )
    held = swap(held, FAR)
    asked = doubled(c_ref, doubled(c_ref, asked, "xl", 0, HEAVY), "yl", 2, 1_000_000)
    (stats,) = call(
        forward_kernel,
        (c_ref, asked, held),
        (shaped((N_NEAR, 8, TILE_Q), F32),),
        300_000_000,
        1,
    )
    half = (TILE_Q // 2, 2 * HD)
    terms, keep, give = call(
        backward_kernel,
        (c_ref, asked, held, swap(stats, NEAR)),
        (stack, shaped(half, F32), shaped(half, BF)),
        900_000_000,
        1,
    )
    quarter = (TILE_Q // 4, 2 * HD)
    keep, give, terms = call(
        functools.partial(halve_kernel, 0),
        (c_ref, keep, shift(give, "yl", 2, 1), terms),
        (shaped(quarter, F32), shaped(quarter, BF), stack),
        HEAVY,
        1,
        True,
    )
    terms = swap(terms, FAR)
    keep, give = call(
        functools.partial(halve_kernel, 3),
        (c_ref, keep, shift(give, "xl", 2, 1)),
        (pair, pair),
        HEAVY,
        1,
    )
    pieces, out = call(
        sum_kernel,
        (c_ref, terms, keep, shift(give, "zl", 2, 1), w_qkv),
        (shaped((N_TP, ROWS, HD), BF), shaped((ROWS, FEATS), BF)),
        100_000_000,
        1,
    )
    (both,) = call(
        head_sum_kernel, (swap(pieces, "tp"), out), (shaped((ROWS, HD + FEATS), BF),), 100_000
    )
    picker, member, length = call(
        place_kernel,
        (c_ref, patch_first, moved, place),
        (
            shaped((ROWS, WINDOW), BF),
            shaped((n_bytes, WINDOW), BF),
            shaped((n_bytes, HD), F32),
        ),
        10_000_000,
        3,
    )
    attn_out, byte_grad = call(
        last_kernel,
        (shift(both, CTX, N_CTX, 1), both, picker, member, length),
        (shaped((ROWS, FEATS), BF), shaped((n_bytes, HD), BF)),
        10_000_000,
    )
    return attn_out, byte_grad


def solution(mesh):
    fine = Mesh(mesh.devices.reshape(SIZES), NAMES)
    placed = (P(CTX, None), P(CTX), P(), P(), P(None, None, "tp"), P(CTX, "tp"))
    return jax.shard_map(
        shards,
        mesh=fine,
        in_specs=placed,
        out_specs=(P(CTX, "tp"), P(CTX, "tp")),
        check_vma=False,
    )
```

```python
import functools

import jax
import jax.numpy as jnp
from jax import lax
from jax.experimental import pallas as pl
from jax.experimental.pallas import tpu as pltpu
from jax.sharding import Mesh, PartitionSpec as P

HD = 128
SIZES = (4, 2, 2, 2, 2, 8)
NAMES = ("zh", "zl", "yl", "xh", "xl", "tp")
CTX = ("zh", "zl", "yl", "xh", "xl")
BITS = {"zl": 3, "yl": 2, "xh": 1, "xl": 0}
SPLIT, TWICE, AGAIN = "zl", "xl", "yl"
NEAR = tuple(a for a in BITS if a in (TWICE, AGAIN))
REST = tuple(a for a in BITS if a not in NEAR)
FAR = ("zh",) + REST
N_CTX = 64
N_TP = 8
N_FAR = 16
N_NEAR = 4
N_ASK = 8
ROWS = 64
HEADS = 2
FEATS = HEADS * HD
TOTAL = N_CTX * ROWS
WINDOW = 2 * ROWS
HALF = ROWS // 2
TILE_Q = N_ASK * ROWS
TILE_K = N_FAR * ROWS
SCALE = HD ** (-0.5)
LOG2E = 1.4426950408889634
NEG = -1e30
FLOOR = -1e29
JOIN = 3_000_000_000
HALVE = 5_000_000_000
BF = jnp.bfloat16
F32 = jnp.float32
I32 = jnp.int32


def dot(a, b, dims):
    return lax.dot_general(a, b, (dims, ((), ())), preferred_element_type=F32)


def shift(x, axis, n, by):
    return lax.ppermute(x, axis, [(i, (i + by) % n) for i in range(n)])


def swap(x, axis):
    return lax.all_to_all(x, axis, split_axis=0, concat_axis=0, tiled=True)


def iota(shape, dim):
    return lax.broadcasted_iota(I32, shape, dim)


def call(kernel, ins, outs, flops, scalars=0, unread=0):
    smem = pl.BlockSpec(memory_space=pltpu.SMEM)
    vmem = pl.BlockSpec(memory_space=pltpu.VMEM)
    size = sum(x.size * x.dtype.itemsize for x in list(ins) + list(outs))
    return pl.pallas_call(
        kernel,
        out_shape=tuple(outs),
        in_specs=[smem] * scalars
        + [vmem] * (len(ins) - scalars - unread)
        + [pl.BlockSpec(memory_space=pl.ANY)] * unread,
        out_specs=tuple([vmem] * len(outs)),
        cost_estimate=pl.CostEstimate(flops=flops, bytes_accessed=size, transcendentals=0),
        compiler_params=pltpu.CompilerParams(vmem_limit_bytes=40 * 1024 * 1024),
    )(*ins)


def shaped(shape, dtype):
    return jax.ShapeDtypeStruct(shape, dtype)


def slot_order(c, first_ref, moved_ref, shape, dim):
    before, after = jnp.maximum(c - 1, 0), jnp.minimum(c + 1, N_CTX - 1)
    first = first_ref[c]
    low = moved_ref[0, c]
    prev_high = jnp.where(c > 0, moved_ref[1, before], 0)
    next_low = jnp.where(c < N_CTX - 1, moved_ref[0, after], 0)
    next_first = jnp.where(c < N_CTX - 1, first_ref[after], TOTAL)
    rank = iota(shape, dim)
    order = jnp.where(
        rank < prev_high,
        first - prev_high + rank,
        jnp.where(
            rank >= ROWS - next_low,
            next_first + rank - (ROWS - next_low),
            first + low + rank - prev_high,
        ),
    )
    return order - (ROWS * c - HALF)


def pool_kernel(
    c_ref, first_hbm, moved_hbm, place_hbm, bytes_hbm, grad_hbm, w_hbm, sent_ref, own_ref,
    first_ref, moved_ref, place_ref, bytes_ref, grad_ref, w_ref, sems,
):
    pairs = [
        (first_hbm, first_ref),
        (moved_hbm, moved_ref),
        (place_hbm, place_ref),
        (bytes_hbm, bytes_ref),
        (grad_hbm, grad_ref),
    ] + [(w_hbm.at[i], w_ref.at[i]) for i in range(3)]
    copies = [pltpu.make_async_copy(a, b, sems.at[i]) for i, (a, b) in enumerate(pairs)]
    for copy in copies:
        copy.start()
    for copy in copies[:5]:
        copy.wait()
    c = c_ref[0]
    offset = first_ref[c] - (ROWS * c - HALF)
    member = iota((WINDOW, bytes_ref.shape[0]), 0) == place_ref[...] + offset
    lengths = jnp.sum(member.astype(F32), axis=1, keepdims=True)
    pooled = dot(member.astype(F32).astype(BF), bytes_ref[...], ((1,), (0,)))
    pooled = (pooled / jnp.maximum(lengths, 1.0)).astype(BF)
    order = slot_order(c, first_ref, moved_ref, (WINDOW, ROWS), 1)
    slotted = (iota((WINDOW, ROWS), 0) == order).astype(F32).astype(BF)
    grads = dot(slotted, grad_ref[...], ((1,), (0,))).astype(BF)
    for at, value in ((0, None), (1, grads), (2, None), (3, None)):
        if value is None:
            part = max(at - 1, 0)
            copies[5 + part].wait()
            value = dot(pooled, w_ref[part], ((1,), (0,))).astype(BF)
        sent_ref[:, at * FEATS : (at + 1) * FEATS] = value[:ROWS]
        own_ref[:, at * FEATS : (at + 1) * FEATS] = value[ROWS:]


def columns(value, kind, head):
    at = kind * FEATS + head * HD
    return value[:, at : at + HD]


def hold_kernel(own_ref, held_ref):
    held_ref[...] = own_ref[...]


def bit(c, axis):
    return (c >> BITS[axis]) & 1


def spread_kernel(c_ref, own_ref, got_ref, keep_ref, give_ref, held_ref):
    both = own_ref[...] + got_ref[...]
    asked, held = [], []
    for e in range(HEADS):
        q, g, k, v = (columns(both, kind, e) for kind in range(4))
        asked.append(jnp.concatenate([q, g], axis=1))
        held.append(jnp.concatenate([k, v], axis=1))
    second = bit(c_ref[0], SPLIT) == 1
    keep_ref[...] = jnp.where(second, asked[1], asked[0])
    give_ref[...] = jnp.where(second, asked[0], asked[1])
    for i in range(N_FAR):
        held_ref[i] = held[head_of(i)]


def head_of(i):
    return (i >> (1 - REST.index(SPLIT))) & 1


def join_kernel(axis, c_ref, mine_ref, got_ref, out_ref):
    second = bit(c_ref[0], axis) == 1
    n = mine_ref.shape[0]
    mine, got = mine_ref[...], got_ref[...]
    out_ref[:n] = jnp.where(second, got, mine)
    out_ref[n:] = jnp.where(second, mine, got)


def halve_kernel(axis, c_ref, keep_ref, got_ref, rest_ref, give_ref):
    second = bit(c_ref[0], axis) == 1
    total = keep_ref[...] + got_ref[...].astype(F32)
    half = total.shape[0] // 2
    rest_ref[...] = jnp.where(second, total[half:], total[:half]).astype(rest_ref.dtype)
    give_ref[...] = jnp.where(second, total[:half], total[half:]).astype(BF)


def unpack(asked_ref, held_ref):
    k = held_ref[:, :, :HD].reshape(TILE_K, HD)
    v = held_ref[:, :, HD:].reshape(TILE_K, HD)
    return asked_ref[:, :HD], asked_ref[:, HD:], k, v


def moved_bits(index, axes, c):
    block = sum(((index >> i) & 1) << BITS[axis] for i, axis in enumerate(axes))
    fixed = sum(1 << BITS[axis] for axis in BITS if axis not in axes)
    return block + (c & fixed)


def scores(c, q, k):
    row = iota((1, TILE_Q), 1)
    block = moved_bits(row >> 6, (SPLIT, TWICE, AGAIN), c) + (c & 48)
    query = ROWS * block + (row & 63) + HALF
    col = iota((TILE_K, 1), 0)
    block = moved_bits(col >> 6, REST[::-1], c) + (col >> 8) * 16
    key = ROWS * block + (col & 63) + HALF
    allowed = (query & (TOTAL - 1)) >= (key & (TOTAL - 1))
    return jnp.where(allowed, dot(k, q, ((1,), (1,))) * (SCALE * LOG2E), NEG)


def forward_kernel(c_ref, asked_ref, held_ref, stats_ref):
    q, g, k, v = unpack(asked_ref, held_ref)
    score = scores(c_ref[0], q, k)
    top = jnp.maximum(jnp.max(score, axis=0, keepdims=True), FLOOR)
    weight = jnp.exp2(score - top)
    dprob = dot(v, g, ((1,), (1,)))
    rows = [
        top,
        jnp.sum(weight, axis=0, keepdims=True),
        jnp.sum(weight * dprob, axis=0, keepdims=True),
    ]
    rows = jnp.concatenate(rows + [top] * 5, axis=0)
    for i in range(N_NEAR):
        stats_ref[i] = rows


def backward_kernel(c_ref, asked_ref, held_ref, stats_ref, term_ref, keep_ref, give_ref):
    tops, sums, dots = (stats_ref[:, i, :] for i in range(3))
    peak = jnp.max(tops, axis=0, keepdims=True)
    each = jnp.exp2(tops - peak)
    norm = jnp.sum(each * sums, axis=0, keepdims=True)
    delta = jnp.sum(each * dots, axis=0, keepdims=True) / norm
    lse = peak + jnp.log(norm) * LOG2E
    q, g, k, v = unpack(asked_ref, held_ref)
    prob = jnp.exp2(scores(c_ref[0], q, k) - lse)
    dprob = dot(v, g, ((1,), (1,)))
    dscore = (prob * (dprob - delta)).astype(BF)
    prob = prob.astype(BF)
    d_key = (dot(dscore, q, ((1,), (0,))) * SCALE).astype(BF)
    d_value = dot(prob, g, ((1,), (0,))).astype(BF)
    term_ref[:, :, :HD] = d_key.reshape(N_FAR, ROWS, HD)
    term_ref[:, :, HD:] = d_value.reshape(N_FAR, ROWS, HD)
    d_query = dot(dscore, k, ((0,), (0,))) * SCALE
    out = dot(prob, v, ((0,), (0,)))
    second = bit(c_ref[0], AGAIN) == 1
    half = TILE_Q // 2
    for value, at in ((d_query, 0), (out, HD)):
        keep_ref[:, at : at + HD] = jnp.where(second, value[half:], value[:half])
        give_ref[:, at : at + HD] = jnp.where(second, value[:half], value[half:]).astype(BF)


def sum_kernel(c_ref, term_ref, keep_ref, got_ref, w_ref, tables_any, piece_ref, out_ref):
    second = bit(c_ref[0], SPLIT) == 1
    keep, got = keep_ref[...], got_ref[...]
    asked = [jnp.where(second, got, keep), jnp.where(second, keep, got)]
    d_query = jnp.concatenate([x[:, :HD] for x in asked], axis=1)
    out_ref[...] = jnp.concatenate([x[:, HD:] for x in asked], axis=1)
    held = []
    for e in range(HEADS):
        total = jnp.zeros((ROWS, 2 * HD), F32)
        for i in range(N_FAR):
            if head_of(i) == e:
                total = total + term_ref[i].astype(F32)
        held.append(total.astype(BF))
    d_key = jnp.concatenate([x[:, :HD] for x in held], axis=1)
    d_value = jnp.concatenate([x[:, HD:] for x in held], axis=1)
    part = dot(d_query, w_ref[0], ((1,), (1,)))
    part = part + dot(d_key, w_ref[1], ((1,), (1,)))
    part = (part + dot(d_value, w_ref[2], ((1,), (1,)))).astype(BF)
    for i in range(N_TP):
        piece_ref[i] = part[:, i * HD : (i + 1) * HD]


def place_kernel(c_ref, first_ref, moved_ref, place_ref, picker_ref, member_ref, length_ref):
    c = c_ref[0]
    order = slot_order(c, first_ref, moved_ref, (ROWS, WINDOW), 0)
    picker_ref[...] = (iota((ROWS, WINDOW), 1) == order).astype(F32).astype(BF)
    offset = first_ref[c] - (ROWS * c - HALF)
    member = (iota((WINDOW, place_ref.shape[1]), 0) == place_ref[...] + offset).astype(F32)
    lengths = jnp.sum(member, axis=1, keepdims=True)
    member = member.T
    member_ref[...] = member.astype(BF)
    spread = jnp.broadcast_to(lengths, (WINDOW, HD)).astype(BF)
    length_ref[...] = dot(member.astype(BF), spread, ((1,), (0,)))


def head_sum_kernel(pieces_ref, out_ref, both_ref):
    both_ref[:, :HD] = jnp.sum(pieces_ref[...].astype(F32), axis=0).astype(BF)
    both_ref[:, HD:] = out_ref[...]


def last_kernel(before_ref, own_ref, picker_ref, member_ref, length_ref, out_ref, grad_ref):
    window = jnp.concatenate([before_ref[...], own_ref[...]], axis=0)
    out_ref[...] = dot(picker_ref[...], window[:, HD:], ((1,), (0,))).astype(BF)
    spread = dot(member_ref[...], window[:, :HD], ((1,), (0,)))
    grad_ref[...] = (spread / length_ref[...]).astype(BF)


def pool(c_ref, first, moved, place, byte_states, d_attn, w_qkv):
    hbm = pl.BlockSpec(memory_space=pltpu.HBM)
    vmem = pl.BlockSpec(memory_space=pltpu.VMEM)
    ins = (first, moved, place, byte_states, d_attn, w_qkv)
    spaces = (pltpu.SMEM, pltpu.SMEM) + (pltpu.VMEM,) * 4
    block = shaped((ROWS, 4 * FEATS), BF)
    return pl.pallas_call(
        pool_kernel,
        out_shape=(block, block),
        in_specs=[pl.BlockSpec(memory_space=pltpu.SMEM)] + [hbm] * len(ins),
        out_specs=(vmem, vmem),
        scratch_shapes=[space(x.shape, x.dtype) for space, x in zip(spaces, ins)]
        + [pltpu.SemaphoreType.DMA((len(ins) + 2,))],
        cost_estimate=pl.CostEstimate(flops=300_000_000, bytes_accessed=2_500_000, transcendentals=0),
        compiler_params=pltpu.CompilerParams(vmem_limit_bytes=60 * 1024 * 1024),
    )(c_ref, *ins)


def pair(rows, dtype=BF):
    return shaped((rows, 2 * HD), dtype)


def joined(c_ref, mine, got, axis):
    kernel = functools.partial(join_kernel, axis)
    return call(kernel, (c_ref, mine, got), (pair(2 * mine.shape[0]),), JOIN, 1)[0]


def halved(c_ref, keep, got, axis, dtype):
    half = keep.shape[0] // 2
    kernel = functools.partial(halve_kernel, axis)
    return call(kernel, (c_ref, keep, got), (pair(half, dtype), pair(half)), HALVE, 1)


def shards(byte_states, patch_of_byte, patch_first, moved, w_qkv, d_attn):
    c_ref = lax.axis_index(CTX).astype(I32).reshape(1)
    n_bytes = patch_of_byte.shape[0]
    place = patch_of_byte.reshape(1, n_bytes)
    stack = shaped((N_FAR, ROWS, 2 * HD), BF)

    sent, own = pool(c_ref, patch_first, moved, place, byte_states, d_attn, w_qkv)
    (own,) = call(hold_kernel, (own,), (shaped(own.shape, BF),), 100_000)
    keep, give, held = call(
        spread_kernel,
        (c_ref, own, shift(sent, CTX, N_CTX, -1)),
        (pair(ROWS), pair(ROWS), stack),
        1_000_000,
        1,
    )
    held = swap(held, FAR)
    asked = joined(c_ref, keep, shift(give, SPLIT, 2, 1), SPLIT)
    for axis in (TWICE, AGAIN):
        asked = joined(c_ref, asked, shift(asked, axis, 2, 1), axis)
    (stats,) = call(
        forward_kernel,
        (c_ref, asked, held),
        (shaped((N_NEAR, 8, TILE_Q), F32),),
        300_000_000,
        1,
    )
    terms, keep, give = call(
        backward_kernel,
        (c_ref, asked, held, swap(stats, NEAR)),
        (stack, pair(TILE_Q // 2, F32), pair(TILE_Q // 2)),
        900_000_000,
        1,
    )
    terms = swap(terms, FAR)
    keep, give = halved(c_ref, keep, shift(give, AGAIN, 2, 1), TWICE, F32)
    keep, give = halved(c_ref, keep, shift(give, TWICE, 2, 1), SPLIT, BF)
    picker, member, length = call(
        place_kernel,
        (c_ref, patch_first, moved, place),
        (
            shaped((ROWS, WINDOW), BF),
            shaped((n_bytes, WINDOW), BF),
            shaped((n_bytes, HD), F32),
        ),
        10_000_000,
        3,
    )
    pieces, out = call(
        sum_kernel,
        (c_ref, terms, keep, shift(give, SPLIT, 2, 1), w_qkv, picker),
        (shaped((N_TP, ROWS, HD), BF), shaped((ROWS, FEATS), BF)),
        100_000_000,
        1,
        1,
    )
    (both,) = call(
        head_sum_kernel, (swap(pieces, "tp"), out), (shaped((ROWS, HD + FEATS), BF),), 100_000
    )
    attn_out, byte_grad = call(
        last_kernel,
        (shift(both, CTX, N_CTX, 1), both, picker, member, length),
        (shaped((ROWS, FEATS), BF), shaped((n_bytes, HD), BF)),
        10_000_000,
    )
    return attn_out, byte_grad


def solution(mesh):
    fine = Mesh(mesh.devices.reshape(SIZES), NAMES)
    placed = (P(CTX, None), P(CTX), P(), P(), P(None, None, "tp"), P(CTX, "tp"))
    return jax.shard_map(
        shards,
        mesh=fine,
        in_specs=placed,
        out_specs=(P(CTX, "tp"), P(CTX, "tp")),
        check_vma=False,
    )
```

```python
import functools

import jax
import jax.numpy as jnp
from jax import lax
from jax.experimental import pallas as pl
from jax.experimental.pallas import tpu as pltpu
from jax.sharding import Mesh, PartitionSpec as P

HD = 128
SIZES = (4, 2, 2, 2, 2, 8)
NAMES = ("zh", "zl", "yl", "xh", "xl", "tp")
CTX = ("zh", "zl", "yl", "xh", "xl")
BITS = {"zl": 3, "yl": 2, "xh": 1, "xl": 0}
SPLIT, TWICE, AGAIN = "xl", "yl", "zl"
NEAR = tuple(a for a in BITS if a in (TWICE, AGAIN))
REST = tuple(a for a in BITS if a not in NEAR)
FAR = ("zh",) + REST
N_CTX = 64
N_TP = 8
N_FAR = 16
N_NEAR = 4
N_ASK = 8
ROWS = 64
HEADS = 2
FEATS = HEADS * HD
TOTAL = N_CTX * ROWS
WINDOW = 2 * ROWS
HALF = ROWS // 2
TILE_Q = N_ASK * ROWS
TILE_K = N_FAR * ROWS
SCALE = HD ** (-0.5)
LOG2E = 1.4426950408889634
NEG = -1e30
FLOOR = -1e29
JOIN = 3_000_000_000
HALVE = 5_000_000_000
BF = jnp.bfloat16
F32 = jnp.float32
I32 = jnp.int32


def dot(a, b, dims):
    return lax.dot_general(a, b, (dims, ((), ())), preferred_element_type=F32)


def shift(x, axis, n, by):
    return lax.ppermute(x, axis, [(i, (i + by) % n) for i in range(n)])


def swap(x, axis):
    return lax.all_to_all(x, axis, split_axis=0, concat_axis=0, tiled=True)


def iota(shape, dim):
    return lax.broadcasted_iota(I32, shape, dim)


def call(kernel, ins, outs, flops, scalars=0, unread=0):
    smem = pl.BlockSpec(memory_space=pltpu.SMEM)
    vmem = pl.BlockSpec(memory_space=pltpu.VMEM)
    size = sum(x.size * x.dtype.itemsize for x in list(ins) + list(outs))
    return pl.pallas_call(
        kernel,
        out_shape=tuple(outs),
        in_specs=[smem] * scalars
        + [vmem] * (len(ins) - scalars - unread)
        + [pl.BlockSpec(memory_space=pl.ANY)] * unread,
        out_specs=tuple([vmem] * len(outs)),
        cost_estimate=pl.CostEstimate(flops=flops, bytes_accessed=size, transcendentals=0),
        compiler_params=pltpu.CompilerParams(vmem_limit_bytes=40 * 1024 * 1024),
    )(*ins)


def shaped(shape, dtype):
    return jax.ShapeDtypeStruct(shape, dtype)


def slot_order(c, first_ref, moved_ref, shape, dim):
    before, after = jnp.maximum(c - 1, 0), jnp.minimum(c + 1, N_CTX - 1)
    first = first_ref[c]
    low = moved_ref[0, c]
    prev_high = jnp.where(c > 0, moved_ref[1, before], 0)
    next_low = jnp.where(c < N_CTX - 1, moved_ref[0, after], 0)
    next_first = jnp.where(c < N_CTX - 1, first_ref[after], TOTAL)
    rank = iota(shape, dim)
    order = jnp.where(
        rank < prev_high,
        first - prev_high + rank,
        jnp.where(
            rank >= ROWS - next_low,
            next_first + rank - (ROWS - next_low),
            first + low + rank - prev_high,
        ),
    )
    return order - (ROWS * c - HALF)


def pool_kernel(
    c_ref, first_hbm, moved_hbm, place_hbm, bytes_hbm, grad_hbm, w_hbm, sent_ref, own_ref,
    first_ref, moved_ref, place_ref, bytes_ref, grad_ref, w_ref, sems,
):
    pairs = [
        (first_hbm, first_ref),
        (moved_hbm, moved_ref),
        (place_hbm, place_ref),
        (bytes_hbm, bytes_ref),
        (grad_hbm, grad_ref),
    ] + [(w_hbm.at[i], w_ref.at[i]) for i in range(3)]
    copies = [pltpu.make_async_copy(a, b, sems.at[i]) for i, (a, b) in enumerate(pairs)]
    for copy in copies:
        copy.start()
    for copy in copies[:5]:
        copy.wait()
    c = c_ref[0]
    offset = first_ref[c] - (ROWS * c - HALF)
    member = iota((WINDOW, bytes_ref.shape[0]), 0) == place_ref[...] + offset
    lengths = jnp.sum(member.astype(F32), axis=1, keepdims=True)
    pooled = dot(member.astype(F32).astype(BF), bytes_ref[...], ((1,), (0,)))
    pooled = (pooled / jnp.maximum(lengths, 1.0)).astype(BF)
    order = slot_order(c, first_ref, moved_ref, (WINDOW, ROWS), 1)
    slotted = (iota((WINDOW, ROWS), 0) == order).astype(F32).astype(BF)
    grads = dot(slotted, grad_ref[...], ((1,), (0,))).astype(BF)
    for at, value in ((0, None), (1, grads), (2, None), (3, None)):
        if value is None:
            part = max(at - 1, 0)
            copies[5 + part].wait()
            value = dot(pooled, w_ref[part], ((1,), (0,))).astype(BF)
        sent_ref[:, at * FEATS : (at + 1) * FEATS] = value[:ROWS]
        own_ref[:, at * FEATS : (at + 1) * FEATS] = value[ROWS:]


def columns(value, kind, head):
    at = kind * FEATS + head * HD
    return value[:, at : at + HD]


def hold_kernel(own_ref, held_ref):
    held_ref[...] = own_ref[...]


def bit(c, axis):
    return (c >> BITS[axis]) & 1


def spread_kernel(c_ref, own_ref, got_ref, keep_ref, give_ref, held_ref):
    both = own_ref[...] + got_ref[...]
    asked, held = [], []
    for e in range(HEADS):
        q, g, k, v = (columns(both, kind, e) for kind in range(4))
        asked.append(jnp.concatenate([q, g], axis=1))
        held.append(jnp.concatenate([k, v], axis=1))
    second = bit(c_ref[0], SPLIT) == 1
    keep_ref[...] = jnp.where(second, asked[1], asked[0])
    give_ref[...] = jnp.where(second, asked[0], asked[1])
    for i in range(N_FAR):
        held_ref[i] = held[head_of(i)]


def head_of(i):
    return (i >> (1 - REST.index(SPLIT))) & 1


def join_kernel(axis, c_ref, mine_ref, got_ref, out_ref):
    second = bit(c_ref[0], axis) == 1
    n = mine_ref.shape[0]
    mine, got = mine_ref[...], got_ref[...]
    out_ref[:n] = jnp.where(second, got, mine)
    out_ref[n:] = jnp.where(second, mine, got)


def halve_kernel(axis, c_ref, keep_ref, got_ref, rest_ref, give_ref):
    second = bit(c_ref[0], axis) == 1
    total = keep_ref[...] + got_ref[...].astype(F32)
    half = total.shape[0] // 2
    rest_ref[...] = jnp.where(second, total[half:], total[:half]).astype(rest_ref.dtype)
    give_ref[...] = jnp.where(second, total[:half], total[half:]).astype(BF)


def unpack(asked_ref, held_ref):
    k = held_ref[:, :, :HD].reshape(TILE_K, HD)
    v = held_ref[:, :, HD:].reshape(TILE_K, HD)
    return asked_ref[:, :HD], asked_ref[:, HD:], k, v


def moved_bits(index, axes, c):
    block = sum(((index >> i) & 1) << BITS[axis] for i, axis in enumerate(axes))
    fixed = sum(1 << BITS[axis] for axis in BITS if axis not in axes)
    return block + (c & fixed)


def scores(c, q, k):
    row = iota((1, TILE_Q), 1)
    block = moved_bits(row >> 6, (SPLIT, TWICE, AGAIN), c) + (c & 48)
    query = ROWS * block + (row & 63) + HALF
    col = iota((TILE_K, 1), 0)
    block = moved_bits(col >> 6, REST[::-1], c) + (col >> 8) * 16
    key = ROWS * block + (col & 63) + HALF
    allowed = (query & (TOTAL - 1)) >= (key & (TOTAL - 1))
    return jnp.where(allowed, dot(k, q, ((1,), (1,))) * (SCALE * LOG2E), NEG)


def forward_kernel(c_ref, asked_ref, held_ref, stats_ref):
    q, g, k, v = unpack(asked_ref, held_ref)
    score = scores(c_ref[0], q, k)
    top = jnp.maximum(jnp.max(score, axis=0, keepdims=True), FLOOR)
    weight = jnp.exp2(score - top)
    dprob = dot(v, g, ((1,), (1,)))
    rows = [
        top,
        jnp.sum(weight, axis=0, keepdims=True),
        jnp.sum(weight * dprob, axis=0, keepdims=True),
    ]
    rows = jnp.concatenate(rows + [top] * 5, axis=0)
    for i in range(N_NEAR):
        stats_ref[i] = rows


def backward_kernel(c_ref, asked_ref, held_ref, stats_ref, term_ref, keep_ref, give_ref):
    tops, sums, dots = (stats_ref[:, i, :] for i in range(3))
    peak = jnp.max(tops, axis=0, keepdims=True)
    each = jnp.exp2(tops - peak)
    norm = jnp.sum(each * sums, axis=0, keepdims=True)
    delta = jnp.sum(each * dots, axis=0, keepdims=True) / norm
    lse = peak + jnp.log(norm) * LOG2E
    q, g, k, v = unpack(asked_ref, held_ref)
    prob = jnp.exp2(scores(c_ref[0], q, k) - lse)
    dprob = dot(v, g, ((1,), (1,)))
    dscore = (prob * (dprob - delta)).astype(BF)
    prob = prob.astype(BF)
    d_key = (dot(dscore, q, ((1,), (0,))) * SCALE).astype(BF)
    d_value = dot(prob, g, ((1,), (0,))).astype(BF)
    term_ref[:, :, :HD] = d_key.reshape(N_FAR, ROWS, HD)
    term_ref[:, :, HD:] = d_value.reshape(N_FAR, ROWS, HD)
    d_query = dot(dscore, k, ((0,), (0,))) * SCALE
    out = dot(prob, v, ((0,), (0,)))
    second = bit(c_ref[0], AGAIN) == 1
    half = TILE_Q // 2
    for value, at in ((d_query, 0), (out, HD)):
        keep_ref[:, at : at + HD] = jnp.where(second, value[half:], value[:half])
        give_ref[:, at : at + HD] = jnp.where(second, value[:half], value[half:]).astype(BF)


def sum_kernel(c_ref, term_ref, keep_ref, got_ref, w_ref, tables_any, piece_ref, out_ref):
    second = bit(c_ref[0], SPLIT) == 1
    keep, got = keep_ref[...], got_ref[...]
    asked = [jnp.where(second, got, keep), jnp.where(second, keep, got)]
    d_query = jnp.concatenate([x[:, :HD] for x in asked], axis=1)
    out_ref[...] = jnp.concatenate([x[:, HD:] for x in asked], axis=1)
    held = []
    for e in range(HEADS):
        total = jnp.zeros((ROWS, 2 * HD), F32)
        for i in range(N_FAR):
            if head_of(i) == e:
                total = total + term_ref[i].astype(F32)
        held.append(total.astype(BF))
    d_key = jnp.concatenate([x[:, :HD] for x in held], axis=1)
    d_value = jnp.concatenate([x[:, HD:] for x in held], axis=1)
    part = dot(d_query, w_ref[0], ((1,), (1,)))
    part = part + dot(d_key, w_ref[1], ((1,), (1,)))
    part = (part + dot(d_value, w_ref[2], ((1,), (1,)))).astype(BF)
    for i in range(N_TP):
        piece_ref[i] = part[:, i * HD : (i + 1) * HD]


def place_kernel(c_ref, first_ref, moved_ref, place_ref, picker_ref, member_ref, length_ref):
    c = c_ref[0]
    order = slot_order(c, first_ref, moved_ref, (ROWS, WINDOW), 0)
    picker_ref[...] = (iota((ROWS, WINDOW), 1) == order).astype(F32).astype(BF)
    offset = first_ref[c] - (ROWS * c - HALF)
    member = (iota((WINDOW, place_ref.shape[1]), 0) == place_ref[...] + offset).astype(F32)
    lengths = jnp.sum(member, axis=1, keepdims=True)
    member = member.T
    member_ref[...] = member.astype(BF)
    spread = jnp.broadcast_to(lengths, (WINDOW, HD)).astype(BF)
    length_ref[...] = dot(member.astype(BF), spread, ((1,), (0,)))


def head_sum_kernel(pieces_ref, out_ref, both_ref):
    both_ref[:, :HD] = jnp.sum(pieces_ref[...].astype(F32), axis=0).astype(BF)
    both_ref[:, HD:] = out_ref[...]


def last_kernel(before_ref, own_ref, picker_ref, member_ref, length_ref, out_ref, grad_ref):
    window = jnp.concatenate([before_ref[...], own_ref[...]], axis=0)
    out_ref[...] = dot(picker_ref[...], window[:, HD:], ((1,), (0,))).astype(BF)
    spread = dot(member_ref[...], window[:, :HD], ((1,), (0,)))
    grad_ref[...] = (spread / length_ref[...]).astype(BF)


def pool(c_ref, first, moved, place, byte_states, d_attn, w_qkv):
    hbm = pl.BlockSpec(memory_space=pltpu.HBM)
    vmem = pl.BlockSpec(memory_space=pltpu.VMEM)
    ins = (first, moved, place, byte_states, d_attn, w_qkv)
    spaces = (pltpu.SMEM, pltpu.SMEM) + (pltpu.VMEM,) * 4
    block = shaped((ROWS, 4 * FEATS), BF)
    return pl.pallas_call(
        pool_kernel,
        out_shape=(block, block),
        in_specs=[pl.BlockSpec(memory_space=pltpu.SMEM)] + [hbm] * len(ins),
        out_specs=(vmem, vmem),
        scratch_shapes=[space(x.shape, x.dtype) for space, x in zip(spaces, ins)]
        + [pltpu.SemaphoreType.DMA((len(ins) + 2,))],
        cost_estimate=pl.CostEstimate(flops=300_000_000, bytes_accessed=2_500_000, transcendentals=0),
        compiler_params=pltpu.CompilerParams(vmem_limit_bytes=60 * 1024 * 1024),
    )(c_ref, *ins)


def pair(rows, dtype=BF):
    return shaped((rows, 2 * HD), dtype)


def joined(c_ref, mine, got, axis):
    kernel = functools.partial(join_kernel, axis)
    return call(kernel, (c_ref, mine, got), (pair(2 * mine.shape[0]),), JOIN, 1)[0]


def halved(c_ref, keep, got, axis, dtype):
    half = keep.shape[0] // 2
    kernel = functools.partial(halve_kernel, axis)
    return call(kernel, (c_ref, keep, got), (pair(half, dtype), pair(half)), HALVE, 1)


def shards(byte_states, patch_of_byte, patch_first, moved, w_qkv, d_attn):
    c_ref = lax.axis_index(CTX).astype(I32).reshape(1)
    n_bytes = patch_of_byte.shape[0]
    place = patch_of_byte.reshape(1, n_bytes)
    stack = shaped((N_FAR, ROWS, 2 * HD), BF)

    sent, own = pool(c_ref, patch_first, moved, place, byte_states, d_attn, w_qkv)
    (own,) = call(hold_kernel, (own,), (shaped(own.shape, BF),), 100_000)
    keep, give, held = call(
        spread_kernel,
        (c_ref, own, shift(sent, CTX, N_CTX, -1)),
        (pair(ROWS), pair(ROWS), stack),
        1_000_000,
        1,
    )
    held = swap(held, FAR)
    asked = joined(c_ref, keep, shift(give, SPLIT, 2, 1), SPLIT)
    for axis in (TWICE, AGAIN):
        asked = joined(c_ref, asked, shift(asked, axis, 2, 1), axis)
    (stats,) = call(
        forward_kernel,
        (c_ref, asked, held),
        (shaped((N_NEAR, 8, TILE_Q), F32),),
        300_000_000,
        1,
    )
    terms, keep, give = call(
        backward_kernel,
        (c_ref, asked, held, swap(stats, NEAR)),
        (stack, pair(TILE_Q // 2, F32), pair(TILE_Q // 2)),
        900_000_000,
        1,
    )
    terms = swap(terms, FAR)
    keep, give = halved(c_ref, keep, shift(give, AGAIN, 2, 1), TWICE, F32)
    keep, give = halved(c_ref, keep, shift(give, TWICE, 2, 1), SPLIT, BF)
    picker, member, length = call(
        place_kernel,
        (c_ref, patch_first, moved, place),
        (
            shaped((ROWS, WINDOW), BF),
            shaped((n_bytes, WINDOW), BF),
            shaped((n_bytes, HD), F32),
        ),
        10_000_000,
        3,
    )
    pieces, out = call(
        sum_kernel,
        (c_ref, terms, keep, shift(give, SPLIT, 2, 1), w_qkv, picker),
        (shaped((N_TP, ROWS, HD), BF), shaped((ROWS, FEATS), BF)),
        100_000_000,
        1,
        1,
    )
    (both,) = call(
        head_sum_kernel, (swap(pieces, "tp"), out), (shaped((ROWS, HD + FEATS), BF),), 100_000
    )
    attn_out, byte_grad = call(
        last_kernel,
        (shift(both, CTX, N_CTX, 1), both, picker, member, length),
        (shaped((ROWS, FEATS), BF), shaped((n_bytes, HD), BF)),
        10_000_000,
    )
    return attn_out, byte_grad


def solution(mesh):
    fine = Mesh(mesh.devices.reshape(SIZES), NAMES)
    placed = (P(CTX, None), P(CTX), P(), P(), P(None, None, "tp"), P(CTX, "tp"))
    return jax.shard_map(
        shards,
        mesh=fine,
        in_specs=placed,
        out_specs=(P(CTX, "tp"), P(CTX, "tp")),
        check_vma=False,
    )
```

```python
import functools

import jax
import jax.numpy as jnp
from jax import lax
from jax.experimental import pallas as pl
from jax.experimental.pallas import tpu as pltpu
from jax.sharding import Mesh, PartitionSpec as P

HD = 128
SIZES = (4, 2, 2, 2, 2, 8)
NAMES = ("zh", "zl", "yl", "xh", "xl", "tp")
CTX = ("zh", "zl", "yl", "xh", "xl")
BITS = {"zl": 3, "yl": 2, "xh": 1, "xl": 0}
SPLIT, TWICE, AGAIN = "xl", "yl", "zl"
NEAR = tuple(a for a in BITS if a in (TWICE, AGAIN))
REST = tuple(a for a in BITS if a not in NEAR)
FAR = ("zh",) + REST
N_CTX = 64
N_TP = 8
N_FAR = 16
N_NEAR = 4
N_ASK = 8
ROWS = 64
HEADS = 2
FEATS = HEADS * HD
TOTAL = N_CTX * ROWS
WINDOW = 2 * ROWS
HALF = ROWS // 2
TILE_Q = N_ASK * ROWS
TILE_K = N_FAR * ROWS
SCALE = HD ** (-0.5)
LOG2E = 1.4426950408889634
NEG = -1e30
FLOOR = -1e29
JOIN = 3_000_000_000
HALVE = 5_000_000_000
BF = jnp.bfloat16
F32 = jnp.float32
I32 = jnp.int32


def dot(a, b, dims):
    return lax.dot_general(a, b, (dims, ((), ())), preferred_element_type=F32)


def shift(x, axis, n, by):
    return lax.ppermute(x, axis, [(i, (i + by) % n) for i in range(n)])


def swap(x, axis):
    return lax.all_to_all(x, axis, split_axis=0, concat_axis=0, tiled=True)


def iota(shape, dim):
    return lax.broadcasted_iota(I32, shape, dim)


def call(kernel, ins, outs, flops, scalars=0, unread=0):
    smem = pl.BlockSpec(memory_space=pltpu.SMEM)
    vmem = pl.BlockSpec(memory_space=pltpu.VMEM)
    size = sum(x.size * x.dtype.itemsize for x in list(ins) + list(outs))
    return pl.pallas_call(
        kernel,
        out_shape=tuple(outs),
        in_specs=[smem] * scalars
        + [vmem] * (len(ins) - scalars - unread)
        + [pl.BlockSpec(memory_space=pl.ANY)] * unread,
        out_specs=tuple([vmem] * len(outs)),
        cost_estimate=pl.CostEstimate(flops=flops, bytes_accessed=size, transcendentals=0),
        compiler_params=pltpu.CompilerParams(vmem_limit_bytes=40 * 1024 * 1024),
    )(*ins)


def shaped(shape, dtype):
    return jax.ShapeDtypeStruct(shape, dtype)


def slot_order(c, first_ref, moved_ref, shape, dim):
    before, after = jnp.maximum(c - 1, 0), jnp.minimum(c + 1, N_CTX - 1)
    first = first_ref[c]
    low = moved_ref[0, c]
    prev_high = jnp.where(c > 0, moved_ref[1, before], 0)
    next_low = jnp.where(c < N_CTX - 1, moved_ref[0, after], 0)
    next_first = jnp.where(c < N_CTX - 1, first_ref[after], TOTAL)
    rank = iota(shape, dim)
    order = jnp.where(
        rank < prev_high,
        first - prev_high + rank,
        jnp.where(
            rank >= ROWS - next_low,
            next_first + rank - (ROWS - next_low),
            first + low + rank - prev_high,
        ),
    )
    return order - (ROWS * c - HALF)


def pool_kernel(
    c_ref, first_hbm, moved_hbm, place_hbm, bytes_hbm, grad_hbm, w_hbm, sent_ref, own_ref,
    first_ref, moved_ref, place_ref, bytes_ref, grad_ref, w_ref, sems,
):
    pairs = [
        (first_hbm, first_ref),
        (moved_hbm, moved_ref),
        (place_hbm, place_ref),
        (bytes_hbm, bytes_ref),
        (grad_hbm, grad_ref),
    ] + [(w_hbm.at[i], w_ref.at[i]) for i in range(3)]
    copies = [pltpu.make_async_copy(a, b, sems.at[i]) for i, (a, b) in enumerate(pairs)]
    for copy in copies:
        copy.start()
    for copy in copies[:5]:
        copy.wait()
    c = c_ref[0]
    offset = first_ref[c] - (ROWS * c - HALF)
    member = iota((WINDOW, bytes_ref.shape[0]), 0) == place_ref[...] + offset
    lengths = jnp.sum(member.astype(F32), axis=1, keepdims=True)
    pooled = dot(member.astype(F32).astype(BF), bytes_ref[...], ((1,), (0,)))
    pooled = (pooled / jnp.maximum(lengths, 1.0)).astype(BF)
    order = slot_order(c, first_ref, moved_ref, (WINDOW, ROWS), 1)
    slotted = (iota((WINDOW, ROWS), 0) == order).astype(F32).astype(BF)
    grads = dot(slotted, grad_ref[...], ((1,), (0,))).astype(BF)
    for at, value in ((0, None), (1, grads), (2, None), (3, None)):
        if value is None:
            part = max(at - 1, 0)
            copies[5 + part].wait()
            value = dot(pooled, w_ref[part], ((1,), (0,))).astype(BF)
        sent_ref[:, at * FEATS : (at + 1) * FEATS] = value[:ROWS]
        own_ref[:, at * FEATS : (at + 1) * FEATS] = value[ROWS:]


def columns(value, kind, head):
    at = kind * FEATS + head * HD
    return value[:, at : at + HD]


def hold_kernel(own_ref, held_ref):
    held_ref[...] = own_ref[...]


def bit(c, axis):
    return (c >> BITS[axis]) & 1


def spread_kernel(c_ref, own_ref, got_ref, keep_ref, give_ref, held_ref):
    both = own_ref[...] + got_ref[...]
    asked, held = [], []
    for e in range(HEADS):
        q, g, k, v = (columns(both, kind, e) for kind in range(4))
        asked.append(jnp.concatenate([q, g], axis=1))
        held.append(jnp.concatenate([k, v], axis=1))
    second = bit(c_ref[0], SPLIT) == 1
    keep_ref[...] = jnp.where(second, asked[1], asked[0])
    give_ref[...] = jnp.where(second, asked[0], asked[1])
    for i in range(N_FAR):
        held_ref[i] = held[head_of(i)]


def head_of(i):
    return (i >> (1 - REST.index(SPLIT))) & 1


def join_kernel(axis, c_ref, mine_ref, got_ref, out_ref):
    second = bit(c_ref[0], axis) == 1
    n = mine_ref.shape[0]
    mine, got = mine_ref[...], got_ref[...]
    out_ref[:n] = jnp.where(second, got, mine)
    out_ref[n:] = jnp.where(second, mine, got)


def halve_kernel(axis, c_ref, keep_ref, got_ref, rest_ref, give_ref):
    second = bit(c_ref[0], axis) == 1
    total = keep_ref[...] + got_ref[...].astype(F32)
    half = total.shape[0] // 2
    rest_ref[...] = jnp.where(second, total[half:], total[:half]).astype(rest_ref.dtype)
    give_ref[...] = jnp.where(second, total[:half], total[half:]).astype(BF)


def unpack(asked_ref, held_ref):
    k = held_ref[:, :, :HD].reshape(TILE_K, HD)
    v = held_ref[:, :, HD:].reshape(TILE_K, HD)
    return asked_ref[:, :HD], asked_ref[:, HD:], k, v


def moved_bits(index, axes, c):
    block = sum(((index >> i) & 1) << BITS[axis] for i, axis in enumerate(axes))
    fixed = sum(1 << BITS[axis] for axis in BITS if axis not in axes)
    return block + (c & fixed)


def scores(c, q, k):
    row = iota((1, TILE_Q), 1)
    block = moved_bits(row >> 6, (SPLIT, TWICE, AGAIN), c) + (c & 48)
    query = ROWS * block + (row & 63) + HALF
    col = iota((TILE_K, 1), 0)
    block = moved_bits(col >> 6, REST[::-1], c) + (col >> 8) * 16
    key = ROWS * block + (col & 63) + HALF
    allowed = (query & (TOTAL - 1)) >= (key & (TOTAL - 1))
    return jnp.where(allowed, dot(k, q, ((1,), (1,))) * (SCALE * LOG2E), NEG)


def forward_kernel(c_ref, asked_ref, held_ref, stats_ref, weight_ref, dprob_ref):
    q, g, k, v = unpack(asked_ref, held_ref)
    score = scores(c_ref[0], q, k)
    top = jnp.maximum(jnp.max(score, axis=0, keepdims=True), FLOOR)
    weight = jnp.exp2(score - top)
    dprob = dot(v, g, ((1,), (1,)))
    weight_ref[...] = weight
    dprob_ref[...] = dprob
    rows = [
        top,
        jnp.sum(weight, axis=0, keepdims=True),
        jnp.sum(weight * dprob, axis=0, keepdims=True),
    ]
    rows = jnp.concatenate(rows + [top] * 5, axis=0)
    for i in range(N_NEAR):
        stats_ref[i] = rows


def backward_kernel(
    c_ref, asked_ref, held_ref, own_ref, stats_ref, weight_ref, dprob_ref, term_ref, keep_ref, give_ref
):
    tops, sums, dots = (stats_ref[:, i, :] for i in range(3))
    peak = jnp.max(tops, axis=0, keepdims=True)
    each = jnp.exp2(tops - peak)
    norm = jnp.sum(each * sums, axis=0, keepdims=True)
    delta = jnp.sum(each * dots, axis=0, keepdims=True) / norm
    factor = jnp.exp2(own_ref[0, 0:1, :] - peak) / norm
    q, g, k, v = unpack(asked_ref, held_ref)
    prob = weight_ref[...] * factor
    dscore = (prob * (dprob_ref[...] - delta)).astype(BF)
    prob = prob.astype(BF)
    d_key = (dot(dscore, q, ((1,), (0,))) * SCALE).astype(BF)
    d_value = dot(prob, g, ((1,), (0,))).astype(BF)
    term_ref[:, :, :HD] = d_key.reshape(N_FAR, ROWS, HD)
    term_ref[:, :, HD:] = d_value.reshape(N_FAR, ROWS, HD)
    d_query = dot(dscore, k, ((0,), (0,))) * SCALE
    out = dot(prob, v, ((0,), (0,)))
    second = bit(c_ref[0], AGAIN) == 1
    half = TILE_Q // 2
    for value, at in ((d_query, 0), (out, HD)):
        keep_ref[:, at : at + HD] = jnp.where(second, value[half:], value[:half])
        give_ref[:, at : at + HD] = jnp.where(second, value[:half], value[half:]).astype(BF)


def sum_kernel(c_ref, term_ref, keep_ref, got_ref, w_ref, tables_any, piece_ref, out_ref):
    second = bit(c_ref[0], SPLIT) == 1
    keep, got = keep_ref[...], got_ref[...]
    asked = [jnp.where(second, got, keep), jnp.where(second, keep, got)]
    d_query = jnp.concatenate([x[:, :HD] for x in asked], axis=1)
    out_ref[...] = jnp.concatenate([x[:, HD:] for x in asked], axis=1)
    held = []
    for e in range(HEADS):
        total = jnp.zeros((ROWS, 2 * HD), F32)
        for i in range(N_FAR):
            if head_of(i) == e:
                total = total + term_ref[i].astype(F32)
        held.append(total.astype(BF))
    d_key = jnp.concatenate([x[:, :HD] for x in held], axis=1)
    d_value = jnp.concatenate([x[:, HD:] for x in held], axis=1)
    part = dot(d_query, w_ref[0], ((1,), (1,)))
    part = part + dot(d_key, w_ref[1], ((1,), (1,)))
    part = (part + dot(d_value, w_ref[2], ((1,), (1,)))).astype(BF)
    for i in range(N_TP):
        piece_ref[i] = part[:, i * HD : (i + 1) * HD]


def place_kernel(c_ref, first_ref, moved_ref, place_ref, picker_ref, member_ref, length_ref):
    c = c_ref[0]
    order = slot_order(c, first_ref, moved_ref, (ROWS, WINDOW), 0)
    picker_ref[...] = (iota((ROWS, WINDOW), 1) == order).astype(F32).astype(BF)
    offset = first_ref[c] - (ROWS * c - HALF)
    member = (iota((WINDOW, place_ref.shape[1]), 0) == place_ref[...] + offset).astype(F32)
    lengths = jnp.sum(member, axis=1, keepdims=True)
    member = member.T
    member_ref[...] = member.astype(BF)
    spread = jnp.broadcast_to(lengths, (WINDOW, HD)).astype(BF)
    length_ref[...] = dot(member.astype(BF), spread, ((1,), (0,)))


def head_sum_kernel(pieces_ref, out_ref, both_ref):
    both_ref[:, :HD] = jnp.sum(pieces_ref[...].astype(F32), axis=0).astype(BF)
    both_ref[:, HD:] = out_ref[...]


def last_kernel(before_ref, own_ref, picker_ref, member_ref, length_ref, out_ref, grad_ref):
    window = jnp.concatenate([before_ref[...], own_ref[...]], axis=0)
    out_ref[...] = dot(picker_ref[...], window[:, HD:], ((1,), (0,))).astype(BF)
    spread = dot(member_ref[...], window[:, :HD], ((1,), (0,)))
    grad_ref[...] = (spread / length_ref[...]).astype(BF)


def pool(c_ref, first, moved, place, byte_states, d_attn, w_qkv):
    hbm = pl.BlockSpec(memory_space=pltpu.HBM)
    vmem = pl.BlockSpec(memory_space=pltpu.VMEM)
    ins = (first, moved, place, byte_states, d_attn, w_qkv)
    spaces = (pltpu.SMEM, pltpu.SMEM) + (pltpu.VMEM,) * 4
    block = shaped((ROWS, 4 * FEATS), BF)
    return pl.pallas_call(
        pool_kernel,
        out_shape=(block, block),
        in_specs=[pl.BlockSpec(memory_space=pltpu.SMEM)] + [hbm] * len(ins),
        out_specs=(vmem, vmem),
        scratch_shapes=[space(x.shape, x.dtype) for space, x in zip(spaces, ins)]
        + [pltpu.SemaphoreType.DMA((len(ins) + 2,))],
        cost_estimate=pl.CostEstimate(flops=300_000_000, bytes_accessed=2_500_000, transcendentals=0),
        compiler_params=pltpu.CompilerParams(vmem_limit_bytes=60 * 1024 * 1024),
    )(c_ref, *ins)


def pair(rows, dtype=BF):
    return shaped((rows, 2 * HD), dtype)


def joined(c_ref, mine, got, axis):
    kernel = functools.partial(join_kernel, axis)
    return call(kernel, (c_ref, mine, got), (pair(2 * mine.shape[0]),), JOIN, 1)[0]


def halved(c_ref, keep, got, axis, dtype):
    half = keep.shape[0] // 2
    kernel = functools.partial(halve_kernel, axis)
    return call(kernel, (c_ref, keep, got), (pair(half, dtype), pair(half)), HALVE, 1)


def shards(byte_states, patch_of_byte, patch_first, moved, w_qkv, d_attn):
    c_ref = lax.axis_index(CTX).astype(I32).reshape(1)
    n_bytes = patch_of_byte.shape[0]
    place = patch_of_byte.reshape(1, n_bytes)
    stack = shaped((N_FAR, ROWS, 2 * HD), BF)

    sent, own = pool(c_ref, patch_first, moved, place, byte_states, d_attn, w_qkv)
    (own,) = call(hold_kernel, (own,), (shaped(own.shape, BF),), 100_000)
    keep, give, held = call(
        spread_kernel,
        (c_ref, own, shift(sent, CTX, N_CTX, -1)),
        (pair(ROWS), pair(ROWS), stack),
        1_000_000,
        1,
    )
    held = swap(held, FAR)
    asked = joined(c_ref, keep, shift(give, SPLIT, 2, 1), SPLIT)
    for axis in (TWICE, AGAIN):
        asked = joined(c_ref, asked, shift(asked, axis, 2, 1), axis)
    tile = shaped((TILE_K, TILE_Q), F32)
    stats, weight, dprob = call(
        forward_kernel,
        (c_ref, asked, held),
        (shaped((N_NEAR, 8, TILE_Q), F32), tile, tile),
        300_000_000,
        1,
    )
    terms, keep, give = call(
        backward_kernel,
        (c_ref, asked, held, stats, swap(stats, NEAR), weight, dprob),
        (stack, pair(TILE_Q // 2, F32), pair(TILE_Q // 2)),
        900_000_000,
        1,
    )
    terms = swap(terms, FAR)
    keep, give = halved(c_ref, keep, shift(give, AGAIN, 2, 1), TWICE, F32)
    keep, give = halved(c_ref, keep, shift(give, TWICE, 2, 1), SPLIT, BF)
    picker, member, length = call(
        place_kernel,
        (c_ref, patch_first, moved, place),
        (
            shaped((ROWS, WINDOW), BF),
            shaped((n_bytes, WINDOW), BF),
            shaped((n_bytes, HD), F32),
        ),
        10_000_000,
        3,
    )
    pieces, out = call(
        sum_kernel,
        (c_ref, terms, keep, shift(give, SPLIT, 2, 1), w_qkv, picker),
        (shaped((N_TP, ROWS, HD), BF), shaped((ROWS, FEATS), BF)),
        100_000_000,
        1,
        1,
    )
    (both,) = call(
        head_sum_kernel, (swap(pieces, "tp"), out), (shaped((ROWS, HD + FEATS), BF),), 100_000
    )
    attn_out, byte_grad = call(
        last_kernel,
        (shift(both, CTX, N_CTX, 1), both, picker, member, length),
        (shaped((ROWS, FEATS), BF), shaped((n_bytes, HD), BF)),
        10_000_000,
    )
    return attn_out, byte_grad


def solution(mesh):
    fine = Mesh(mesh.devices.reshape(SIZES), NAMES)
    placed = (P(CTX, None), P(CTX), P(), P(), P(None, None, "tp"), P(CTX, "tp"))
    return jax.shard_map(
        shards,
        mesh=fine,
        in_specs=placed,
        out_specs=(P(CTX, "tp"), P(CTX, "tp")),
        check_vma=False,
    )
```

```python
import functools

import jax
import jax.numpy as jnp
from jax import lax
from jax.experimental import pallas as pl
from jax.experimental.pallas import tpu as pltpu
from jax.sharding import Mesh, PartitionSpec as P

HD = 128
SIZES = (4, 2, 2, 2, 2, 8)
NAMES = ("zh", "zl", "yl", "xh", "xl", "tp")
CTX = ("zh", "zl", "yl", "xh", "xl")
BITS = {"zl": 3, "yl": 2, "xh": 1, "xl": 0}
SPLIT, TWICE, AGAIN = "xl", "yl", "zl"
NEAR = tuple(a for a in BITS if a in (TWICE, AGAIN))
REST = tuple(a for a in BITS if a not in NEAR)
FAR = ("zh",) + REST
N_CTX = 64
N_TP = 8
N_FAR = 16
N_NEAR = 4
N_ASK = 8
ROWS = 64
HEADS = 2
FEATS = HEADS * HD
TOTAL = N_CTX * ROWS
WINDOW = 2 * ROWS
HALF = ROWS // 2
TILE_Q = N_ASK * ROWS
TILE_K = N_FAR * ROWS
SCALE = HD ** (-0.5)
LOG2E = 1.4426950408889634
NEG = -1e30
FLOOR = -1e29
JOIN = 5_000_000_000
HALVE = 5_000_000_000
BF = jnp.bfloat16
F32 = jnp.float32
I32 = jnp.int32


def dot(a, b, dims):
    return lax.dot_general(a, b, (dims, ((), ())), preferred_element_type=F32)


def shift(x, axis, n, by):
    return lax.ppermute(x, axis, [(i, (i + by) % n) for i in range(n)])


def swap(x, axis):
    return lax.all_to_all(x, axis, split_axis=0, concat_axis=0, tiled=True)


def iota(shape, dim):
    return lax.broadcasted_iota(I32, shape, dim)


def call(kernel, ins, outs, flops, scalars=0, unread=0):
    smem = pl.BlockSpec(memory_space=pltpu.SMEM)
    vmem = pl.BlockSpec(memory_space=pltpu.VMEM)
    size = sum(x.size * x.dtype.itemsize for x in list(ins) + list(outs))
    return pl.pallas_call(
        kernel,
        out_shape=tuple(outs),
        in_specs=[smem] * scalars
        + [vmem] * (len(ins) - scalars - unread)
        + [pl.BlockSpec(memory_space=pl.ANY)] * unread,
        out_specs=tuple([vmem] * len(outs)),
        cost_estimate=pl.CostEstimate(flops=flops, bytes_accessed=size, transcendentals=0),
        compiler_params=pltpu.CompilerParams(vmem_limit_bytes=40 * 1024 * 1024),
    )(*ins)


def shaped(shape, dtype):
    return jax.ShapeDtypeStruct(shape, dtype)


def slot_order(c, first_ref, moved_ref, shape, dim):
    before, after = jnp.maximum(c - 1, 0), jnp.minimum(c + 1, N_CTX - 1)
    first = first_ref[c]
    low = moved_ref[0, c]
    prev_high = jnp.where(c > 0, moved_ref[1, before], 0)
    next_low = jnp.where(c < N_CTX - 1, moved_ref[0, after], 0)
    next_first = jnp.where(c < N_CTX - 1, first_ref[after], TOTAL)
    rank = iota(shape, dim)
    order = jnp.where(
        rank < prev_high,
        first - prev_high + rank,
        jnp.where(
            rank >= ROWS - next_low,
            next_first + rank - (ROWS - next_low),
            first + low + rank - prev_high,
        ),
    )
    return order - (ROWS * c - HALF)


def pool_kernel(
    c_ref, first_hbm, moved_hbm, place_hbm, bytes_hbm, grad_hbm, w_hbm, sent_ref, own_ref,
    first_ref, moved_ref, place_ref, bytes_ref, grad_ref, w_ref, sems,
):
    pairs = [
        (first_hbm, first_ref),
        (moved_hbm, moved_ref),
        (place_hbm, place_ref),
        (bytes_hbm, bytes_ref),
        (grad_hbm, grad_ref),
    ] + [(w_hbm.at[i], w_ref.at[i]) for i in range(3)]
    copies = [pltpu.make_async_copy(a, b, sems.at[i]) for i, (a, b) in enumerate(pairs)]
    for copy in copies:
        copy.start()
    for copy in copies[:5]:
        copy.wait()
    c = c_ref[0]
    offset = first_ref[c] - (ROWS * c - HALF)
    member = iota((WINDOW, bytes_ref.shape[0]), 0) == place_ref[...] + offset
    lengths = jnp.sum(member.astype(F32), axis=1, keepdims=True)
    pooled = dot(member.astype(F32).astype(BF), bytes_ref[...], ((1,), (0,)))
    pooled = (pooled / jnp.maximum(lengths, 1.0)).astype(BF)
    order = slot_order(c, first_ref, moved_ref, (WINDOW, ROWS), 1)
    slotted = (iota((WINDOW, ROWS), 0) == order).astype(F32).astype(BF)
    grads = dot(slotted, grad_ref[...], ((1,), (0,))).astype(BF)
    for at, value in ((0, None), (1, grads), (2, None), (3, None)):
        if value is None:
            part = max(at - 1, 0)
            copies[5 + part].wait()
            value = dot(pooled, w_ref[part], ((1,), (0,))).astype(BF)
        sent_ref[:, at * FEATS : (at + 1) * FEATS] = value[:ROWS]
        own_ref[:, at * FEATS : (at + 1) * FEATS] = value[ROWS:]


def columns(value, kind, head):
    at = kind * FEATS + head * HD
    return value[:, at : at + HD]


def hold_kernel(own_ref, held_ref):
    held_ref[...] = own_ref[...]


def bit(c, axis):
    return (c >> BITS[axis]) & 1


def spread_kernel(c_ref, own_ref, got_ref, keep_ref, give_ref, held_ref):
    both = own_ref[...] + got_ref[...]
    asked, held = [], []
    for e in range(HEADS):
        q, g, k, v = (columns(both, kind, e) for kind in range(4))
        asked.append(jnp.concatenate([q, g], axis=1))
        held.append(jnp.concatenate([k, v], axis=1))
    second = bit(c_ref[0], SPLIT) == 1
    keep_ref[...] = jnp.where(second, asked[1], asked[0])
    give_ref[...] = jnp.where(second, asked[0], asked[1])
    for i in range(N_FAR):
        held_ref[i] = held[head_of(i)]


def head_of(i):
    return (i >> (1 - REST.index(SPLIT))) & 1


def join_kernel(axis, c_ref, mine_ref, got_ref, out_ref):
    second = bit(c_ref[0], axis) == 1
    n = mine_ref.shape[0]
    mine, got = mine_ref[...], got_ref[...]
    out_ref[:n] = jnp.where(second, got, mine)
    out_ref[n:] = jnp.where(second, mine, got)


def halve_kernel(axis, c_ref, keep_ref, got_ref, rest_ref, give_ref):
    second = bit(c_ref[0], axis) == 1
    total = keep_ref[...] + got_ref[...].astype(F32)
    half = total.shape[0] // 2
    rest_ref[...] = jnp.where(second, total[half:], total[:half]).astype(rest_ref.dtype)
    give_ref[...] = jnp.where(second, total[:half], total[half:]).astype(BF)


def unpack(asked_ref, held_ref):
    k = held_ref[:, :, :HD].reshape(TILE_K, HD)
    v = held_ref[:, :, HD:].reshape(TILE_K, HD)
    return asked_ref[:, :HD], asked_ref[:, HD:], k, v


def moved_bits(index, axes, c):
    block = sum(((index >> i) & 1) << BITS[axis] for i, axis in enumerate(axes))
    fixed = sum(1 << BITS[axis] for axis in BITS if axis not in axes)
    return block + (c & fixed)


def scores(c, q, k):
    row = iota((1, TILE_Q), 1)
    block = moved_bits(row >> 6, (SPLIT, TWICE, AGAIN), c) + (c & 48)
    query = ROWS * block + (row & 63) + HALF
    col = iota((TILE_K, 1), 0)
    block = moved_bits(col >> 6, REST[::-1], c) + (col >> 8) * 16
    key = ROWS * block + (col & 63) + HALF
    allowed = (query & (TOTAL - 1)) >= (key & (TOTAL - 1))
    return jnp.where(allowed, dot(k, q, ((1,), (1,))) * (SCALE * LOG2E), NEG)


def forward_kernel(
    c_ref, mine_ref, got_ref, held_ref, stats_ref, weight_ref, dprob_ref, asked_ref
):
    join_kernel(AGAIN, c_ref, mine_ref, got_ref, asked_ref)
    q, g, k, v = unpack(asked_ref, held_ref)
    score = scores(c_ref[0], q, k)
    top = jnp.maximum(jnp.max(score, axis=0, keepdims=True), FLOOR)
    weight = jnp.exp2(score - top)
    dprob = dot(v, g, ((1,), (1,)))
    weight_ref[...] = weight
    dprob_ref[...] = dprob
    rows = [
        top,
        jnp.sum(weight, axis=0, keepdims=True),
        jnp.sum(weight * dprob, axis=0, keepdims=True),
    ]
    rows = jnp.concatenate(rows + [top] * 5, axis=0)
    for i in range(N_NEAR):
        stats_ref[i] = rows


def backward_kernel(
    c_ref, asked_ref, held_ref, own_ref, stats_ref, weight_ref, dprob_ref, term_ref, keep_ref, give_ref
):
    tops, sums, dots = (stats_ref[:, i, :] for i in range(3))
    peak = jnp.max(tops, axis=0, keepdims=True)
    each = jnp.exp2(tops - peak)
    norm = jnp.sum(each * sums, axis=0, keepdims=True)
    delta = jnp.sum(each * dots, axis=0, keepdims=True) / norm
    factor = jnp.exp2(own_ref[0, 0:1, :] - peak) / norm
    q, g, k, v = unpack(asked_ref, held_ref)
    prob = weight_ref[...] * factor
    dscore = (prob * (dprob_ref[...] - delta)).astype(BF)
    prob = prob.astype(BF)
    d_key = (dot(dscore, q, ((1,), (0,))) * SCALE).astype(BF)
    d_value = dot(prob, g, ((1,), (0,))).astype(BF)
    term_ref[:, :, :HD] = d_key.reshape(N_FAR, ROWS, HD)
    term_ref[:, :, HD:] = d_value.reshape(N_FAR, ROWS, HD)
    d_query = dot(dscore, k, ((0,), (0,))) * SCALE
    out = dot(prob, v, ((0,), (0,)))
    second = bit(c_ref[0], AGAIN) == 1
    half = TILE_Q // 2
    for value, at in ((d_query, 0), (out, HD)):
        keep_ref[:, at : at + HD] = jnp.where(second, value[half:], value[:half])
        give_ref[:, at : at + HD] = jnp.where(second, value[:half], value[half:]).astype(BF)


def sum_kernel(c_ref, term_ref, keep_ref, got_ref, w_ref, tables_any, piece_ref, out_ref):
    second = bit(c_ref[0], SPLIT) == 1
    keep, got = keep_ref[...], got_ref[...]
    asked = [jnp.where(second, got, keep), jnp.where(second, keep, got)]
    d_query = jnp.concatenate([x[:, :HD] for x in asked], axis=1)
    out_ref[...] = jnp.concatenate([x[:, HD:] for x in asked], axis=1)
    held = []
    for e in range(HEADS):
        total = jnp.zeros((ROWS, 2 * HD), F32)
        for i in range(N_FAR):
            if head_of(i) == e:
                total = total + term_ref[i].astype(F32)
        held.append(total.astype(BF))
    d_key = jnp.concatenate([x[:, :HD] for x in held], axis=1)
    d_value = jnp.concatenate([x[:, HD:] for x in held], axis=1)
    part = dot(d_query, w_ref[0], ((1,), (1,)))
    part = part + dot(d_key, w_ref[1], ((1,), (1,)))
    part = (part + dot(d_value, w_ref[2], ((1,), (1,)))).astype(BF)
    for i in range(N_TP):
        piece_ref[i] = part[:, i * HD : (i + 1) * HD]


def place_kernel(c_ref, first_ref, moved_ref, place_ref, picker_ref, member_ref, length_ref):
    c = c_ref[0]
    order = slot_order(c, first_ref, moved_ref, (ROWS, WINDOW), 0)
    picker_ref[...] = (iota((ROWS, WINDOW), 1) == order).astype(F32).astype(BF)
    offset = first_ref[c] - (ROWS * c - HALF)
    member = (iota((WINDOW, place_ref.shape[1]), 0) == place_ref[...] + offset).astype(F32)
    lengths = jnp.sum(member, axis=1, keepdims=True)
    member = member.T
    member_ref[...] = member.astype(BF)
    spread = jnp.broadcast_to(lengths, (WINDOW, HD)).astype(BF)
    length_ref[...] = dot(member.astype(BF), spread, ((1,), (0,)))


def head_sum_kernel(pieces_ref, out_ref, both_ref):
    both_ref[:, :HD] = jnp.sum(pieces_ref[...].astype(F32), axis=0).astype(BF)
    both_ref[:, HD:] = out_ref[...]


def last_kernel(before_ref, own_ref, picker_ref, member_ref, length_ref, out_ref, grad_ref):
    window = jnp.concatenate([before_ref[...], own_ref[...]], axis=0)
    out_ref[...] = dot(picker_ref[...], window[:, HD:], ((1,), (0,))).astype(BF)
    spread = dot(member_ref[...], window[:, :HD], ((1,), (0,)))
    grad_ref[...] = (spread / length_ref[...]).astype(BF)


def pool(c_ref, first, moved, place, byte_states, d_attn, w_qkv):
    hbm = pl.BlockSpec(memory_space=pltpu.HBM)
    vmem = pl.BlockSpec(memory_space=pltpu.VMEM)
    ins = (first, moved, place, byte_states, d_attn, w_qkv)
    spaces = (pltpu.SMEM, pltpu.SMEM) + (pltpu.VMEM,) * 4
    block = shaped((ROWS, 4 * FEATS), BF)
    return pl.pallas_call(
        pool_kernel,
        out_shape=(block, block),
        in_specs=[pl.BlockSpec(memory_space=pltpu.SMEM)] + [hbm] * len(ins),
        out_specs=(vmem, vmem),
        scratch_shapes=[space(x.shape, x.dtype) for space, x in zip(spaces, ins)]
        + [pltpu.SemaphoreType.DMA((len(ins) + 2,))],
        cost_estimate=pl.CostEstimate(flops=300_000_000, bytes_accessed=2_500_000, transcendentals=0),
        compiler_params=pltpu.CompilerParams(vmem_limit_bytes=60 * 1024 * 1024),
    )(c_ref, *ins)


def pair(rows, dtype=BF):
    return shaped((rows, 2 * HD), dtype)


def joined(c_ref, mine, got, axis):
    kernel = functools.partial(join_kernel, axis)
    return call(kernel, (c_ref, mine, got), (pair(2 * mine.shape[0]),), JOIN, 1)[0]


def halved(c_ref, keep, got, axis, dtype):
    half = keep.shape[0] // 2
    kernel = functools.partial(halve_kernel, axis)
    return call(kernel, (c_ref, keep, got), (pair(half, dtype), pair(half)), HALVE, 1)


def shards(byte_states, patch_of_byte, patch_first, moved, w_qkv, d_attn):
    c_ref = lax.axis_index(CTX).astype(I32).reshape(1)
    n_bytes = patch_of_byte.shape[0]
    place = patch_of_byte.reshape(1, n_bytes)
    stack = shaped((N_FAR, ROWS, 2 * HD), BF)

    sent, own = pool(c_ref, patch_first, moved, place, byte_states, d_attn, w_qkv)
    (own,) = call(hold_kernel, (own,), (shaped(own.shape, BF),), 100_000)
    keep, give, held = call(
        spread_kernel,
        (c_ref, own, shift(sent, CTX, N_CTX, -1)),
        (pair(ROWS), pair(ROWS), stack),
        1_000_000,
        1,
    )
    held = swap(held, FAR)
    asked = joined(c_ref, keep, shift(give, SPLIT, 2, 1), SPLIT)
    mine = joined(c_ref, asked, shift(asked, TWICE, 2, 1), TWICE)
    tile = shaped((TILE_K, TILE_Q), F32)
    stats, weight, dprob, asked = call(
        forward_kernel,
        (c_ref, mine, shift(mine, AGAIN, 2, 1), held),
        (shaped((N_NEAR, 8, TILE_Q), F32), tile, tile, pair(TILE_Q)),
        300_000_000,
        1,
    )
    terms, keep, give = call(
        backward_kernel,
        (c_ref, asked, held, stats, swap(stats, NEAR), weight, dprob),
        (stack, pair(TILE_Q // 2, F32), pair(TILE_Q // 2)),
        900_000_000,
        1,
    )
    terms = swap(terms, FAR)
    keep, give = halved(c_ref, keep, shift(give, AGAIN, 2, 1), TWICE, F32)
    keep, give = halved(c_ref, keep, shift(give, TWICE, 2, 1), SPLIT, BF)
    picker, member, length = call(
        place_kernel,
        (c_ref, patch_first, moved, place),
        (
            shaped((ROWS, WINDOW), BF),
            shaped((n_bytes, WINDOW), BF),
            shaped((n_bytes, HD), F32),
        ),
        10_000_000,
        3,
    )
    pieces, out = call(
        sum_kernel,
        (c_ref, terms, keep, shift(give, SPLIT, 2, 1), w_qkv, picker),
        (shaped((N_TP, ROWS, HD), BF), shaped((ROWS, FEATS), BF)),
        100_000_000,
        1,
        1,
    )
    (both,) = call(
        head_sum_kernel, (swap(pieces, "tp"), out), (shaped((ROWS, HD + FEATS), BF),), 100_000
    )
    attn_out, byte_grad = call(
        last_kernel,
        (shift(both, CTX, N_CTX, 1), both, picker, member, length),
        (shaped((ROWS, FEATS), BF), shaped((n_bytes, HD), BF)),
        10_000_000,
    )
    return attn_out, byte_grad


def solution(mesh):
    fine = Mesh(mesh.devices.reshape(SIZES), NAMES)
    placed = (P(CTX, None), P(CTX), P(), P(), P(None, None, "tp"), P(CTX, "tp"))
    return jax.shard_map(
        shards,
        mesh=fine,
        in_specs=placed,
        out_specs=(P(CTX, "tp"), P(CTX, "tp")),
        check_vma=False,
    )
```

```python
import functools

import jax
import jax.numpy as jnp
from jax import lax
from jax.experimental import pallas as pl
from jax.experimental.pallas import tpu as pltpu
from jax.sharding import Mesh, PartitionSpec as P

HD = 128
SIZES = (4, 2, 2, 2, 2, 8)
NAMES = ("zh", "zl", "yl", "xh", "xl", "tp")
CTX = ("zh", "zl", "yl", "xh", "xl")
BITS = {"zl": 3, "yl": 2, "xh": 1, "xl": 0}
SPLIT, TWICE, AGAIN = "xl", "yl", "zl"
NEAR = tuple(a for a in BITS if a in (TWICE, AGAIN))
REST = tuple(a for a in BITS if a not in NEAR)
FAR = ("zh",) + REST
N_CTX = 64
N_TP = 8
N_FAR = 16
N_NEAR = 4
N_ASK = 8
ROWS = 64
HEADS = 2
FEATS = HEADS * HD
TOTAL = N_CTX * ROWS
WINDOW = 2 * ROWS
HALF = ROWS // 2
TILE_Q = N_ASK * ROWS
TILE_K = N_FAR * ROWS
SCALE = HD ** (-0.5)
LOG2E = 1.4426950408889634
NEG = -1e30
FLOOR = -1e29
JOIN = 5_000_000_000
HALVE = 5_000_000_000
BF = jnp.bfloat16
F32 = jnp.float32
I32 = jnp.int32


def dot(a, b, dims):
    return lax.dot_general(a, b, (dims, ((), ())), preferred_element_type=F32)


def shift(x, axis, n, by):
    return lax.ppermute(x, axis, [(i, (i + by) % n) for i in range(n)])


def swap(x, axis):
    return lax.all_to_all(x, axis, split_axis=0, concat_axis=0, tiled=True)


def iota(shape, dim):
    return lax.broadcasted_iota(I32, shape, dim)


def call(kernel, ins, outs, flops, scalars=0, unread=0):
    smem = pl.BlockSpec(memory_space=pltpu.SMEM)
    vmem = pl.BlockSpec(memory_space=pltpu.VMEM)
    size = sum(x.size * x.dtype.itemsize for x in list(ins) + list(outs))
    return pl.pallas_call(
        kernel,
        out_shape=tuple(outs),
        in_specs=[smem] * scalars
        + [vmem] * (len(ins) - scalars - unread)
        + [pl.BlockSpec(memory_space=pl.ANY)] * unread,
        out_specs=tuple([vmem] * len(outs)),
        cost_estimate=pl.CostEstimate(flops=flops, bytes_accessed=size, transcendentals=0),
        compiler_params=pltpu.CompilerParams(vmem_limit_bytes=40 * 1024 * 1024),
    )(*ins)


def shaped(shape, dtype):
    return jax.ShapeDtypeStruct(shape, dtype)


def slot_order(c, first_ref, moved_ref, shape, dim):
    before, after = jnp.maximum(c - 1, 0), jnp.minimum(c + 1, N_CTX - 1)
    first = first_ref[c]
    low = moved_ref[0, c]
    prev_high = jnp.where(c > 0, moved_ref[1, before], 0)
    next_low = jnp.where(c < N_CTX - 1, moved_ref[0, after], 0)
    next_first = jnp.where(c < N_CTX - 1, first_ref[after], TOTAL)
    rank = iota(shape, dim)
    order = jnp.where(
        rank < prev_high,
        first - prev_high + rank,
        jnp.where(
            rank >= ROWS - next_low,
            next_first + rank - (ROWS - next_low),
            first + low + rank - prev_high,
        ),
    )
    return order - (ROWS * c - HALF)


def pool_kernel(
    c_ref, first_hbm, moved_hbm, place_hbm, bytes_hbm, grad_hbm, w_hbm, sent_hbm, own_hbm,
    first_ref, moved_ref, place_ref, bytes_ref, grad_ref, w_ref, sems, sent_ref, own_ref, outs,
):
    pairs = [
        (first_hbm, first_ref),
        (moved_hbm, moved_ref),
        (place_hbm, place_ref),
        (bytes_hbm, bytes_ref),
        (grad_hbm, grad_ref),
    ] + [(w_hbm.at[i], w_ref.at[i]) for i in range(3)]
    copies = [pltpu.make_async_copy(a, b, sems.at[i]) for i, (a, b) in enumerate(pairs)]
    for copy in copies:
        copy.start()
    for copy in copies[:5]:
        copy.wait()
    c = c_ref[0]
    offset = first_ref[c] - (ROWS * c - HALF)
    member = iota((WINDOW, bytes_ref.shape[0]), 0) == place_ref[...] + offset
    lengths = jnp.sum(member.astype(F32), axis=1, keepdims=True)
    pooled = dot(member.astype(F32).astype(BF), bytes_ref[...], ((1,), (0,)))
    pooled = (pooled / jnp.maximum(lengths, 1.0)).astype(BF)
    order = slot_order(c, first_ref, moved_ref, (WINDOW, ROWS), 1)
    slotted = (iota((WINDOW, ROWS), 0) == order).astype(F32).astype(BF)
    grads = dot(slotted, grad_ref[...], ((1,), (0,))).astype(BF)
    leaving = []
    for at, value in ((1, grads), (0, None), (2, None), (3, None)):
        if value is None:
            part = max(at - 1, 0)
            copies[5 + part].wait()
            value = dot(pooled, w_ref[part], ((1,), (0,))).astype(BF)
        place = slice(at * FEATS, (at + 1) * FEATS)
        sent_ref[:, place] = value[:ROWS]
        own_ref[:, place] = value[ROWS:]
        for i, (a, b) in enumerate(((sent_ref, sent_hbm), (own_ref, own_hbm))):
            copy = pltpu.make_async_copy(a.at[:, place], b.at[:, place], outs.at[2 * at + i])
            copy.start()
            leaving.append(copy)
    for copy in leaving:
        copy.wait()


def columns(value, kind, head):
    at = kind * FEATS + head * HD
    return value[:, at : at + HD]


def hold_kernel(own_ref, held_ref):
    held_ref[...] = own_ref[...]


def bit(c, axis):
    return (c >> BITS[axis]) & 1


def spread_kernel(c_ref, own_ref, got_ref, keep_ref, give_ref, held_ref):
    both = own_ref[...] + got_ref[...]
    asked, held = [], []
    for e in range(HEADS):
        q, g, k, v = (columns(both, kind, e) for kind in range(4))
        asked.append(jnp.concatenate([q, g], axis=1))
        held.append(jnp.concatenate([k, v], axis=1))
    second = bit(c_ref[0], SPLIT) == 1
    keep_ref[...] = jnp.where(second, asked[1], asked[0])
    give_ref[...] = jnp.where(second, asked[0], asked[1])
    for i in range(N_FAR):
        held_ref[i] = held[head_of(i)]


def head_of(i):
    return (i >> (1 - REST.index(SPLIT))) & 1


def join_kernel(axis, c_ref, mine_ref, got_ref, out_ref):
    second = bit(c_ref[0], axis) == 1
    n = mine_ref.shape[0]
    mine, got = mine_ref[...], got_ref[...]
    out_ref[:n] = jnp.where(second, got, mine)
    out_ref[n:] = jnp.where(second, mine, got)


def halve_kernel(axis, c_ref, keep_ref, got_ref, rest_ref, give_ref):
    second = bit(c_ref[0], axis) == 1
    total = keep_ref[...] + got_ref[...].astype(F32)
    half = total.shape[0] // 2
    rest_ref[...] = jnp.where(second, total[half:], total[:half]).astype(rest_ref.dtype)
    give_ref[...] = jnp.where(second, total[:half], total[half:]).astype(BF)


def unpack(asked_ref, held_ref):
    k = held_ref[:, :, :HD].reshape(TILE_K, HD)
    v = held_ref[:, :, HD:].reshape(TILE_K, HD)
    return asked_ref[:, :HD], asked_ref[:, HD:], k, v


def moved_bits(index, axes, c):
    block = sum(((index >> i) & 1) << BITS[axis] for i, axis in enumerate(axes))
    fixed = sum(1 << BITS[axis] for axis in BITS if axis not in axes)
    return block + (c & fixed)


def scores(c, q, k):
    row = iota((1, TILE_Q), 1)
    block = moved_bits(row >> 6, (SPLIT, TWICE, AGAIN), c) + (c & 48)
    query = ROWS * block + (row & 63) + HALF
    col = iota((TILE_K, 1), 0)
    block = moved_bits(col >> 6, REST[::-1], c) + (col >> 8) * 16
    key = ROWS * block + (col & 63) + HALF
    allowed = (query & (TOTAL - 1)) >= (key & (TOTAL - 1))
    return jnp.where(allowed, dot(k, q, ((1,), (1,))) * (SCALE * LOG2E), NEG)


def forward_kernel(
    c_ref, mine_ref, got_ref, held_ref, stats_ref, weight_ref, dprob_ref, asked_ref
):
    join_kernel(AGAIN, c_ref, mine_ref, got_ref, asked_ref)
    q, g, k, v = unpack(asked_ref, held_ref)
    score = scores(c_ref[0], q, k)
    top = jnp.maximum(jnp.max(score, axis=0, keepdims=True), FLOOR)
    weight = jnp.exp2(score - top)
    dprob = dot(v, g, ((1,), (1,)))
    weight_ref[...] = weight
    dprob_ref[...] = dprob
    rows = [
        top,
        jnp.sum(weight, axis=0, keepdims=True),
        jnp.sum(weight * dprob, axis=0, keepdims=True),
    ]
    rows = jnp.concatenate(rows + [top] * 5, axis=0)
    for i in range(N_NEAR):
        stats_ref[i] = rows


def backward_kernel(
    c_ref, asked_ref, held_ref, own_ref, stats_ref, weight_ref, dprob_ref, term_ref, keep_ref, give_ref
):
    tops, sums, dots = (stats_ref[:, i, :] for i in range(3))
    peak = jnp.max(tops, axis=0, keepdims=True)
    each = jnp.exp2(tops - peak)
    norm = jnp.sum(each * sums, axis=0, keepdims=True)
    delta = jnp.sum(each * dots, axis=0, keepdims=True) / norm
    factor = jnp.exp2(own_ref[0, 0:1, :] - peak) / norm
    q, g, k, v = unpack(asked_ref, held_ref)
    prob = weight_ref[...] * factor
    dscore = (prob * (dprob_ref[...] - delta)).astype(BF)
    prob = prob.astype(BF)
    d_key = (dot(dscore, q, ((1,), (0,))) * SCALE).astype(BF)
    d_value = dot(prob, g, ((1,), (0,))).astype(BF)
    term_ref[:, :, :HD] = d_key.reshape(N_FAR, ROWS, HD)
    term_ref[:, :, HD:] = d_value.reshape(N_FAR, ROWS, HD)
    d_query = dot(dscore, k, ((0,), (0,))) * SCALE
    out = dot(prob, v, ((0,), (0,)))
    second = bit(c_ref[0], AGAIN) == 1
    half = TILE_Q // 2
    for value, at in ((d_query, 0), (out, HD)):
        keep_ref[:, at : at + HD] = jnp.where(second, value[half:], value[:half])
        give_ref[:, at : at + HD] = jnp.where(second, value[:half], value[half:]).astype(BF)


def sum_kernel(c_ref, term_ref, keep_ref, got_ref, w_ref, tables_any, piece_ref, out_ref):
    second = bit(c_ref[0], SPLIT) == 1
    keep, got = keep_ref[...], got_ref[...]
    asked = [jnp.where(second, got, keep), jnp.where(second, keep, got)]
    d_query = jnp.concatenate([x[:, :HD] for x in asked], axis=1)
    out_ref[...] = jnp.concatenate([x[:, HD:] for x in asked], axis=1)
    held = []
    for e in range(HEADS):
        total = jnp.zeros((ROWS, 2 * HD), F32)
        for i in range(N_FAR):
            if head_of(i) == e:
                total = total + term_ref[i].astype(F32)
        held.append(total.astype(BF))
    d_key = jnp.concatenate([x[:, :HD] for x in held], axis=1)
    d_value = jnp.concatenate([x[:, HD:] for x in held], axis=1)
    part = dot(d_query, w_ref[0], ((1,), (1,)))
    part = part + dot(d_key, w_ref[1], ((1,), (1,)))
    part = (part + dot(d_value, w_ref[2], ((1,), (1,)))).astype(BF)
    for i in range(N_TP):
        piece_ref[i] = part[:, i * HD : (i + 1) * HD]


def place_kernel(c_ref, first_ref, moved_ref, place_ref, picker_ref, member_ref, length_ref):
    c = c_ref[0]
    order = slot_order(c, first_ref, moved_ref, (ROWS, WINDOW), 0)
    picker_ref[...] = (iota((ROWS, WINDOW), 1) == order).astype(F32).astype(BF)
    offset = first_ref[c] - (ROWS * c - HALF)
    member = (iota((WINDOW, place_ref.shape[1]), 0) == place_ref[...] + offset).astype(F32)
    lengths = jnp.sum(member, axis=1, keepdims=True)
    member = member.T
    member_ref[...] = member.astype(BF)
    spread = jnp.broadcast_to(lengths, (WINDOW, HD)).astype(BF)
    length_ref[...] = dot(member.astype(BF), spread, ((1,), (0,)))


def head_sum_kernel(pieces_ref, out_ref, both_ref):
    both_ref[:, :HD] = jnp.sum(pieces_ref[...].astype(F32), axis=0).astype(BF)
    both_ref[:, HD:] = out_ref[...]


def last_kernel(before_ref, own_ref, picker_ref, member_ref, length_ref, out_ref, grad_ref):
    window = jnp.concatenate([before_ref[...], own_ref[...]], axis=0)
    out_ref[...] = dot(picker_ref[...], window[:, HD:], ((1,), (0,))).astype(BF)
    spread = dot(member_ref[...], window[:, :HD], ((1,), (0,)))
    grad_ref[...] = (spread / length_ref[...]).astype(BF)


def pool(c_ref, first, moved, place, byte_states, d_attn, w_qkv):
    hbm = pl.BlockSpec(memory_space=pltpu.HBM)
    ins = (first, moved, place, byte_states, d_attn, w_qkv)
    spaces = (pltpu.SMEM, pltpu.SMEM) + (pltpu.VMEM,) * 4
    block = shaped((ROWS, 4 * FEATS), BF)
    return pl.pallas_call(
        pool_kernel,
        out_shape=(block, block),
        in_specs=[pl.BlockSpec(memory_space=pltpu.SMEM)] + [hbm] * len(ins),
        out_specs=(hbm, hbm),
        scratch_shapes=[space(x.shape, x.dtype) for space, x in zip(spaces, ins)]
        + [
            pltpu.SemaphoreType.DMA((len(ins) + 2,)),
            pltpu.VMEM(block.shape, BF),
            pltpu.VMEM(block.shape, BF),
            pltpu.SemaphoreType.DMA((8,)),
        ],
        cost_estimate=pl.CostEstimate(flops=300_000_000, bytes_accessed=2_500_000, transcendentals=0),
        compiler_params=pltpu.CompilerParams(vmem_limit_bytes=60 * 1024 * 1024),
    )(c_ref, *ins)


def pair(rows, dtype=BF):
    return shaped((rows, 2 * HD), dtype)


def joined(c_ref, mine, got, axis):
    kernel = functools.partial(join_kernel, axis)
    return call(kernel, (c_ref, mine, got), (pair(2 * mine.shape[0]),), JOIN, 1)[0]


def halved(c_ref, keep, got, axis, dtype):
    half = keep.shape[0] // 2
    kernel = functools.partial(halve_kernel, axis)
    return call(kernel, (c_ref, keep, got), (pair(half, dtype), pair(half)), HALVE, 1)


def shards(byte_states, patch_of_byte, patch_first, moved, w_qkv, d_attn):
    c_ref = lax.axis_index(CTX).astype(I32).reshape(1)
    n_bytes = patch_of_byte.shape[0]
    place = patch_of_byte.reshape(1, n_bytes)
    stack = shaped((N_FAR, ROWS, 2 * HD), BF)

    sent, own = pool(c_ref, patch_first, moved, place, byte_states, d_attn, w_qkv)
    (own,) = call(hold_kernel, (own,), (shaped(own.shape, BF),), 100_000)
    keep, give, held = call(
        spread_kernel,
        (c_ref, own, shift(sent, CTX, N_CTX, -1)),
        (pair(ROWS), pair(ROWS), stack),
        1_000_000,
        1,
    )
    held = swap(held, FAR)
    asked = joined(c_ref, keep, shift(give, SPLIT, 2, 1), SPLIT)
    mine = joined(c_ref, asked, shift(asked, TWICE, 2, 1), TWICE)
    tile = shaped((TILE_K, TILE_Q), F32)
    stats, weight, dprob, asked = call(
        forward_kernel,
        (c_ref, mine, shift(mine, AGAIN, 2, 1), held),
        (shaped((N_NEAR, 8, TILE_Q), F32), tile, tile, pair(TILE_Q)),
        300_000_000,
        1,
    )
    terms, keep, give = call(
        backward_kernel,
        (c_ref, asked, held, stats, swap(stats, NEAR), weight, dprob),
        (stack, pair(TILE_Q // 2, F32), pair(TILE_Q // 2)),
        900_000_000,
        1,
    )
    terms = swap(terms, FAR)
    keep, give = halved(c_ref, keep, shift(give, AGAIN, 2, 1), TWICE, F32)
    keep, give = halved(c_ref, keep, shift(give, TWICE, 2, 1), SPLIT, BF)
    picker, member, length = call(
        place_kernel,
        (c_ref, patch_first, moved, place),
        (
            shaped((ROWS, WINDOW), BF),
            shaped((n_bytes, WINDOW), BF),
            shaped((n_bytes, HD), F32),
        ),
        10_000_000,
        3,
    )
    pieces, out = call(
        sum_kernel,
        (c_ref, terms, keep, shift(give, SPLIT, 2, 1), w_qkv, picker),
        (shaped((N_TP, ROWS, HD), BF), shaped((ROWS, FEATS), BF)),
        100_000_000,
        1,
        1,
    )
    (both,) = call(
        head_sum_kernel, (swap(pieces, "tp"), out), (shaped((ROWS, HD + FEATS), BF),), 100_000
    )
    attn_out, byte_grad = call(
        last_kernel,
        (shift(both, CTX, N_CTX, 1), both, picker, member, length),
        (shaped((ROWS, FEATS), BF), shaped((n_bytes, HD), BF)),
        10_000_000,
    )
    return attn_out, byte_grad


def solution(mesh):
    fine = Mesh(mesh.devices.reshape(SIZES), NAMES)
    placed = (P(CTX, None), P(CTX), P(), P(), P(None, None, "tp"), P(CTX, "tp"))
    return jax.shard_map(
        shards,
        mesh=fine,
        in_specs=placed,
        out_specs=(P(CTX, "tp"), P(CTX, "tp")),
        check_vma=False,
    )
```

```python
import functools

import jax
import jax.numpy as jnp
from jax import lax
from jax.experimental import pallas as pl
from jax.experimental.pallas import tpu as pltpu
from jax.sharding import Mesh, PartitionSpec as P

HD = 128
SIZES = (4, 2, 2, 2, 2, 8)
NAMES = ("zh", "zl", "yl", "xh", "xl", "tp")
CTX = ("zh", "zl", "yl", "xh", "xl")
BITS = {"zl": 3, "yl": 2, "xh": 1, "xl": 0}
SPLIT, TWICE, AGAIN = "xl", "yl", "zl"
NEAR = tuple(a for a in BITS if a in (TWICE, AGAIN))
REST = tuple(a for a in BITS if a not in NEAR)
FAR = ("zh",) + REST
N_CTX = 64
N_TP = 8
N_FAR = 16
N_NEAR = 4
N_ASK = 8
ROWS = 64
HEADS = 2
FEATS = HEADS * HD
TOTAL = N_CTX * ROWS
WINDOW = 2 * ROWS
HALF = ROWS // 2
TILE_Q = N_ASK * ROWS
TILE_K = N_FAR * ROWS
SCALE = HD ** (-0.5)
LOG2E = 1.4426950408889634
NEG = -1e30
FLOOR = -1e29
JOIN = 5_000_000_000
HALVE = 5_000_000_000
BF = jnp.bfloat16
F32 = jnp.float32
I32 = jnp.int32


def dot(a, b, dims):
    return lax.dot_general(a, b, (dims, ((), ())), preferred_element_type=F32)


def shift(x, axis, n, by):
    return lax.ppermute(x, axis, [(i, (i + by) % n) for i in range(n)])


def swap(x, axis):
    return lax.all_to_all(x, axis, split_axis=0, concat_axis=0, tiled=True)


def iota(shape, dim):
    return lax.broadcasted_iota(I32, shape, dim)


def call(kernel, ins, outs, flops, scalars=0, unread=0):
    smem = pl.BlockSpec(memory_space=pltpu.SMEM)
    vmem = pl.BlockSpec(memory_space=pltpu.VMEM)
    size = sum(x.size * x.dtype.itemsize for x in list(ins) + list(outs))
    return pl.pallas_call(
        kernel,
        out_shape=tuple(outs),
        in_specs=[smem] * scalars
        + [vmem] * (len(ins) - scalars - unread)
        + [pl.BlockSpec(memory_space=pl.ANY)] * unread,
        out_specs=tuple([vmem] * len(outs)),
        cost_estimate=pl.CostEstimate(flops=flops, bytes_accessed=size, transcendentals=0),
        compiler_params=pltpu.CompilerParams(vmem_limit_bytes=40 * 1024 * 1024),
    )(*ins)


def shaped(shape, dtype):
    return jax.ShapeDtypeStruct(shape, dtype)


def slot_order(c, first_ref, moved_ref, shape, dim):
    before, after = jnp.maximum(c - 1, 0), jnp.minimum(c + 1, N_CTX - 1)
    first = first_ref[c]
    low = moved_ref[0, c]
    prev_high = jnp.where(c > 0, moved_ref[1, before], 0)
    next_low = jnp.where(c < N_CTX - 1, moved_ref[0, after], 0)
    next_first = jnp.where(c < N_CTX - 1, first_ref[after], TOTAL)
    rank = iota(shape, dim)
    order = jnp.where(
        rank < prev_high,
        first - prev_high + rank,
        jnp.where(
            rank >= ROWS - next_low,
            next_first + rank - (ROWS - next_low),
            first + low + rank - prev_high,
        ),
    )
    return order - (ROWS * c - HALF)


def pool_kernel(
    c_ref, first_hbm, moved_hbm, place_hbm, bytes_hbm, grad_hbm, w_hbm, sent_ref, own_ref,
    first_ref, moved_ref, place_ref, bytes_ref, grad_ref, w_ref, sems,
):
    pairs = [
        (first_hbm, first_ref),
        (moved_hbm, moved_ref),
        (place_hbm, place_ref),
        (bytes_hbm, bytes_ref),
        (grad_hbm, grad_ref),
    ] + [(w_hbm.at[i], w_ref.at[i]) for i in range(3)]
    copies = [pltpu.make_async_copy(a, b, sems.at[i]) for i, (a, b) in enumerate(pairs)]
    for i in (3, 2, 5, 6, 7, 0, 1, 4):
        copies[i].start()
    for copy in copies[:5]:
        copy.wait()
    c = c_ref[0]
    offset = first_ref[c] - (ROWS * c - HALF)
    member = iota((WINDOW, bytes_ref.shape[0]), 0) == place_ref[...] + offset
    lengths = jnp.sum(member.astype(F32), axis=1, keepdims=True)
    pooled = dot(member.astype(F32).astype(BF), bytes_ref[...], ((1,), (0,)))
    pooled = (pooled / jnp.maximum(lengths, 1.0)).astype(BF)
    order = slot_order(c, first_ref, moved_ref, (WINDOW, ROWS), 1)
    slotted = (iota((WINDOW, ROWS), 0) == order).astype(F32).astype(BF)
    grads = dot(slotted, grad_ref[...], ((1,), (0,))).astype(BF)
    for at, value in ((0, None), (1, grads), (2, None), (3, None)):
        if value is None:
            part = max(at - 1, 0)
            copies[5 + part].wait()
            value = dot(pooled, w_ref[part], ((1,), (0,))).astype(BF)
        sent_ref[:, at * FEATS : (at + 1) * FEATS] = value[:ROWS]
        own_ref[:, at * FEATS : (at + 1) * FEATS] = value[ROWS:]


def columns(value, kind, head):
    at = kind * FEATS + head * HD
    return value[:, at : at + HD]


def hold_kernel(own_ref, held_ref):
    held_ref[...] = own_ref[...]


def bit(c, axis):
    return (c >> BITS[axis]) & 1


def spread_kernel(c_ref, own_ref, got_ref, keep_ref, give_ref, held_ref):
    both = own_ref[...] + got_ref[...]
    asked, held = [], []
    for e in range(HEADS):
        q, g, k, v = (columns(both, kind, e) for kind in range(4))
        asked.append(jnp.concatenate([q, g], axis=1))
        held.append(jnp.concatenate([k, v], axis=1))
    second = bit(c_ref[0], SPLIT) == 1
    keep_ref[...] = jnp.where(second, asked[1], asked[0])
    give_ref[...] = jnp.where(second, asked[0], asked[1])
    for i in range(N_FAR):
        held_ref[i] = held[head_of(i)]


def head_of(i):
    return (i >> (1 - REST.index(SPLIT))) & 1


def join_kernel(axis, c_ref, mine_ref, got_ref, out_ref):
    second = bit(c_ref[0], axis) == 1
    n = mine_ref.shape[0]
    mine, got = mine_ref[...], got_ref[...]
    out_ref[:n] = jnp.where(second, got, mine)
    out_ref[n:] = jnp.where(second, mine, got)


def halve_kernel(axis, c_ref, keep_ref, got_ref, rest_ref, give_ref):
    second = bit(c_ref[0], axis) == 1
    total = keep_ref[...] + got_ref[...].astype(F32)
    half = total.shape[0] // 2
    rest_ref[...] = jnp.where(second, total[half:], total[:half]).astype(rest_ref.dtype)
    give_ref[...] = jnp.where(second, total[:half], total[half:]).astype(BF)


def unpack(asked_ref, held_ref):
    k = held_ref[:, :, :HD].reshape(TILE_K, HD)
    v = held_ref[:, :, HD:].reshape(TILE_K, HD)
    return asked_ref[:, :HD], asked_ref[:, HD:], k, v


def moved_bits(index, axes, c):
    block = sum(((index >> i) & 1) << BITS[axis] for i, axis in enumerate(axes))
    fixed = sum(1 << BITS[axis] for axis in BITS if axis not in axes)
    return block + (c & fixed)


def scores(c, q, k):
    row = iota((1, TILE_Q), 1)
    block = moved_bits(row >> 6, (SPLIT, TWICE, AGAIN), c) + (c & 48)
    query = ROWS * block + (row & 63) + HALF
    col = iota((TILE_K, 1), 0)
    block = moved_bits(col >> 6, REST[::-1], c) + (col >> 8) * 16
    key = ROWS * block + (col & 63) + HALF
    allowed = (query & (TOTAL - 1)) >= (key & (TOTAL - 1))
    return jnp.where(allowed, dot(k, q, ((1,), (1,))) * (SCALE * LOG2E), NEG)


def forward_kernel(
    c_ref, mine_ref, got_ref, held_ref, stats_ref, weight_ref, dprob_ref, asked_ref
):
    join_kernel(AGAIN, c_ref, mine_ref, got_ref, asked_ref)
    q, g, k, v = unpack(asked_ref, held_ref)
    score = scores(c_ref[0], q, k)
    top = jnp.maximum(jnp.max(score, axis=0, keepdims=True), FLOOR)
    weight = jnp.exp2(score - top)
    dprob = dot(v, g, ((1,), (1,)))
    weight_ref[...] = weight
    dprob_ref[...] = dprob
    rows = [
        top,
        jnp.sum(weight, axis=0, keepdims=True),
        jnp.sum(weight * dprob, axis=0, keepdims=True),
    ]
    rows = jnp.concatenate(rows + [top] * 5, axis=0)
    for i in range(N_NEAR):
        stats_ref[i] = rows


def backward_kernel(
    c_ref, asked_ref, held_ref, own_ref, stats_ref, weight_ref, dprob_ref, term_ref, keep_ref, give_ref
):
    tops, sums, dots = (stats_ref[:, i, :] for i in range(3))
    peak = jnp.max(tops, axis=0, keepdims=True)
    each = jnp.exp2(tops - peak)
    norm = jnp.sum(each * sums, axis=0, keepdims=True)
    delta = jnp.sum(each * dots, axis=0, keepdims=True) / norm
    factor = jnp.exp2(own_ref[0, 0:1, :] - peak) / norm
    q, g, k, v = unpack(asked_ref, held_ref)
    prob = weight_ref[...] * factor
    dscore = (prob * (dprob_ref[...] - delta)).astype(BF)
    prob = prob.astype(BF)
    d_key = (dot(dscore, q, ((1,), (0,))) * SCALE).astype(BF)
    d_value = dot(prob, g, ((1,), (0,))).astype(BF)
    term_ref[:, :, :HD] = d_key.reshape(N_FAR, ROWS, HD)
    term_ref[:, :, HD:] = d_value.reshape(N_FAR, ROWS, HD)
    d_query = dot(dscore, k, ((0,), (0,))) * SCALE
    out = dot(prob, v, ((0,), (0,)))
    second = bit(c_ref[0], AGAIN) == 1
    half = TILE_Q // 2
    for value, at in ((d_query, 0), (out, HD)):
        keep_ref[:, at : at + HD] = jnp.where(second, value[half:], value[:half])
        give_ref[:, at : at + HD] = jnp.where(second, value[:half], value[half:]).astype(BF)


def sum_kernel(c_ref, term_ref, keep_ref, got_ref, w_ref, tables_any, piece_ref, out_ref):
    second = bit(c_ref[0], SPLIT) == 1
    keep, got = keep_ref[...], got_ref[...]
    asked = [jnp.where(second, got, keep), jnp.where(second, keep, got)]
    d_query = jnp.concatenate([x[:, :HD] for x in asked], axis=1)
    out_ref[...] = jnp.concatenate([x[:, HD:] for x in asked], axis=1)
    held = []
    for e in range(HEADS):
        total = jnp.zeros((ROWS, 2 * HD), F32)
        for i in range(N_FAR):
            if head_of(i) == e:
                total = total + term_ref[i].astype(F32)
        held.append(total.astype(BF))
    d_key = jnp.concatenate([x[:, :HD] for x in held], axis=1)
    d_value = jnp.concatenate([x[:, HD:] for x in held], axis=1)
    part = dot(d_query, w_ref[0], ((1,), (1,)))
    part = part + dot(d_key, w_ref[1], ((1,), (1,)))
    part = (part + dot(d_value, w_ref[2], ((1,), (1,)))).astype(BF)
    for i in range(N_TP):
        piece_ref[i] = part[:, i * HD : (i + 1) * HD]


def place_kernel(c_ref, first_ref, moved_ref, place_ref, picker_ref, member_ref, length_ref):
    c = c_ref[0]
    order = slot_order(c, first_ref, moved_ref, (ROWS, WINDOW), 0)
    picker_ref[...] = (iota((ROWS, WINDOW), 1) == order).astype(F32).astype(BF)
    offset = first_ref[c] - (ROWS * c - HALF)
    member = (iota((WINDOW, place_ref.shape[1]), 0) == place_ref[...] + offset).astype(F32)
    lengths = jnp.sum(member, axis=1, keepdims=True)
    member = member.T
    member_ref[...] = member.astype(BF)
    spread = jnp.broadcast_to(lengths, (WINDOW, HD)).astype(BF)
    length_ref[...] = dot(member.astype(BF), spread, ((1,), (0,)))


def head_sum_kernel(pieces_ref, out_ref, both_ref):
    both_ref[:, :HD] = jnp.sum(pieces_ref[...].astype(F32), axis=0).astype(BF)
    both_ref[:, HD:] = out_ref[...]


def last_kernel(before_ref, own_ref, picker_ref, member_ref, length_ref, out_ref, grad_ref):
    window = jnp.concatenate([before_ref[...], own_ref[...]], axis=0)
    out_ref[...] = dot(picker_ref[...], window[:, HD:], ((1,), (0,))).astype(BF)
    spread = dot(member_ref[...], window[:, :HD], ((1,), (0,)))
    grad_ref[...] = (spread / length_ref[...]).astype(BF)


def pool(c_ref, first, moved, place, byte_states, d_attn, w_qkv):
    hbm = pl.BlockSpec(memory_space=pltpu.HBM)
    vmem = pl.BlockSpec(memory_space=pltpu.VMEM)
    ins = (first, moved, place, byte_states, d_attn, w_qkv)
    spaces = (pltpu.SMEM, pltpu.SMEM) + (pltpu.VMEM,) * 4
    block = shaped((ROWS, 4 * FEATS), BF)
    return pl.pallas_call(
        pool_kernel,
        out_shape=(block, block),
        in_specs=[pl.BlockSpec(memory_space=pltpu.SMEM)] + [hbm] * len(ins),
        out_specs=(vmem, vmem),
        scratch_shapes=[space(x.shape, x.dtype) for space, x in zip(spaces, ins)]
        + [pltpu.SemaphoreType.DMA((len(ins) + 2,))],
        cost_estimate=pl.CostEstimate(flops=300_000_000, bytes_accessed=2_500_000, transcendentals=0),
        compiler_params=pltpu.CompilerParams(vmem_limit_bytes=60 * 1024 * 1024),
    )(c_ref, *ins)


def pair(rows, dtype=BF):
    return shaped((rows, 2 * HD), dtype)


def joined(c_ref, mine, got, axis):
    kernel = functools.partial(join_kernel, axis)
    return call(kernel, (c_ref, mine, got), (pair(2 * mine.shape[0]),), JOIN, 1)[0]


def halved(c_ref, keep, got, axis, dtype):
    half = keep.shape[0] // 2
    kernel = functools.partial(halve_kernel, axis)
    return call(kernel, (c_ref, keep, got), (pair(half, dtype), pair(half)), HALVE, 1)


def shards(byte_states, patch_of_byte, patch_first, moved, w_qkv, d_attn):
    c_ref = lax.axis_index(CTX).astype(I32).reshape(1)
    n_bytes = patch_of_byte.shape[0]
    place = patch_of_byte.reshape(1, n_bytes)
    stack = shaped((N_FAR, ROWS, 2 * HD), BF)

    sent, own = pool(c_ref, patch_first, moved, place, byte_states, d_attn, w_qkv)
    (own,) = call(hold_kernel, (own,), (shaped(own.shape, BF),), 100_000)
    keep, give, held = call(
        spread_kernel,
        (c_ref, own, shift(sent, CTX, N_CTX, -1)),
        (pair(ROWS), pair(ROWS), stack),
        1_000_000,
        1,
    )
    held = swap(held, FAR)
    asked = joined(c_ref, keep, shift(give, SPLIT, 2, 1), SPLIT)
    mine = joined(c_ref, asked, shift(asked, TWICE, 2, 1), TWICE)
    tile = shaped((TILE_K, TILE_Q), F32)
    stats, weight, dprob, asked = call(
        forward_kernel,
        (c_ref, mine, shift(mine, AGAIN, 2, 1), held),
        (shaped((N_NEAR, 8, TILE_Q), F32), tile, tile, pair(TILE_Q)),
        300_000_000,
        1,
    )
    terms, keep, give = call(
        backward_kernel,
        (c_ref, asked, held, stats, swap(stats, NEAR), weight, dprob),
        (stack, pair(TILE_Q // 2, F32), pair(TILE_Q // 2)),
        900_000_000,
        1,
    )
    terms = swap(terms, FAR)
    keep, give = halved(c_ref, keep, shift(give, AGAIN, 2, 1), TWICE, F32)
    keep, give = halved(c_ref, keep, shift(give, TWICE, 2, 1), SPLIT, BF)
    picker, member, length = call(
        place_kernel,
        (c_ref, patch_first, moved, place),
        (
            shaped((ROWS, WINDOW), BF),
            shaped((n_bytes, WINDOW), BF),
            shaped((n_bytes, HD), F32),
        ),
        10_000_000,
        3,
    )
    pieces, out = call(
        sum_kernel,
        (c_ref, terms, keep, shift(give, SPLIT, 2, 1), w_qkv, picker),
        (shaped((N_TP, ROWS, HD), BF), shaped((ROWS, FEATS), BF)),
        100_000_000,
        1,
        1,
    )
    (both,) = call(
        head_sum_kernel, (swap(pieces, "tp"), out), (shaped((ROWS, HD + FEATS), BF),), 100_000
    )
    attn_out, byte_grad = call(
        last_kernel,
        (shift(both, CTX, N_CTX, 1), both, picker, member, length),
        (shaped((ROWS, FEATS), BF), shaped((n_bytes, HD), BF)),
        10_000_000,
    )
    return attn_out, byte_grad


def solution(mesh):
    fine = Mesh(mesh.devices.reshape(SIZES), NAMES)
    placed = (P(CTX, None), P(CTX), P(), P(), P(None, None, "tp"), P(CTX, "tp"))
    return jax.shard_map(
        shards,
        mesh=fine,
        in_specs=placed,
        out_specs=(P(CTX, "tp"), P(CTX, "tp")),
        check_vma=False,
    )
```
